128 devices in a mesh: dp: 16 (over y_lo, x, core), tensor: 8 (over y_hi, z).
Axes of the slice: x: 4, y: 4 (y_hi: 2, y_lo: 2; y = y_hi * 2 + y_lo), z: 4, core: 2. Of those that a mesh axis runs over, the one named last changes fastest.
Arguments:
- hidden: bfloat16 [16, 128, 8192], P('dp', 'tensor'), may hold values from -6 to 6
- query_weight: bfloat16 [8192, 4096], P(None, 'tensor'), may hold values from -0.0625 to 0.0625
- key_value_weight: bfloat16 [2, 8192, 1024], P(None, None, 'tensor'), may hold values from -0.0625 to 0.0625
- output_weight: bfloat16 [4096, 8192], P('tensor'), may hold values from -0.09375 to 0.09375
- head: bfloat16 [8192, 5], replicated, may hold values from -0.5 to 0.5
- lens: int32 [16], P('dp'), may hold values from 32 to 128
- partner: int32 [16], replicated, may hold values from 0 to 15, as said below
- adapter_down_qkv: bfloat16 [3, 8192, 16], replicated, may hold values from -0.0625 to 0.0625
- adapter_up_query: bfloat16 [16, 4096], P(None, 'tensor'), may hold values from -2 to 2
- adapter_up_key_value: bfloat16 [2, 16, 1024], P(None, None, 'tensor'), may hold values from -2 to 2
- adapter_down_output: bfloat16 [4096, 16], P('tensor'), may hold values from -0.09375 to 0.09375
- adapter_up_output: bfloat16 [16, 8192], replicated, may hold values from -2 to 2
- initial_down_qkv: float32 [3, 8192, 16], replicated, may hold values from -6 to 6
- initial_up_query: float32 [16, 4096], replicated, may hold values from -6 to 6
- initial_up_key_value: float32 [2, 16, 1024], replicated, may hold values from -6 to 6
- initial_down_output: float32 [4096, 16], replicated, may hold values from -6 to 6
- initial_up_output: float32 [16, 8192], replicated, may hold values from -6 to 6
Outputs:
- next_a: float32 [3, 8192, 16], replicated
- next_bq: float32 [16, 4096], replicated
- next_bkv: float32 [2, 16, 1024], replicated
- next_ao: float32 [4096, 16], replicated
- next_bo: float32 [16, 8192], replicated
The draws below stay inside these ranges and needn't reach their ends.
Inputs may be any that keep to these rules, and one draw needn't show every extreme that they name: partner pairs the sequences: partner[partner[i]] = i and partner[i] differs from i.
All inputs are finite; a program needn't handle non-finite values.
Results may differ from the reference program's by a relative error of at most 0.013.
Values may be sent and summed in bfloat16 or wider, within the bound.
No kernel may reach another device: no remote copies, remote signals or barrier semaphores. Data moves between devices by JAX's collectives and lax.ppermute only.
A program may use at most 128 MiB of HBM per device.

```python
import math
import jax
import jax.numpy as jnp
from jax import lax

MODEL_WIDTH = 8192
QUERY_HEADS = 32
KEY_VALUE_HEADS = 8
HEAD_SIZE = 128
ADAPTER_RANK = 16
OBJ = 5
SEQ_LEN = 128
NSEQ = 16
NPARAM = 688128


def draw_partner(key, part):
    key = jax.random.fold_in(key, 11)
    order = jax.random.permutation(key, NSEQ).astype(jnp.int32)
    swapped = order.reshape(NSEQ // 2, 2)[:, ::-1].reshape(NSEQ)
    return jnp.zeros((NSEQ,), jnp.int32).at[order].set(swapped)


def place_ends(values, own_key, least, high):
    longest = values.shape.index(max(values.shape))
    spots = []
    for shift in (0, 1):
        where = [jax.random.randint(jax.random.fold_in(own_key, axis), (), 0, length) for axis, length in enumerate(values.shape)]
        where[longest] = (where[longest] + shift) % values.shape[longest]
        spots.append(tuple(where))
    return values.at[spots[0]].set(least).at[spots[1]].set(high)


def shard_levels(own_key, dims, split, low, high):
    loudness = 1.0
    for position, shards_of in split:
        draws = jax.random.uniform(jax.random.fold_in(jax.random.fold_in(own_key, 6), position), (shards_of,), jnp.float32, low / len(split), high / len(split))
        loudness = loudness * jnp.repeat(jnp.exp(draws), dims[position] // shards_of).reshape((-1,) + (1,) * (len(dims) - 1 - position))
    return loudness


def bell_draw(rng, shape, deviation, limit, pieces=(), kind=jnp.bfloat16):
    array = jax.random.normal(rng, shape, jnp.float32) * deviation
    if len(pieces) > 0:
        array = shard_levels(rng, shape, pieces, -0.22, 0.18) * array
    return jnp.clip(array, min=-limit, max=limit).astype(kind)


def setup_inputs(seed: int = 0) -> dict:
    key_list = jax.random.split(jax.random.key(seed), 18)
    return {
        "hidden": bell_draw(key_list[0], (NSEQ, SEQ_LEN, MODEL_WIDTH), 1.0, 6.0, ((0, 16), (1, 8))),
        "query_weight": bell_draw(key_list[1], (MODEL_WIDTH, QUERY_HEADS * HEAD_SIZE), MODEL_WIDTH ** -0.5, 0.0625, ((1, 8),)),
        "key_value_weight": bell_draw(key_list[2], (2, MODEL_WIDTH, KEY_VALUE_HEADS * HEAD_SIZE), MODEL_WIDTH ** -0.5, 0.0625, ((2, 8),)),
        "output_weight": bell_draw(key_list[3], (QUERY_HEADS * HEAD_SIZE, MODEL_WIDTH), (QUERY_HEADS * HEAD_SIZE) ** -0.5, 0.09375, ((0, 8),)),
        "head": bell_draw(key_list[4], (MODEL_WIDTH, OBJ), (MODEL_WIDTH // 64) ** -0.5, 0.5),
        "lens": place_ends(jax.random.randint(key_list[5], (NSEQ,), SEQ_LEN // 4, SEQ_LEN + 1), jax.random.fold_in(key_list[5], 1), SEQ_LEN // 4, SEQ_LEN).astype(jnp.int32),
        "partner": draw_partner(jax.random.fold_in(key_list[17], 71), 0),
        "adapter_down_qkv": bell_draw(key_list[7], (3, MODEL_WIDTH, ADAPTER_RANK), MODEL_WIDTH ** -0.5, 0.0625),
        "adapter_up_query": bell_draw(key_list[8], (ADAPTER_RANK, QUERY_HEADS * HEAD_SIZE), 0.125, 2.0, ((1, 8),)),
        "adapter_up_key_value": bell_draw(key_list[9], (2, ADAPTER_RANK, KEY_VALUE_HEADS * HEAD_SIZE), 0.125, 2.0, ((2, 8),)),
        "adapter_down_output": bell_draw(key_list[10], (QUERY_HEADS * HEAD_SIZE, ADAPTER_RANK), (QUERY_HEADS * HEAD_SIZE) ** -0.5, 0.09375, ((0, 8),)),
        "adapter_up_output": bell_draw(key_list[11], (ADAPTER_RANK, MODEL_WIDTH), 0.125, 2.0),
        "initial_down_qkv": bell_draw(key_list[12], (3, MODEL_WIDTH, ADAPTER_RANK), 1.0, 6.0, (), jnp.float32),
        "initial_up_query": bell_draw(key_list[13], (ADAPTER_RANK, QUERY_HEADS * HEAD_SIZE), 1.0, 6.0, (), jnp.float32),
        "initial_up_key_value": bell_draw(key_list[14], (2, ADAPTER_RANK, KEY_VALUE_HEADS * HEAD_SIZE), 1.0, 6.0, (), jnp.float32),
        "initial_down_output": bell_draw(key_list[15], (QUERY_HEADS * HEAD_SIZE, ADAPTER_RANK), 1.0, 6.0, (), jnp.float32),
        "initial_up_output": bell_draw(key_list[16], (ADAPTER_RANK, MODEL_WIDTH), 1.0, 6.0, (), jnp.float32),
    }


ADAPTER_SCALE = 2.0
NORM_EPS = 1e-05
LANCZOS_EPS = 1e-06
SCORE_CAP = 30.0
PRECISE = lax.Precision.HIGHEST

def contract_halved(left_side, right_side, left_dim, right_dim):
    return lax.dot_general(left_side, right_side, (((left_dim,), (right_dim,)), ((), ())), preferred_element_type=jnp.float32)

def contract_entire(left_side, right_side, left_dim, right_dim):
    return lax.dot_general(left_side, right_side, (((left_dim,), (right_dim,)), ((), ())), precision=PRECISE, preferred_element_type=jnp.float32)

def attend(query_matrix_rows, key_matrix_rows, value_matrix_rows):
    seq_count, length, query_cols = query_matrix_rows.shape
    kv_heads = key_matrix_rows.shape[2] // HEAD_SIZE
    groups = query_cols // HEAD_SIZE // kv_heads
    query_split = query_matrix_rows.reshape(seq_count, length, kv_heads, groups, HEAD_SIZE)
    key_split = key_matrix_rows.reshape(seq_count, length, kv_heads, HEAD_SIZE)
    value_split = value_matrix_rows.reshape(seq_count, length, kv_heads, HEAD_SIZE)
    scores = jnp.einsum('sqgjd,skgd->sgjqk', query_split, key_split, precision=PRECISE) / math.sqrt(HEAD_SIZE)
    scores = SCORE_CAP * jnp.tanh(scores / SCORE_CAP)
    causal = jnp.arange(length)[:, None] >= jnp.arange(length)[None, :]
    weights = jnp.where(causal, jnp.exp(scores), 0.0)
    probabilities = weights / lax.optimization_barrier(jnp.sum(weights, axis=-1, keepdims=True))
    mixed_rows = jnp.einsum('sgjqk,skgd->sqgjd', probabilities, value_split, precision=PRECISE)
    return mixed_rows.reshape(seq_count, length, query_cols)

def rms_norm(resid_rows):
    return resid_rows * lax.rsqrt(lax.optimization_barrier(jnp.mean(resid_rows * resid_rows, axis=-1, keepdims=True)) + NORM_EPS)

def adapter_projection(halved_tokens, entire_tokens, weight_matrix, adapter_down, adapter_up):
    reduced_rank = contract_entire(entire_tokens, adapter_down, 1, 0)
    return (contract_halved(halved_tokens, weight_matrix, 1, 0) + ADAPTER_SCALE * contract_entire(reduced_rank, adapter_up, 1, 0), reduced_rank)

def pooled(normed, head_full, share):
    seq_count, length, width = normed.shape
    logits = contract_entire(normed.reshape(-1, width), head_full, 1, 0).reshape(seq_count, length, -1)
    return lax.optimization_barrier(jnp.sum(logits * share[:, :, None], axis=1))

def lanczos_inner(first_set, second_set):
    return sum((jnp.sum(part_one * part_two) for part_one, part_two in zip(first_set, second_set))) / NPARAM

def reference(hidden, query_weight, key_value_weight, output_weight, head, lens, partner, adapter_down_qkv, adapter_up_query, adapter_up_key_value, adapter_down_output, adapter_up_output, initial_down_qkv, initial_up_query, initial_up_key_value, initial_down_output, initial_up_output):
    seq_count, length, width = hidden.shape
    query_cols = query_weight.shape[1]
    kv_cols = key_value_weight.shape[2]
    halved_tokens = hidden.reshape(-1, width)
    entire_tokens = halved_tokens.astype(jnp.float32)
    down_every_factor = adapter_down_qkv.astype(jnp.float32)
    up_query_factor = adapter_up_query.astype(jnp.float32)
    up_key_value = adapter_up_key_value.astype(jnp.float32)
    down_output = adapter_down_output.astype(jnp.float32)
    up_output = adapter_up_output.astype(jnp.float32)
    head_full = head.astype(jnp.float32)
    query_matrix_rows, reduced_query = adapter_projection(halved_tokens, entire_tokens, query_weight, down_every_factor[0], up_query_factor)
    key_matrix_rows, reduced_key = adapter_projection(halved_tokens, entire_tokens, key_value_weight[0], down_every_factor[1], up_key_value[0])
    value_matrix_rows, reduced_value = adapter_projection(halved_tokens, entire_tokens, key_value_weight[1], down_every_factor[2], up_key_value[1])
    shaped = (query_matrix_rows.reshape(seq_count, length, query_cols), key_matrix_rows.reshape(seq_count, length, kv_cols), value_matrix_rows.reshape(seq_count, length, kv_cols))
    context = attend(*shaped).reshape(-1, query_cols)
    context_low = contract_entire(context, down_output, 1, 0)
    out_rows = contract_halved(context.astype(jnp.bfloat16), output_weight, 1, 0) + ADAPTER_SCALE * contract_entire(context_low, up_output, 1, 0)
    resid = (entire_tokens + out_rows).reshape(seq_count, length, width)
    normed = rms_norm(resid)
    share = (jnp.arange(length)[None, :] < lens[:, None]).astype(jnp.float32) / lens.astype(jnp.float32)[:, None]
    rewards = pooled(normed, head_full, share)
    squashed = jax.nn.sigmoid(rewards - jnp.take(rewards, partner, axis=0))
    curvature = squashed * (1.0 - squashed) / (seq_count // 2)

    def product(vector):
        vec_a, vec_bq, vec_bkv, vec_ao, vec_bo = vector
        tangent_query = ADAPTER_SCALE * (contract_entire(contract_entire(entire_tokens, vec_a[0], 1, 0), up_query_factor, 1, 0) + contract_entire(reduced_query, vec_bq, 1, 0))
        tangent_key = ADAPTER_SCALE * (contract_entire(contract_entire(entire_tokens, vec_a[1], 1, 0), up_key_value[0], 1, 0) + contract_entire(reduced_key, vec_bkv[0], 1, 0))
        tangent_value = ADAPTER_SCALE * (contract_entire(contract_entire(entire_tokens, vec_a[2], 1, 0), up_key_value[1], 1, 0) + contract_entire(reduced_value, vec_bkv[1], 1, 0))
        tangents = (tangent_query.reshape(seq_count, length, query_cols), tangent_key.reshape(seq_count, length, kv_cols), tangent_value.reshape(seq_count, length, kv_cols))
        tangent_context = jax.jvp(attend, shaped, tangents)[1].reshape(-1, query_cols)
        tangent_terms = contract_halved(tangent_context.astype(jnp.bfloat16), output_weight, 1, 0) + ADAPTER_SCALE * (contract_entire(contract_entire(tangent_context, down_output, 1, 0), up_output, 1, 0) + contract_entire(contract_entire(context, vec_ao, 1, 0), up_output, 1, 0) + contract_entire(context_low, vec_bo, 1, 0))
        tangent_normed = jax.jvp(rms_norm, (resid,), (tangent_terms.reshape(resid.shape),))[1]
        tangent_rewards = pooled(tangent_normed, head_full, share)
        pull_all = curvature * (tangent_rewards - jnp.take(tangent_rewards, partner, axis=0))
        cot_normed = contract_entire((pull_all[:, None, :] * share[:, :, None]).reshape(-1, pull_all.shape[1]), head_full, 1, 1).reshape(resid.shape)
        cot_resid = jax.vjp(rms_norm, resid)[1](cot_normed)[0]
        cot_half = cot_resid.astype(jnp.bfloat16).reshape(-1, width)
        cot_full = cot_half.astype(jnp.float32)
        cot_low = contract_entire(cot_full, up_output, 1, 1)
        cot_context = contract_halved(cot_half, output_weight, 1, 1) + ADAPTER_SCALE * contract_entire(cot_low, down_output, 1, 1)
        grad_ao = ADAPTER_SCALE * contract_entire(context, cot_low, 0, 0)
        grad_bo = ADAPTER_SCALE * contract_entire(context_low, cot_full, 0, 0)
        cot_query, cot_key, cot_value = jax.vjp(attend, *shaped)[1](cot_context.reshape(seq_count, length, query_cols))
        cot_query = cot_query.reshape(-1, query_cols)
        cot_key = cot_key.reshape(-1, kv_cols)
        cot_value = cot_value.reshape(-1, kv_cols)
        grad_bq = ADAPTER_SCALE * contract_entire(reduced_query, cot_query, 0, 0)
        grad_bkv = ADAPTER_SCALE * jnp.stack([contract_entire(reduced_key, cot_key, 0, 0), contract_entire(reduced_value, cot_value, 0, 0)])
        factors = (contract_entire(cot_query, up_query_factor, 1, 1), contract_entire(cot_key, up_key_value[0], 1, 1), contract_entire(cot_value, up_key_value[1], 1, 1))
        grad_a = ADAPTER_SCALE * jnp.stack([contract_entire(entire_tokens, factor, 0, 0) for factor in factors])
        return (grad_a, grad_bq, grad_bkv, grad_ao, grad_bo)
    start_set = (initial_down_qkv, initial_up_query, initial_up_key_value, initial_down_output, initial_up_output)
    start_scale = lax.rsqrt(lanczos_inner(start_set, start_set) + LANCZOS_EPS)
    first_set = tuple((block_part * start_scale for block_part in start_set))
    image_one = product(first_set)
    alpha_one = lanczos_inner(image_one, first_set)
    resid_one = tuple((image_part - alpha_one * base_part for image_part, base_part in zip(image_one, first_set)))
    beta_one = jnp.sqrt(lanczos_inner(resid_one, resid_one) + LANCZOS_EPS)
    second_set = tuple((block_part / beta_one for block_part in resid_one))
    image_two = tuple((image_part - beta_one * base_part for image_part, base_part in zip(product(second_set), first_set)))
    alpha_two = lanczos_inner(image_two, second_set)
    resid_two = tuple((image_part - alpha_two * base_part for image_part, base_part in zip(image_two, second_set)))
    beta_two = jnp.sqrt(lanczos_inner(resid_two, resid_two) + LANCZOS_EPS)
    next_a, next_bq, next_bkv, next_ao, next_bo = tuple((block_part / beta_two for block_part in resid_two))
    return (next_a, next_bq, next_bkv, next_ao, next_bo)
```

```python
import math

import jax
import jax.numpy as jnp
from jax import lax
from jax.sharding import PartitionSpec as P

HEAD_SIZE = 128
NPARAM = 688128
ADAPTER_SCALE = 2.0
NORM_EPS = 1e-05
LANCZOS_EPS = 1e-06
SCORE_CAP = 30.0
PRECISE = lax.Precision.HIGHEST
OBJ = 5
PIECES = 11
PIECE_ROWS = 56
LANES = 512


def dot_halved(left_side, right_side, left_dim, right_dim):
    return lax.dot_general(
        left_side,
        right_side,
        (((left_dim,), (right_dim,)), ((), ())),
        preferred_element_type=jnp.float32,
    )


def dot_entire(left_side, right_side, left_dim, right_dim):
    return lax.dot_general(
        left_side,
        right_side,
        (((left_dim,), (right_dim,)), ((), ())),
        precision=PRECISE,
        preferred_element_type=jnp.float32,
    )


def two_halves(entire):
    upper = lax.reduce_precision(entire, 8, 7)
    return upper.astype(jnp.bfloat16), (entire - upper).astype(jnp.bfloat16)


def three_halves(entire):
    upper = lax.reduce_precision(entire, 8, 7)
    rest = entire - upper
    middle = lax.reduce_precision(rest, 8, 7)
    return (
        upper.astype(jnp.bfloat16),
        middle.astype(jnp.bfloat16),
        (rest - middle).astype(jnp.bfloat16),
    )


def gather_by_exchange(block, axis):
    count = lax.axis_size(axis)
    copies = jnp.broadcast_to(block[None], (count,) + block.shape)
    return lax.all_to_all(copies, axis, 0, 0)


def local(
    hidden,
    query_weight,
    key_value_weight,
    output_weight,
    head,
    lens,
    partner,
    adapter_down_qkv,
    adapter_up_query,
    adapter_up_key_value,
    adapter_down_output,
    adapter_up_output,
    initial_down_qkv,
    initial_up_query,
    initial_up_key_value,
    initial_down_output,
    initial_up_output,
):
    _, part_length, width = hidden.shape
    shards = lax.axis_size("tensor")
    groups = lax.axis_size("dp")
    tensor_rank = lax.axis_index("tensor")
    group_rank = lax.axis_index("dp")
    query_cols = query_weight.shape[1]
    heads = query_cols // HEAD_SIZE
    length = part_length * shards
    root = 1.0 / math.sqrt(HEAD_SIZE)

    down_qkv = jnp.transpose(adapter_down_qkv, (0, 2, 1))
    down_output = adapter_down_output.T.astype(jnp.float32)
    up_query = adapter_up_query.astype(jnp.float32)
    up_key_value = adapter_up_key_value.astype(jnp.float32)
    head_rows = head.T

    tokens = gather_by_exchange(hidden[0], "tensor").reshape(length, width)

    low = dot_halved(tokens, down_qkv.reshape(48, width), 1, 1)
    low_q, low_k, low_v = low[:, :16], low[:, 16:32], low[:, 32:]
    query = dot_halved(tokens, query_weight, 1, 0) + ADAPTER_SCALE * dot_entire(
        low_q, up_query, 1, 0
    )
    keys = dot_halved(tokens, key_value_weight[0], 1, 0) + ADAPTER_SCALE * dot_entire(
        low_k, up_key_value[0], 1, 0
    )
    values = dot_halved(tokens, key_value_weight[1], 1, 0) + ADAPTER_SCALE * dot_entire(
        low_v, up_key_value[1], 1, 0
    )
    query_split = query.reshape(length, heads, HEAD_SIZE)
    capped = jnp.tanh(
        jnp.einsum("qjd,kd->jqk", query_split, keys, precision=PRECISE) * (root / SCORE_CAP)
    )
    causal = jnp.arange(length)[:, None] >= jnp.arange(length)[None, :]
    weights = jnp.where(causal, jnp.exp(SCORE_CAP * capped), 0.0)
    probabilities = weights / jnp.sum(weights, axis=-1, keepdims=True)
    context_split = jnp.einsum("jqk,kd->qjd", probabilities, values, precision=PRECISE)
    context = context_split.reshape(length, query_cols)
    context_low = dot_entire(down_output, context, 1, 1)
    low_upper, low_lower = two_halves(ADAPTER_SCALE * context_low)
    out_terms = dot_halved(context.astype(jnp.bfloat16), output_weight, 1, 0) + dot_halved(
        jnp.concatenate([low_upper, low_lower], 0),
        jnp.concatenate([adapter_up_output, adapter_up_output], 0),
        0,
        0,
    )
    out_pieces = lax.all_to_all(
        out_terms.astype(jnp.bfloat16).reshape(shards, part_length, width), "tensor", 0, 0
    )
    resid_own = hidden[0].astype(jnp.float32) + jnp.sum(out_pieces.astype(jnp.float32), 0)
    resid = gather_by_exchange(resid_own.astype(jnp.bfloat16), "tensor").reshape(length, width)

    resid_entire = resid.astype(jnp.float32)
    inverse = lax.rsqrt(jnp.mean(resid_entire * resid_entire, axis=1, keepdims=True) + NORM_EPS)
    length_own = lens[0]
    share = jnp.where(
        jnp.arange(length)[:, None] < length_own, 1.0 / length_own.astype(jnp.float32), 0.0
    )
    stacked = jnp.concatenate([resid, head_rows], 0)
    logits = inverse * dot_halved(resid, head_rows, 1, 1)
    rewards = jnp.sum(logits * share, 0)
    through = dot_halved(stacked, output_weight, 1, 1)
    through_low = dot_halved(stacked, adapter_up_output, 1, 1)
    through = through + ADAPTER_SCALE * dot_entire(through_low, down_output, 1, 0)
    lead = share * inverse
    pulled = (lead * inverse * logits / width).T
    cot_context = (
        lead[None] * through[length:][:, None, :] - pulled[:, :, None] * through[None, :length]
    )
    cot_low = (
        lead[None] * through_low[length:][:, None, :]
        - pulled[:, :, None] * through_low[None, :length]
    )
    cot_split = cot_context.reshape(OBJ, length, heads, HEAD_SIZE)
    cot_prob = jnp.einsum("oqjd,kd->ojqk", cot_split, values, precision=PRECISE)
    inner = jnp.einsum("oqjd,qjd->ojq", cot_split, context_split)
    cot_score = (
        probabilities[None]
        * (cot_prob - inner[..., None])
        * ((1.0 - capped * capped) * root)[None]
    )
    cot_query = jnp.einsum("ojqk,kd->oqjd", cot_score, keys, precision=PRECISE).reshape(
        OBJ, length, query_cols
    )
    cot_keys = jnp.einsum("ojqk,qjd->okd", cot_score, query_split, precision=PRECISE)
    cot_values = jnp.einsum("jqk,oqjd->okd", probabilities, cot_split, precision=PRECISE)

    factor_q = jnp.einsum("rc,otc->rot", up_query, cot_query, precision=PRECISE)
    factor_k = jnp.einsum("rc,otc->rot", up_key_value[0], cot_keys, precision=PRECISE)
    factor_v = jnp.einsum("rc,otc->rot", up_key_value[1], cot_values, precision=PRECISE)
    factors = jnp.concatenate(
        [factor_q, factor_k, factor_v, context_low[:, None, :]], 1
    ) * ADAPTER_SCALE
    factors = jnp.sum(
        lax.all_to_all(factors.reshape(shards, 2, 3 * OBJ + 1, length), "tensor", 0, 0), 0
    )
    context_lead = factors[:, 3 * OBJ] * lead.T
    rows_a = factors[:, : 3 * OBJ].reshape(2 * 3 * OBJ, length)
    rows_bo = (factors[:, 3 * OBJ][:, None, :] * pulled[None]).reshape(2 * OBJ, length)

    def split_dot(rows, right_side):
        upper, lower = two_halves(rows)
        both = dot_halved(jnp.concatenate([upper, lower], 0), right_side, 1, 0)
        return both[: rows.shape[0]] + both[rows.shape[0] :]

    jac_a = split_dot(rows_a, tokens).reshape(2, 3, OBJ, groups, LANES)
    jac_bo = (
        jnp.sum(context_lead, 1)[:, None, None] * head_rows.astype(jnp.float32)[None]
        - split_dot(rows_bo, resid).reshape(2, OBJ, width)
    ).reshape(2, 1, OBJ, groups, LANES)
    wide = jnp.concatenate([jac_a, jac_bo], 1).reshape(8 * OBJ, groups, LANES)
    wide = jnp.transpose(wide, (1, 0, 2)).astype(jnp.bfloat16)
    jac_bq = ADAPTER_SCALE * jnp.einsum("tr,otc->roc", low_q, cot_query, precision=PRECISE)
    jac_bk = ADAPTER_SCALE * jnp.einsum("tr,otc->roc", low_k, cot_keys, precision=PRECISE)
    jac_bv = ADAPTER_SCALE * jnp.einsum("tr,otc->roc", low_v, cot_values, precision=PRECISE)
    jac_ao = ADAPTER_SCALE * jnp.einsum("otr,tc->roc", cot_low, context, precision=PRECISE)
    spare = jnp.zeros((16, OBJ, LANES - 2 * HEAD_SIZE), jnp.float32)
    narrow = jnp.concatenate(
        [jac_bq, jac_ao, jnp.concatenate([jac_bk, jac_bv, spare], 2)], 1
    ).astype(jnp.bfloat16)
    payload = jnp.concatenate(
        [wide, narrow, jnp.zeros((16, PIECE_ROWS - PIECES * OBJ, LANES), jnp.bfloat16)], 1
    )
    spread = lax.all_to_all(payload, "dp", 0, 0)
    jac = (
        spread[:, : PIECES * OBJ]
        .reshape(groups, PIECES, OBJ, LANES)
        .transpose(0, 2, 1, 3)
        .reshape(groups * OBJ, PIECES * LANES)
    )

    own_a = lax.dynamic_slice(
        jnp.transpose(initial_down_qkv, (0, 2, 1)),
        (0, 2 * tensor_rank, group_rank * LANES),
        (3, 2, LANES),
    )
    own_bo = lax.dynamic_slice(
        initial_up_output, (2 * tensor_rank, group_rank * LANES), (2, LANES)
    )
    own_bq = lax.dynamic_slice(
        initial_up_query, (group_rank, tensor_rank * query_cols), (1, query_cols)
    )
    own_ao = lax.dynamic_slice(
        initial_down_output.T, (group_rank, tensor_rank * query_cols), (1, query_cols)
    )
    own_bkv = lax.dynamic_slice(
        initial_up_key_value, (0, group_rank, tensor_rank * HEAD_SIZE), (2, 1, HEAD_SIZE)
    )
    own_start = jnp.concatenate(
        [
            jnp.concatenate([own_a.transpose(1, 0, 2), own_bo[:, None]], 1).reshape(8, LANES),
            own_bq,
            own_ao,
            jnp.concatenate(
                [own_bkv.reshape(1, 2 * HEAD_SIZE), jnp.zeros((1, LANES - 2 * HEAD_SIZE))], 1
            ),
        ],
        0,
    ).reshape(1, PIECES * LANES)
    start_rows = jnp.concatenate(three_halves(own_start), 0)
    rows = groups * OBJ
    gram = dot_halved(jac, jac, 1, 1)
    along = jnp.sum(dot_halved(jac, start_rows, 1, 1), 1, keepdims=True)
    start_square = jnp.sum(own_start * own_start)
    own_rewards = jnp.where(
        (jnp.arange(groups)[:, None] == group_rank) & (tensor_rank == 0), rewards[None], 0.0
    ).reshape(rows, 1)
    message = jnp.concatenate(
        [
            gram,
            along,
            own_rewards,
            jnp.full((rows, 1), start_square),
            jnp.zeros((rows, 128 - rows - 3), jnp.float32),
        ],
        1,
    )
    message = jnp.sum(gather_by_exchange(message, "dp"), 0)
    message = jnp.sum(gather_by_exchange(message, "tensor"), 0)
    gram = message[:, :rows]
    along = message[:, rows]
    all_rewards = message[:, rows + 1].reshape(groups, OBJ)
    start_square = message[0, rows + 2] / NPARAM

    def against(per_row):
        shaped = per_row.reshape(groups, OBJ)
        return shaped - jnp.take(shaped, partner, axis=0)

    def gram_times(vector):
        return jnp.sum(gram * vector[None, :], 1)

    squashed = jax.nn.sigmoid(against(all_rewards))
    curvature = squashed * (1.0 - squashed) / (groups // 2)
    start_scale = lax.rsqrt(start_square + LANCZOS_EPS)
    first_square = start_square * start_scale * start_scale
    along_one = along * start_scale
    pull_one = (curvature * against(along_one)).reshape(rows)
    alpha_one = jnp.sum(pull_one * along_one) / NPARAM
    gram_pull = gram_times(pull_one)
    beta_one = jnp.sqrt(
        jnp.sum(pull_one * gram_pull) / NPARAM
        - alpha_one * alpha_one * (2.0 - first_square)
        + LANCZOS_EPS
    )
    along_two = (gram_pull - alpha_one * along_one) / beta_one
    pull_two = (curvature * against(along_two)).reshape(rows)
    first_second = alpha_one * (1.0 - first_square) / beta_one
    alpha_two = jnp.sum(pull_two * along_two) / NPARAM - beta_one * first_second
    mixed = pull_two - (alpha_two / beta_one) * pull_one
    first_part = alpha_two * alpha_one / beta_one - beta_one
    beta_two = jnp.sqrt(
        jnp.sum(mixed * gram_times(mixed)) / NPARAM
        + 2.0 * first_part * jnp.sum(mixed * along_one) / NPARAM
        + first_part * first_part * first_square
        + LANCZOS_EPS
    )
    mixed = mixed / beta_two
    start_part = first_part * start_scale / beta_two
    own_result = jnp.sum(
        dot_halved(jnp.stack(three_halves(mixed), 0), jac, 1, 0), 0
    ).astype(jnp.bfloat16)
    own_result = own_result.reshape(PIECES * LANES // 128, 128)[:42]
    own_result = jnp.concatenate([own_result, jnp.zeros((6, 128), jnp.bfloat16)], 0)
    every = lax.all_to_all(
        jnp.broadcast_to(own_result[None], (groups * shards,) + own_result.shape),
        ("dp", "tensor"),
        0,
        0,
    ).reshape(groups, shards, 48 * 128)
    wide = every[:, :, : 8 * LANES].reshape(groups, shards, 2, 4, LANES)
    wide = wide.transpose(3, 1, 2, 0, 4).reshape(4, 16, width).astype(jnp.float32)
    narrow = every[:, :, 8 * LANES : 10 * LANES].reshape(groups, shards, 2, LANES)
    narrow = narrow.transpose(2, 0, 1, 3).reshape(2, 16, shards * LANES).astype(jnp.float32)
    small = every[:, :, 10 * LANES : 10 * LANES + 256].reshape(groups, shards, 2, HEAD_SIZE)
    small = small.transpose(2, 0, 1, 3).reshape(2, 16, shards * HEAD_SIZE).astype(jnp.float32)
    return (
        jnp.transpose(wide[:3], (0, 2, 1)) + start_part * initial_down_qkv,
        narrow[0] + start_part * initial_up_query,
        small + start_part * initial_up_key_value,
        narrow[1].T + start_part * initial_down_output,
        wide[3] + start_part * initial_up_output,
    )


def solution(mesh):
    in_specs = (
        P("dp", "tensor", None),
        P(None, "tensor"),
        P(None, None, "tensor"),
        P("tensor", None),
        P(),
        P("dp"),
        P(),
        P(),
        P(None, "tensor"),
        P(None, None, "tensor"),
        P("tensor", None),
        P(),
        P(),
        P(),
        P(),
        P(),
        P(),
    )
    out_specs = (P(), P(), P(), P(), P())
    return jax.shard_map(local, mesh=mesh, in_specs=in_specs, out_specs=out_specs, check_vma=False)
```

```python
import math

import jax
import jax.numpy as jnp
from jax import lax
from jax.experimental import pallas as pl
from jax.experimental.pallas import tpu as pltpu
from jax.sharding import PartitionSpec as P

HEAD_SIZE = 128
NPARAM = 688128
ADAPTER_SCALE = 2.0
NORM_EPS = 1e-05
LANCZOS_EPS = 1e-06
SCORE_CAP = 30.0
PRECISE = lax.Precision.HIGHEST
OBJ = 5
PIECES = 11
PIECE_ROWS = 56
LANES = 512


def dot_halved(left_side, right_side, left_dim, right_dim):
    return lax.dot_general(
        left_side,
        right_side,
        (((left_dim,), (right_dim,)), ((), ())),
        preferred_element_type=jnp.float32,
    )


def dot_entire(left_side, right_side, left_dim, right_dim):
    return lax.dot_general(
        left_side,
        right_side,
        (((left_dim,), (right_dim,)), ((), ())),
        precision=PRECISE,
        preferred_element_type=jnp.float32,
    )


def two_halves(entire):
    upper = lax.reduce_precision(entire, 8, 7)
    return upper.astype(jnp.bfloat16), (entire - upper).astype(jnp.bfloat16)


def three_halves(entire):
    upper = lax.reduce_precision(entire, 8, 7)
    rest = entire - upper
    middle = lax.reduce_precision(rest, 8, 7)
    return (
        upper.astype(jnp.bfloat16),
        middle.astype(jnp.bfloat16),
        (rest - middle).astype(jnp.bfloat16),
    )


def gather_by_exchange(block, axis):
    count = lax.axis_size(axis)
    copies = jnp.broadcast_to(block[None], (count,) + block.shape)
    return lax.all_to_all(copies, axis, 0, 0)


PAIR_ROWS = 40
PACK_ROWS = 48
PACK_LANES = 42
RESULT_LANES = 768


def rounded_parts(entire, count):
    parts = []
    for _ in range(count):
        part = entire.astype(jnp.bfloat16)
        parts.append(part)
        entire = entire - part.astype(jnp.float32)
    return parts


def lane_sum(values):
    return jnp.sum(values, axis=1, keepdims=True)


def row_sum(values):
    return jnp.sum(values, axis=0, keepdims=True)


def gram_body(rank_ref, jac_ref, start_ref, pairs_ref, rewards_ref, packed_ref):
    jac = jac_ref[...]
    start = start_ref[...]
    pairs = pairs_ref[...]
    rows = jac.shape[0]
    gram = dot_halved(jac, jac, 1, 1)
    starts = jnp.concatenate(rounded_parts(start, 3), 0)
    along = lane_sum(dot_halved(jac, starts, 1, 1))
    own_pairs = pairs[:, :rows]
    gram = dot_entire(dot_entire(own_pairs, gram, 1, 0), own_pairs, 1, 1)
    along = dot_entire(own_pairs, jnp.broadcast_to(along, (rows, 128)), 1, 0)
    rewards = pltpu.roll(rewards_ref[...], OBJ * rank_ref[0], axis=1)[:1]
    rewards = jnp.where(rank_ref[1] == 0, rewards, 0.0)
    apart = lane_sum(pairs * rewards)
    square = jnp.sum(start * start)
    lane = lax.broadcasted_iota(jnp.int32, (PACK_ROWS, 128), 1)
    row = lax.broadcasted_iota(jnp.int32, (PACK_ROWS, 128), 0)
    wide = jnp.concatenate([gram, jnp.zeros((PACK_ROWS, 128 - PACK_ROWS), jnp.float32)], 1)
    wide = jnp.where(lane < PAIR_ROWS, wide, 0.0)
    wide = jnp.where(lane == PAIR_ROWS, along, wide)
    wide = jnp.where(lane == PAIR_ROWS + 1, apart, wide)
    wide = jnp.where((row == PAIR_ROWS) & (lane == 0), square, wide)
    packed_ref[...] = (
        wide[:16]
        + pltpu.roll(wide[16:32], PACK_LANES, axis=1)
        + pltpu.roll(wide[32:], 2 * PACK_LANES, axis=1)
    )


def lanczos_body(packed_ref, pairs_ref, jac_ref, result_ref, part_ref):
    packed = jnp.sum(packed_ref[...], axis=0)
    wide = jnp.concatenate(
        [
            packed,
            pltpu.roll(packed, 128 - PACK_LANES, axis=1),
            pltpu.roll(packed, 128 - 2 * PACK_LANES, axis=1),
        ],
        0,
    )
    lane = lax.broadcasted_iota(jnp.int32, (PACK_ROWS, 128), 1)
    row = lax.broadcasted_iota(jnp.int32, (PACK_ROWS, 128), 0)
    inside = row < PAIR_ROWS
    gram = jnp.where(inside & (lane < PAIR_ROWS), wide, 0.0)
    along = lane_sum(jnp.where(inside & (lane == PAIR_ROWS), wide, 0.0))
    apart = lane_sum(jnp.where(inside & (lane == PAIR_ROWS + 1), wide, 0.0))
    picked = jnp.where((row == PAIR_ROWS) & (lane == 0), wide, 0.0)
    start_square = lane_sum(row_sum(picked)) / NPARAM
    diagonal = row == lane

    def gram_times(column):
        across = row_sum(jnp.where(diagonal, column, 0.0))
        return lane_sum(gram * across)

    def inner(left_side, right_side):
        return row_sum(left_side * right_side) / NPARAM

    decayed = jnp.exp(-jnp.abs(apart))
    curvature = decayed / ((1.0 + decayed) * (1.0 + decayed)) / (16 // 2)
    start_scale = lax.rsqrt(start_square + LANCZOS_EPS)
    first_square = start_square * start_scale * start_scale
    along_one = along * start_scale
    pull_one = curvature * along_one
    alpha_one = inner(pull_one, along_one)
    gram_pull = gram_times(pull_one)
    beta_one = jnp.sqrt(
        inner(pull_one, gram_pull) - alpha_one * alpha_one * (2.0 - first_square) + LANCZOS_EPS
    )
    along_two = (gram_pull - alpha_one * along_one) / beta_one
    pull_two = curvature * along_two
    first_second = alpha_one * (1.0 - first_square) / beta_one
    alpha_two = inner(pull_two, along_two) - beta_one * first_second
    mixed = pull_two - (alpha_two / beta_one) * pull_one
    first_part = alpha_two * alpha_one / beta_one - beta_one
    beta_two = jnp.sqrt(
        inner(mixed, gram_times(mixed))
        + 2.0 * first_part * inner(mixed, along_one)
        + first_part * first_part * first_square
        + LANCZOS_EPS
    )
    part_ref[...] = jnp.broadcast_to(first_part * start_scale / beta_two, part_ref.shape)
    across = row_sum(pairs_ref[...] * (mixed / beta_two))
    jac = jac_ref[...]
    rows = jac.shape[0]
    parts = rounded_parts(jnp.broadcast_to(across[:, :rows], (8, rows)), 3)
    result = sum(dot_halved(part, jac, 1, 0) for part in parts)[:1]
    spare = jnp.zeros((6, 128), jnp.float32)

    def chunks(start, count, size):
        return [result[:, start + size * step : start + size * (step + 1)] for step in range(count)]

    main = jnp.concatenate(chunks(0, 8, LANES), 0)
    middle = jnp.concatenate(chunks(8 * LANES, 8, 128), 0)
    last = jnp.concatenate(chunks(10 * LANES, 2, 128) + [spare], 0)
    result_ref[...] = jnp.concatenate([main, middle, last], 1).astype(jnp.bfloat16)


def assemble_body(
    part_ref,
    every_ref,
    a_ref,
    bq_ref,
    bkv_ref,
    ao_ref,
    bo_ref,
    out_a_ref,
    out_bq_ref,
    out_bkv_ref,
    out_ao_ref,
    out_bo_ref,
):
    step = pl.program_id(0)
    part = part_ref[0, 0]

    def one_hot(size, first, second):
        row = lax.broadcasted_iota(jnp.int32, (size, size), 0)
        lane = lax.broadcasted_iota(jnp.int32, (size, size), 1)
        wanted = (row % second) * first + row // second
        return jnp.where(lane == wanted, 1.0, 0.0).astype(jnp.bfloat16)

    row = lax.broadcasted_iota(jnp.int32, (64, 64), 0)
    lane = lax.broadcasted_iota(jnp.int32, (64, 64), 1)
    wanted = (row % 8) * 8 + ((row % 16) // 8) * 4 + row // 16
    moved = jnp.where(lane == wanted, 1.0, 0.0).astype(jnp.bfloat16)
    for half in range(2):
        group = 2 * step + half
        block = every_ref[pl.ds(8 * group, 8), :, :LANES].reshape(64, LANES)
        placed = dot_halved(moved, block, 1, 0).reshape(4, 16, LANES)
        lanes = slice(half * LANES, (half + 1) * LANES)
        out_a_ref[:, :, lanes] = placed[:3] + part * a_ref[:, :, lanes]
        out_bo_ref[:, lanes] = placed[3] + part * bo_ref[:, lanes]
    block = jnp.concatenate(
        [every_ref[8 * group + step, :, LANES:] for group in range(16)], 0
    )
    placed = dot_halved(one_hot(128, 8, 16), block, 1, 0)
    for chunk in range(4):
        lanes = slice(chunk * 128, (chunk + 1) * 128)
        out_bq_ref[:, lanes] = placed[16 * chunk : 16 * chunk + 16, :128] + part * bq_ref[:, lanes]
        out_ao_ref[:, lanes] = (
            placed[64 + 16 * chunk : 80 + 16 * chunk, :128] + part * ao_ref[:, lanes]
        )
    out_bkv_ref[0] = placed[:16, 128:] + part * bkv_ref[0]
    out_bkv_ref[1] = placed[16:32, 128:] + part * bkv_ref[1]


def whole(count):
    return [pl.BlockSpec(memory_space=pltpu.VMEM)] * count


def dot_parts(left_parts, right_parts, left_dim, right_dim):
    total = None
    for left_at, left_part in enumerate(left_parts):
        for right_at, right_part in enumerate(right_parts):
            if left_at + right_at < 2:
                term = dot_halved(left_part, right_part, left_dim, right_dim)
                total = term if total is None else total + term
    return total


COT_CHUNK = 2048


def cotangents_body(
    lens_ref,
    resid_ref,
    weight_ref,
    side_ref,
    query_ref,
    keys_ref,
    values_ref,
    prob_ref,
    capped_ref,
    context_ref,
    low_ref,
    context_low_ref,
    down_ref,
    up_query_ref,
    up_kv_ref,
    factors_ref,
    narrow_ref,
    rewards_ref,
    repeated_ref,
    through_ref,
    slow_ref,
    square_ref,
):
    step = pl.program_id(0)
    chunk = resid_ref[...]
    side = side_ref[...]
    left = jnp.concatenate([chunk, side[16:]], 0)
    through = dot_halved(left, weight_ref[...], 1, 1)
    slow = dot_halved(left, side, 1, 1)
    wide = chunk.astype(jnp.float32)
    square = jnp.zeros((128, 128), jnp.float32)
    for at in range(0, chunk.shape[1], 128):
        square = square + wide[:, at : at + 128] * wide[:, at : at + 128]

    @pl.when(step == 0)
    def _():
        slow_ref[...] = jnp.zeros(slow_ref.shape, jnp.float32)
        through_ref[...] = through
        slow_ref[:144, :32] = slow
        square_ref[...] = square

    @pl.when(step > 0)
    def _():
        through_ref[...] += through
        slow_ref[:144, :32] += slow
        square_ref[...] += square

    @pl.when(step == pl.num_programs(0) - 1)
    def _():
        width = chunk.shape[1] * pl.num_programs(0)
        length_own = lens_ref[0]
        root = 1.0 / math.sqrt(HEAD_SIZE)
        slow = slow_ref[...]
        slow_turned = slow.T
        square = square_ref[...]
        inverse = lax.rsqrt(lane_sum(square) / width + NORM_EPS)
        inverse_turned = lax.rsqrt(row_sum(square.T) / width + NORM_EPS)
        each = 1.0 / jnp.broadcast_to(length_own, (1, 1)).astype(jnp.float32)
        share = jnp.where(
            lax.broadcasted_iota(jnp.int32, (128, 1), 0) < length_own, each, 0.0
        )
        share_turned = jnp.where(
            lax.broadcasted_iota(jnp.int32, (1, 128), 1) < length_own, each, 0.0
        )
        logits = inverse * slow[:128, 16:32]
        lead = share * inverse
        pulled = lead * inverse * logits / width
        lead_turned = share_turned * inverse_turned
        pulled_turned = (
            lead_turned * inverse_turned * inverse_turned * slow_turned[16:32, :128] / width
        )
        low_turned = slow_turned[:16, :128]
        rewards_ref[...] = jnp.zeros(rewards_ref.shape, jnp.float32)
        rewards_ref[:1, :16] = row_sum(share * logits)
        through = through_ref[...] + ADAPTER_SCALE * dot_entire(
            slow[:144, :16], down_ref[...], 1, 0
        )

        def stack(rows):
            return jnp.concatenate([rows[:, at : at + 128] for at in range(0, 512, 128)], 0)

        narrow_ref[...] = jnp.zeros(narrow_ref.shape, jnp.float32)
        context = context_ref[...]
        context_rows = stack(context)
        probs = prob_ref[...].reshape(512, 128)
        capped = capped_ref[...].reshape(512, 128)
        slope = probs * (1.0 - capped * capped) * root
        probs_turned = rounded_parts(probs.T, 2)
        query_turned = rounded_parts(stack(query_ref[...]).T, 2)
        keys = rounded_parts(keys_ref[...], 2)
        values = rounded_parts(values_ref[...], 2)
        low = [rounded_parts(low_ref[16 * piece : 16 * piece + 16], 2) for piece in range(3)]
        up_query = up_query_ref[...]
        context_low = context_low_ref[...]
        cot_low = []
        for obj in range(OBJ):
            lead_row = through[128 + obj : 129 + obj]
            cot = stack(lead * lead_row - pulled[:, obj : obj + 1] * through[:128])
            cot_parts = rounded_parts(cot, 2)
            cot_prob = dot_parts(cot_parts, values, 1, 1)
            cot_score = slope * (cot_prob - lane_sum(cot * context_rows))
            score_parts = rounded_parts(cot_score, 2)
            cot_query = dot_parts(score_parts, keys, 1, 0)
            query_parts = rounded_parts(cot_query, 2)
            keys_parts = rounded_parts(dot_parts(query_turned, score_parts, 1, 0), 2)
            values_parts = rounded_parts(dot_parts(probs_turned, cot_parts, 1, 0), 2)
            factor_query = 0.0
            jac_query = []
            for at in range(0, 512, 128):
                block = [part[at : at + 128] for part in query_parts]
                factor_query += dot_parts([up_query[:, at : at + 128]], block, 1, 1)
                jac_query.append(dot_parts(low[0], block, 1, 0))
            rows = [
                ADAPTER_SCALE * factor_query,
                ADAPTER_SCALE * dot_parts([up_kv_ref[0]], keys_parts, 1, 0),
                ADAPTER_SCALE * dot_parts([up_kv_ref[1]], values_parts, 1, 1),
                context_low,
            ]
            for piece in range(4):
                for half in range(2):
                    factors_ref[pl.ds(20 * half + 5 * piece + obj, 8, stride=40), :] = rows[
                        piece
                    ][8 * half : 8 * half + 8]
            blocks = jac_query + [
                dot_parts(low[1], keys_parts, 1, 1),
                dot_parts(low[2], values_parts, 1, 0),
            ]
            spots = [(obj, at) for at in range(0, 512, 128)] + [(10 + obj, 0), (10 + obj, 128)]
            for (row, at), block in zip(spots, blocks):
                for half in range(2):
                    narrow_ref[at // 128, pl.ds(128 * half + row, 8, stride=16), :] = (
                        ADAPTER_SCALE * block[8 * half : 8 * half + 8]
                    )
            cot_low.append(
                slow_turned[:16, 128 + obj : 129 + obj] * lead_turned
                - pulled_turned[obj : obj + 1] * low_turned
            )
        jac_down = ADAPTER_SCALE * dot_parts(
            rounded_parts(jnp.concatenate(cot_low, 0), 2), rounded_parts(context, 2), 1, 0
        )
        for obj in range(OBJ):
            for half in range(2):
                start = 16 * obj + 8 * half
                for tile in range(4):
                    narrow_ref[tile, pl.ds(128 * half + 5 + obj, 8, stride=16), :] = jac_down[
                        start : start + 8, 128 * tile : 128 * tile + 128
                    ]
        blank = jnp.zeros((15, 128), jnp.float32)
        repeated_ref[0] = jnp.concatenate([blank, pulled_turned[:5]] * 2, 0)
        repeated_ref[1] = jnp.broadcast_to(lead_turned, (40, 128))


def cotangents(lens, resid, output_weight, side, *others):
    length, width = resid.shape
    query_cols = output_weight.shape[0]

    def chunked(rows):
        return pl.BlockSpec((rows, COT_CHUNK), lambda step: (0, step))

    def fixed(array):
        zeros = (0,) * array.ndim
        return pl.BlockSpec(array.shape, lambda step: zeros)

    shapes = [
        jax.ShapeDtypeStruct((320, 128), jnp.float32),
        jax.ShapeDtypeStruct((4, 256, 128), jnp.float32),
        jax.ShapeDtypeStruct((8, 128), jnp.float32),
        jax.ShapeDtypeStruct((2, 40, 128), jnp.float32),
    ]
    return pl.pallas_call(
        cotangents_body,
        grid=(width // COT_CHUNK,),
        in_specs=[
            pl.BlockSpec(memory_space=pltpu.SMEM),
            chunked(length),
            chunked(query_cols),
            chunked(32),
        ]
        + [fixed(array) for array in others],
        out_specs=[fixed(shape) for shape in shapes],
        out_shape=shapes,
        scratch_shapes=[
            pltpu.VMEM((144, query_cols), jnp.float32),
            pltpu.VMEM((256, 128), jnp.float32),
            pltpu.VMEM((128, 128), jnp.float32),
        ],
        compiler_params=pltpu.CompilerParams(vmem_limit_bytes=40 * 2**20),
        name="cotangents",
    )(lens, resid, output_weight, side, *others)


def jacobian_body(
    factors_ref, tokens_ref, resid_ref, side_ref, repeated_ref, narrow_ref, payload_ref
):
    factors = jnp.sum(factors_ref[...], axis=0)
    row = lax.broadcasted_iota(jnp.int32, (40, 1), 0) % 20
    last = row >= 15
    left = jnp.concatenate(
        [jnp.where(last, 0.0, factors), jnp.where(last, -factors * repeated_ref[0], 0.0)], 1
    )
    left = rounded_parts(left, 2)
    lane = lax.broadcasted_iota(jnp.int32, (40, 16), 1)
    lead = rounded_parts(
        jnp.where(lane == row - 15, lane_sum(factors * repeated_ref[1]), 0.0), 2
    )

    def place(group, _):
        lanes = pl.ds(pl.multiple_of(group * LANES, LANES), LANES)
        right = jnp.concatenate([tokens_ref[:, lanes], resid_ref[:, lanes]], 0)
        rows = dot_parts(left, [right], 1, 0) + dot_parts(lead, [side_ref[16:, lanes]], 1, 0)
        below = jnp.concatenate(
            [narrow_ref[tile, pl.ds(pl.multiple_of(group * 16, 16), 16), :] for tile in range(4)], 1
        )
        payload_ref[group] = jnp.concatenate([rows, below], 0).astype(jnp.bfloat16)
        return 0

    lax.fori_loop(0, 16, place, 0)


def jacobian(*arrays):
    return pl.pallas_call(
        jacobian_body,
        in_specs=whole(len(arrays)),
        out_specs=pl.BlockSpec(memory_space=pltpu.VMEM),
        out_shape=jax.ShapeDtypeStruct((16, PIECE_ROWS, LANES), jnp.bfloat16),
        compiler_params=pltpu.CompilerParams(vmem_limit_bytes=24 * 2**20),
        name="jacobian",
    )(*arrays)


def assemble(part, every, start_a, start_bq, start_bkv, start_ao, start_bo):
    steps = 8
    shapes = [start_a, start_bq, start_bkv, start_ao, start_bo]
    blocks = [
        pl.BlockSpec((3, 16, 2 * LANES), lambda step: (0, 0, step)),
        pl.BlockSpec((16, LANES), lambda step: (0, step)),
        pl.BlockSpec((2, 16, HEAD_SIZE), lambda step: (0, 0, step)),
        pl.BlockSpec((16, LANES), lambda step: (0, step)),
        pl.BlockSpec((16, 2 * LANES), lambda step: (0, step)),
    ]
    return pl.pallas_call(
        assemble_body,
        grid=(steps,),
        in_specs=[
            pl.BlockSpec(memory_space=pltpu.SMEM),
            pl.BlockSpec(every.shape, lambda step: (0, 0, 0)),
        ]
        + blocks,
        out_specs=blocks,
        out_shape=[jax.ShapeDtypeStruct(shape.shape, jnp.float32) for shape in shapes],
        compiler_params=pltpu.CompilerParams(vmem_limit_bytes=32 * 2**20),
        name="assemble",
    )(part, every, start_a, start_bq, start_bkv, start_ao, start_bo)


def local(
    hidden,
    query_weight,
    key_value_weight,
    output_weight,
    head,
    lens,
    partner,
    adapter_down_qkv,
    adapter_up_query,
    adapter_up_key_value,
    adapter_down_output,
    adapter_up_output,
    initial_down_qkv,
    initial_up_query,
    initial_up_key_value,
    initial_down_output,
    initial_up_output,
):
    _, part_length, width = hidden.shape
    shards = lax.axis_size("tensor")
    groups = lax.axis_size("dp")
    tensor_rank = lax.axis_index("tensor")
    group_rank = lax.axis_index("dp")
    query_cols = query_weight.shape[1]
    heads = query_cols // HEAD_SIZE
    length = part_length * shards
    root = 1.0 / math.sqrt(HEAD_SIZE)

    down_qkv = jnp.transpose(adapter_down_qkv, (0, 2, 1))
    down_output = adapter_down_output.T.astype(jnp.float32)
    up_query = adapter_up_query.astype(jnp.float32)
    up_key_value = adapter_up_key_value.astype(jnp.float32)
    head_rows = head.T

    tokens = gather_by_exchange(hidden[0], "tensor").reshape(length, width)

    low = dot_halved(tokens, down_qkv.reshape(48, width), 1, 1)
    low_q, low_k, low_v = low[:, :16], low[:, 16:32], low[:, 32:]
    query = dot_halved(tokens, query_weight, 1, 0) + ADAPTER_SCALE * dot_entire(
        low_q, up_query, 1, 0
    )
    keys = dot_halved(tokens, key_value_weight[0], 1, 0) + ADAPTER_SCALE * dot_entire(
        low_k, up_key_value[0], 1, 0
    )
    values = dot_halved(tokens, key_value_weight[1], 1, 0) + ADAPTER_SCALE * dot_entire(
        low_v, up_key_value[1], 1, 0
    )
    query_split = query.reshape(length, heads, HEAD_SIZE)
    capped = jnp.tanh(
        jnp.einsum("qjd,kd->jqk", query_split, keys, precision=PRECISE) * (root / SCORE_CAP)
    )
    causal = jnp.arange(length)[:, None] >= jnp.arange(length)[None, :]
    weights = jnp.where(causal, jnp.exp(SCORE_CAP * capped), 0.0)
    probabilities = weights / jnp.sum(weights, axis=-1, keepdims=True)
    context_split = jnp.einsum("jqk,kd->qjd", probabilities, values, precision=PRECISE)
    context = context_split.reshape(length, query_cols)
    context_low = dot_entire(down_output, context, 1, 1)
    low_upper, low_lower = two_halves(ADAPTER_SCALE * context_low)
    out_terms = dot_halved(context.astype(jnp.bfloat16), output_weight, 1, 0) + dot_halved(
        jnp.concatenate([low_upper, low_lower], 0),
        jnp.concatenate([adapter_up_output, adapter_up_output], 0),
        0,
        0,
    )
    out_pieces = lax.all_to_all(
        out_terms.astype(jnp.bfloat16).reshape(shards, part_length, width), "tensor", 0, 0
    )
    resid_own = hidden[0].astype(jnp.float32) + jnp.sum(out_pieces.astype(jnp.float32), 0)
    resid = gather_by_exchange(resid_own.astype(jnp.bfloat16), "tensor").reshape(length, width)

    side = jnp.concatenate([adapter_up_output, head_rows, jnp.zeros((11, width), head.dtype)], 0)
    factors, narrow, rewards, repeated = cotangents(
        lens,
        resid,
        output_weight,
        side,
        query,
        keys,
        values,
        probabilities,
        capped,
        context,
        low.T,
        ADAPTER_SCALE * context_low,
        down_output,
        adapter_up_query,
        adapter_up_key_value,
    )
    factors = lax.all_to_all(factors.reshape(shards, 8 * OBJ, length), "tensor", 0, 0)
    payload = jacobian(factors, tokens, resid, side, repeated, narrow)
    spread = lax.all_to_all(payload, "dp", 0, 0)
    jac = (
        spread[:, : PIECES * OBJ]
        .reshape(groups, PIECES, OBJ, LANES)
        .transpose(0, 2, 1, 3)
        .reshape(groups * OBJ, PIECES * LANES)
    )

    own_a = lax.dynamic_slice(
        jnp.transpose(initial_down_qkv, (0, 2, 1)).reshape(3, 2, shards, width),
        (0, 0, tensor_rank, group_rank * LANES),
        (3, 2, 1, LANES),
    ).reshape(3, 2, LANES)
    own_bo = lax.dynamic_slice(
        initial_up_output.reshape(2, shards, width),
        (0, tensor_rank, group_rank * LANES),
        (2, 1, LANES),
    ).reshape(2, LANES)
    own_bq = lax.dynamic_slice(
        initial_up_query, (group_rank, tensor_rank * query_cols), (1, query_cols)
    )
    own_ao = lax.dynamic_slice(
        initial_down_output.T, (group_rank, tensor_rank * query_cols), (1, query_cols)
    )
    own_bkv = lax.dynamic_slice(
        initial_up_key_value, (0, group_rank, tensor_rank * HEAD_SIZE), (2, 1, HEAD_SIZE)
    )
    own_start = jnp.concatenate(
        [
            jnp.concatenate([own_a.transpose(1, 0, 2), own_bo[:, None]], 1).reshape(8, LANES),
            own_bq,
            own_ao,
            jnp.concatenate(
                [own_bkv.reshape(1, 2 * HEAD_SIZE), jnp.zeros((1, LANES - 2 * HEAD_SIZE))], 1
            ),
        ],
        0,
    ).reshape(1, PIECES * LANES)
    own_start = own_start.astype(jnp.float32)
    sequences = jnp.arange(groups)
    leads = sequences < partner
    order = jnp.sum((sequences[None, :] < sequences[:, None]) & leads[None, :], 1)
    chosen = (
        leads[None, :] & (order[None, :] == jnp.arange(groups // 2)[:, None])
    ).astype(jnp.float32)
    differences = chosen - jnp.take(chosen, partner, axis=1)
    pairs = (
        differences[:, None, :, None] * jnp.eye(OBJ, dtype=jnp.float32)[None, :, None, :]
    ).reshape(PAIR_ROWS, groups * OBJ)
    pairs = jnp.pad(pairs, ((0, PACK_ROWS - PAIR_ROWS), (0, 128 - groups * OBJ)))
    packed = pl.pallas_call(
        gram_body,
        in_specs=[pl.BlockSpec(memory_space=pltpu.SMEM)] + whole(4),
        out_specs=pl.BlockSpec(memory_space=pltpu.VMEM),
        out_shape=jax.ShapeDtypeStruct((16, 128), jnp.float32),
        compiler_params=pltpu.CompilerParams(vmem_limit_bytes=32 * 2**20),
        name="gram",
    )(
        jnp.stack([group_rank, tensor_rank]).astype(jnp.int32),
        jac,
        own_start,
        pairs,
        rewards,
    )
    packed = jnp.sum(gather_by_exchange(packed, "dp"), 0)
    packed = gather_by_exchange(packed, "tensor")
    own_result, part = pl.pallas_call(
        lanczos_body,
        in_specs=whole(3),
        out_specs=whole(2),
        out_shape=[
            jax.ShapeDtypeStruct((8, RESULT_LANES), jnp.bfloat16),
            jax.ShapeDtypeStruct((1, 128), jnp.float32),
        ],
        compiler_params=pltpu.CompilerParams(vmem_limit_bytes=32 * 2**20),
        name="lanczos",
    )(packed, pairs, jac)
    every = lax.all_to_all(
        jnp.broadcast_to(own_result[None], (groups * shards,) + own_result.shape),
        ("dp", "tensor"),
        0,
        0,
    )
    next_a, next_bq, next_bkv, next_ao, next_bo = assemble(
        part,
        every,
        jnp.transpose(initial_down_qkv, (0, 2, 1)),
        initial_up_query,
        initial_up_key_value,
        initial_down_output.T,
        initial_up_output,
    )
    return jnp.transpose(next_a, (0, 2, 1)), next_bq, next_bkv, next_ao.T, next_bo


def solution(mesh):
    in_specs = (
        P("dp", "tensor", None),
        P(None, "tensor"),
        P(None, None, "tensor"),
        P("tensor", None),
        P(),
        P("dp"),
        P(),
        P(),
        P(None, "tensor"),
        P(None, None, "tensor"),
        P("tensor", None),
        P(),
        P(),
        P(),
        P(),
        P(),
        P(),
    )
    out_specs = (P(), P(), P(), P(), P())
    return jax.shard_map(local, mesh=mesh, in_specs=in_specs, out_specs=out_specs, check_vma=False)
```

```python
import math

import jax
import jax.numpy as jnp
from jax import lax
from jax.experimental import pallas as pl
from jax.experimental.pallas import tpu as pltpu
from jax.sharding import PartitionSpec as P

HEAD_SIZE = 128
NPARAM = 688128
ADAPTER_SCALE = 2.0
NORM_EPS = 1e-05
LANCZOS_EPS = 1e-06
SCORE_CAP = 30.0
PRECISE = lax.Precision.HIGHEST
OBJ = 5
PIECES = 11
PIECE_ROWS = 56
LANES = 512


def dot_halved(left_side, right_side, left_dim, right_dim):
    return lax.dot_general(
        left_side,
        right_side,
        (((left_dim,), (right_dim,)), ((), ())),
        preferred_element_type=jnp.float32,
    )


def dot_entire(left_side, right_side, left_dim, right_dim):
    return lax.dot_general(
        left_side,
        right_side,
        (((left_dim,), (right_dim,)), ((), ())),
        precision=PRECISE,
        preferred_element_type=jnp.float32,
    )


def gather_by_exchange(block, axis):
    count = lax.axis_size(axis)
    copies = jnp.broadcast_to(block[None], (count,) + block.shape)
    return lax.all_to_all(copies, axis, 0, 0)


PAIR_ROWS = 40
PACK_ROWS = 48
PACK_LANES = 42
RESULT_LANES = 768


def rounded_parts(entire, count):
    parts = []
    for _ in range(count):
        part = entire.astype(jnp.bfloat16)
        parts.append(part)
        entire = entire - part.astype(jnp.float32)
    return parts


def lane_sum(values):
    return jnp.sum(values, axis=1, keepdims=True)


def row_sum(values):
    return jnp.sum(values, axis=0, keepdims=True)


def gram_body(rank_ref, jac_ref, start_ref, pairs_ref, rewards_ref, packed_ref):
    jac = jac_ref[...]
    start = start_ref[...]
    pairs = pairs_ref[...]
    rows = jac.shape[0]
    gram = dot_halved(jac, jac, 1, 1)
    starts = jnp.concatenate(rounded_parts(start, 3), 0)
    along = lane_sum(dot_halved(jac, starts, 1, 1))
    own_pairs = pairs[:, :rows]
    gram = dot_entire(dot_entire(own_pairs, gram, 1, 0), own_pairs, 1, 1)
    along = dot_entire(own_pairs, jnp.broadcast_to(along, (rows, 128)), 1, 0)
    rewards = pltpu.roll(rewards_ref[...], OBJ * rank_ref[0], axis=1)[:1]
    rewards = jnp.where(rank_ref[1] == 0, rewards, 0.0)
    apart = lane_sum(pairs * rewards)
    square = jnp.sum(start * start)
    lane = lax.broadcasted_iota(jnp.int32, (PACK_ROWS, 128), 1)
    row = lax.broadcasted_iota(jnp.int32, (PACK_ROWS, 128), 0)
    wide = jnp.concatenate([gram, jnp.zeros((PACK_ROWS, 128 - PACK_ROWS), jnp.float32)], 1)
    wide = jnp.where(lane < PAIR_ROWS, wide, 0.0)
    wide = jnp.where(lane == PAIR_ROWS, along, wide)
    wide = jnp.where(lane == PAIR_ROWS + 1, apart, wide)
    wide = jnp.where((row == PAIR_ROWS) & (lane == 0), square, wide)
    packed_ref[...] = (
        wide[:16]
        + pltpu.roll(wide[16:32], PACK_LANES, axis=1)
        + pltpu.roll(wide[32:], 2 * PACK_LANES, axis=1)
    )


def lanczos_body(packed_ref, pairs_ref, jac_ref, result_ref, part_ref):
    packed = jnp.sum(packed_ref[...], axis=0)
    wide = jnp.concatenate(
        [
            packed,
            pltpu.roll(packed, 128 - PACK_LANES, axis=1),
            pltpu.roll(packed, 128 - 2 * PACK_LANES, axis=1),
        ],
        0,
    )
    lane = lax.broadcasted_iota(jnp.int32, (PACK_ROWS, 128), 1)
    row = lax.broadcasted_iota(jnp.int32, (PACK_ROWS, 128), 0)
    inside = row < PAIR_ROWS
    gram = jnp.where(inside & (lane < PAIR_ROWS), wide, 0.0)
    along = lane_sum(jnp.where(inside & (lane == PAIR_ROWS), wide, 0.0))
    apart = lane_sum(jnp.where(inside & (lane == PAIR_ROWS + 1), wide, 0.0))
    picked = jnp.where((row == PAIR_ROWS) & (lane == 0), wide, 0.0)
    start_square = lane_sum(row_sum(picked)) / NPARAM
    diagonal = row == lane

    def gram_times(column):
        across = row_sum(jnp.where(diagonal, column, 0.0))
        return lane_sum(gram * across)

    def inner(left_side, right_side):
        return row_sum(left_side * right_side) / NPARAM

    decayed = jnp.exp(-jnp.abs(apart))
    curvature = decayed / ((1.0 + decayed) * (1.0 + decayed)) / (16 // 2)
    start_scale = lax.rsqrt(start_square + LANCZOS_EPS)
    first_square = start_square * start_scale * start_scale
    along_one = along * start_scale
    pull_one = curvature * along_one
    alpha_one = inner(pull_one, along_one)
    gram_pull = gram_times(pull_one)
    beta_one = jnp.sqrt(
        inner(pull_one, gram_pull) - alpha_one * alpha_one * (2.0 - first_square) + LANCZOS_EPS
    )
    along_two = (gram_pull - alpha_one * along_one) / beta_one
    pull_two = curvature * along_two
    first_second = alpha_one * (1.0 - first_square) / beta_one
    alpha_two = inner(pull_two, along_two) - beta_one * first_second
    mixed = pull_two - (alpha_two / beta_one) * pull_one
    first_part = alpha_two * alpha_one / beta_one - beta_one
    beta_two = jnp.sqrt(
        inner(mixed, gram_times(mixed))
        + 2.0 * first_part * inner(mixed, along_one)
        + first_part * first_part * first_square
        + LANCZOS_EPS
    )
    part_ref[...] = jnp.broadcast_to(first_part * start_scale / beta_two, part_ref.shape)
    across = row_sum(pairs_ref[...] * (mixed / beta_two))
    jac = jac_ref[...]
    rows = jac.shape[0]
    parts = rounded_parts(jnp.broadcast_to(across[:, :rows], (8, rows)), 3)
    result = sum(dot_halved(part, jac, 1, 0) for part in parts)[:1]
    spare = jnp.zeros((6, 128), jnp.float32)

    def chunks(start, count, size):
        return [result[:, start + size * step : start + size * (step + 1)] for step in range(count)]

    main = jnp.concatenate(chunks(0, 8, LANES), 0)
    middle = jnp.concatenate(chunks(8 * LANES, 8, 128), 0)
    last = jnp.concatenate(chunks(10 * LANES, 2, 128) + [spare], 0)
    result_ref[...] = jnp.concatenate([main, middle, last], 1).astype(jnp.bfloat16)


def assemble_body(
    part_ref,
    every_ref,
    a_ref,
    bq_ref,
    bkv_ref,
    ao_ref,
    bo_ref,
    out_a_ref,
    out_bq_ref,
    out_bkv_ref,
    out_ao_ref,
    out_bo_ref,
):
    step = pl.program_id(0)
    part = part_ref[0, 0]

    def one_hot(size, first, second):
        row = lax.broadcasted_iota(jnp.int32, (size, size), 0)
        lane = lax.broadcasted_iota(jnp.int32, (size, size), 1)
        wanted = (row % second) * first + row // second
        return jnp.where(lane == wanted, 1.0, 0.0).astype(jnp.bfloat16)

    row = lax.broadcasted_iota(jnp.int32, (64, 64), 0)
    lane = lax.broadcasted_iota(jnp.int32, (64, 64), 1)
    wanted = (row % 8) * 8 + ((row % 16) // 8) * 4 + row // 16
    moved = jnp.where(lane == wanted, 1.0, 0.0).astype(jnp.bfloat16)
    for half in range(2):
        group = 2 * step + half
        block = every_ref[pl.ds(8 * group, 8), :, :LANES].reshape(64, LANES)
        placed = dot_halved(moved, block, 1, 0).reshape(4, 16, LANES)
        lanes = slice(half * LANES, (half + 1) * LANES)
        out_a_ref[:, :, lanes] = placed[:3] + part * a_ref[:, :, lanes]
        out_bo_ref[:, lanes] = placed[3] + part * bo_ref[:, lanes]
    block = jnp.concatenate(
        [every_ref[8 * group + step, :, LANES:] for group in range(16)], 0
    )
    placed = dot_halved(one_hot(128, 8, 16), block, 1, 0)
    for chunk in range(4):
        lanes = slice(chunk * 128, (chunk + 1) * 128)
        out_bq_ref[:, lanes] = placed[16 * chunk : 16 * chunk + 16, :128] + part * bq_ref[:, lanes]
        out_ao_ref[:, lanes] = (
            placed[64 + 16 * chunk : 80 + 16 * chunk, :128] + part * ao_ref[:, lanes]
        )
    out_bkv_ref[0] = placed[:16, 128:] + part * bkv_ref[0]
    out_bkv_ref[1] = placed[16:32, 128:] + part * bkv_ref[1]


def whole(count):
    return [pl.BlockSpec(memory_space=pltpu.VMEM)] * count


def product(left, right, right_dim):
    left_both = jnp.concatenate(rounded_parts(left, 2), 1)
    upper, lower = rounded_parts(right, 2)
    if right_dim == 0:
        rows = jnp.concatenate([upper, lower], 1)
        both = dot_halved(left_both, jnp.concatenate([rows, rows], 0), 1, 0)
    else:
        rows = jnp.concatenate([upper, lower], 0)
        both = dot_halved(left_both, jnp.concatenate([rows, rows], 1), 1, 1)
    size = right.shape[1 - right_dim]
    return both[:, :size] + both[:, size:]


def tall(parts):
    return jnp.concatenate(parts, 0)


def flat(parts):
    return jnp.concatenate(parts, 1)


def corners(both, rows, lanes):
    upper = both[:rows] + both[rows:]
    return upper[:, :lanes] + upper[:, lanes:]


def stack(rows):
    return tall([rows[:, at : at + 128] for at in range(0, rows.shape[1], 128)])


def unstack(rows):
    return flat([rows[at : at + 128] for at in range(0, rows.shape[0], 128)])


def place_shards(spots_ref, whole_ref, shards, first_half):
    for at in range(6):
        rows = pl.ds(pl.multiple_of(spots_ref[at] * 16, 16), 16)
        whole_ref[rows, :] = shards[at][...]
    for at in range(2):
        rows = pl.ds(pl.multiple_of(spots_ref[6 + at] * 16, 16), 16)
        whole_ref[rows, :] = jnp.where(
            first_half, shards[6 + 2 * at][...], shards[7 + 2 * at][...]
        )


def shard_specs(last_step):
    half = last_step // 2
    full = pl.BlockSpec((16, CHUNK), lambda step: (0, jnp.minimum(step, last_step)))
    early = pl.BlockSpec((16, CHUNK), lambda step: (0, jnp.minimum(step, half)))
    late = pl.BlockSpec(
        (16, CHUNK), lambda step: (0, jnp.clip(step - half - 1, 0, last_step - half - 1))
    )
    return [full] * 6 + [early, late] * 2


def gather_by_relays(block):
    half = block.shape[1] // 2

    def permute(array, y_step, z_step):
        pairs = [
            (at, ((at // 4 + y_step) % 2) * 4 + (at % 4 + z_step) % 4) for at in range(8)
        ]
        return lax.ppermute(array, "tensor", pairs)

    across = permute(block, 1, 0)
    below = permute(block, 0, 1)
    above = permute(block, 0, 3)
    across_below = permute(across, 0, 1)
    across_above = permute(across, 0, 3)
    far = [permute(below[:, :half], 0, 1), permute(above[:, half:], 0, 3)]
    across_far = [
        permute(across_below[:, :half], 0, 1),
        permute(across_above[:, half:], 0, 3),
    ]
    return [block, across, below, above, across_below, across_above] + far + across_far


def shard_spots():
    rank = lax.axis_index("tensor").astype(jnp.int32)
    y, z = rank // 4 * 4, rank % 4
    other = 4 - y
    return jnp.stack(
        [
            y + z,
            other + z,
            y + (z + 3) % 4,
            y + (z + 1) % 4,
            other + (z + 3) % 4,
            other + (z + 1) % 4,
            y + (z + 2) % 4,
            other + (z + 2) % 4,
        ]
    )


CHUNK = 2048


def forward_body(
    spots_ref,
    shard_0,
    shard_1,
    shard_2,
    shard_3,
    shard_4,
    shard_5,
    shard_6,
    shard_7,
    shard_8,
    shard_9,
    query_weight_ref,
    kv_weight_ref,
    down_ref,
    output_weight_ref,
    up_output_ref,
    down_output_ref,
    up_query_ref,
    up_kv_ref,
    tokens_ref,
    out_ref,
    query_ref,
    keys_ref,
    values_ref,
    prob_ref,
    capped_ref,
    context_ref,
    low_ref,
    context_low_ref,
    query_sum,
    kv_sum,
    low_sum,
    halved_ref,
    halved_low_ref,
):
    step = pl.program_id(0)
    steps = pl.num_programs(0) // 2
    shards = [
        shard_0,
        shard_1,
        shard_2,
        shard_3,
        shard_4,
        shard_5,
        shard_6,
        shard_7,
        shard_8,
        shard_9,
    ]

    @pl.when(step < steps)
    def _():
        place_shards(spots_ref, tokens_ref, shards, step < steps // 2)
        tokens = tokens_ref[...]
        query = dot_halved(tokens, query_weight_ref[...], 1, 0)
        kv = dot_halved(tokens, flat([kv_weight_ref[0], kv_weight_ref[1]]), 1, 0)
        low = dot_halved(down_ref[...], tokens, 1, 1)

        @pl.when(step == 0)
        def _():
            query_sum[...] = query
            kv_sum[...] = kv
            low_sum[...] = jnp.zeros(low_sum.shape, jnp.float32)
            low_sum[:48] = low

        @pl.when(step > 0)
        def _():
            query_sum[...] += query
            kv_sum[...] += kv
            low_sum[:48] += low

    @pl.when(step == steps - 1)
    def _():
        low_turned = low_sum[...]
        low = low_turned.T
        low_ref[...] = low_turned[:48]
        root = 1.0 / math.sqrt(HEAD_SIZE)

        def adapted(total, piece, up):
            parts = rounded_parts(low[:, 16 * piece : 16 * piece + 16], 2)
            return total + ADAPTER_SCALE * dot_halved(flat(parts), tall([up, up]), 1, 0)

        query = adapted(query_sum[...], 0, up_query_ref[...])
        keys = adapted(kv_sum[:, :128], 1, up_kv_ref[0])
        values = adapted(kv_sum[:, 128:], 2, up_kv_ref[1])
        capped = jnp.tanh(product(stack(query), keys, 1) * (root / SCORE_CAP))
        row = lax.broadcasted_iota(jnp.int32, (512, 128), 0) % 128
        lane = lax.broadcasted_iota(jnp.int32, (512, 128), 1)
        weights = jnp.where(row >= lane, jnp.exp(SCORE_CAP * capped), 0.0)
        probs = weights / lane_sum(weights)
        context = unstack(product(probs, values, 0))
        low_pair = dot_halved(down_output_ref[...], tall(rounded_parts(context, 2)), 1, 1)
        context_low = ADAPTER_SCALE * (low_pair[:, :128] + low_pair[:, 128:])
        query_ref[...] = query
        keys_ref[...] = keys
        values_ref[...] = values
        prob_ref[...] = probs
        capped_ref[...] = capped
        context_ref[...] = context
        context_low_ref[...] = context_low
        halved_ref[...] = context.astype(jnp.bfloat16)
        turned = tall([context_low, jnp.zeros((112, 128), jnp.float32)]).T[:, :16]
        halved_low_ref[...] = flat(rounded_parts(turned, 2))

    @pl.when(step >= steps)
    def _():
        up = up_output_ref[...]
        terms = dot_halved(halved_ref[...], output_weight_ref[...], 1, 0) + dot_halved(
            halved_low_ref[...], tall([up, up]), 1, 0
        )
        out_ref[...] = terms.astype(jnp.bfloat16).reshape(out_ref.shape)


def fixed(array):
    zeros = (0,) * array.ndim
    return pl.BlockSpec(array.shape, lambda step: zeros)


def forward(
    spots,
    shards,
    query_weight,
    key_value_weight,
    down_rows,
    output_weight,
    up_output,
    down_output,
    up_query,
    up_key_value,
):
    width = shards[0].shape[1]
    steps = width // CHUNK
    last = steps - 1
    query_cols = query_weight.shape[1]

    def first_part(step):
        return jnp.minimum(step, last)

    def second_part(step):
        return jnp.maximum(step - steps, 0)

    shapes = [
        jax.ShapeDtypeStruct((128, width), jnp.bfloat16),
        jax.ShapeDtypeStruct((8, 16, width), jnp.bfloat16),
        jax.ShapeDtypeStruct((128, query_cols), jnp.float32),
        jax.ShapeDtypeStruct((128, 128), jnp.float32),
        jax.ShapeDtypeStruct((128, 128), jnp.float32),
        jax.ShapeDtypeStruct((512, 128), jnp.float32),
        jax.ShapeDtypeStruct((512, 128), jnp.float32),
        jax.ShapeDtypeStruct((128, query_cols), jnp.float32),
        jax.ShapeDtypeStruct((48, 128), jnp.float32),
        jax.ShapeDtypeStruct((16, 128), jnp.float32),
    ]
    return pl.pallas_call(
        forward_body,
        grid=(2 * steps,),
        in_specs=[pl.BlockSpec(memory_space=pltpu.SMEM)]
        + shard_specs(last)
        + [
            pl.BlockSpec((CHUNK, query_cols), lambda step: (first_part(step), 0)),
            pl.BlockSpec((2, CHUNK, 128), lambda step: (0, first_part(step), 0)),
            pl.BlockSpec((48, CHUNK), lambda step: (0, first_part(step))),
            pl.BlockSpec((query_cols, CHUNK), lambda step: (0, second_part(step))),
            pl.BlockSpec((16, CHUNK), lambda step: (0, second_part(step))),
            fixed(down_output),
            fixed(up_query),
            fixed(up_key_value),
        ],
        out_specs=[
            pl.BlockSpec((128, CHUNK), lambda step: (0, first_part(step))),
            pl.BlockSpec((8, 16, CHUNK), lambda step: (0, 0, second_part(step))),
        ]
        + [fixed(shape) for shape in shapes[2:]],
        out_shape=shapes,
        scratch_shapes=[
            pltpu.VMEM((128, query_cols), jnp.float32),
            pltpu.VMEM((128, 256), jnp.float32),
            pltpu.VMEM((128, 128), jnp.float32),
            pltpu.VMEM((128, query_cols), jnp.bfloat16),
            pltpu.VMEM((128, 32), jnp.bfloat16),
        ],
        compiler_params=pltpu.CompilerParams(vmem_limit_bytes=24 * 2**20),
        name="forward",
    )(
        spots,
        *shards,
        query_weight,
        key_value_weight,
        down_rows,
        output_weight,
        up_output,
        down_output,
        up_query,
        up_key_value,
    )


def cotangents_body(
    lens_ref,
    spots_ref,
    shard_0,
    shard_1,
    shard_2,
    shard_3,
    shard_4,
    shard_5,
    shard_6,
    shard_7,
    shard_8,
    shard_9,
    weight_ref,
    side_ref,
    query_ref,
    keys_ref,
    values_ref,
    prob_ref,
    capped_ref,
    context_ref,
    low_ref,
    context_low_ref,
    down_ref,
    up_query_ref,
    up_kv_ref,
    resid_ref,
    factors_ref,
    narrow_ref,
    rewards_ref,
    repeated_ref,
    through_ref,
    slow_ref,
    square_ref,
):
    step = pl.program_id(0)
    shards = [
        shard_0,
        shard_1,
        shard_2,
        shard_3,
        shard_4,
        shard_5,
        shard_6,
        shard_7,
        shard_8,
        shard_9,
    ]
    place_shards(spots_ref, resid_ref, shards, step < pl.num_programs(0) // 2)
    chunk = resid_ref[...]
    side = side_ref[...]
    left = tall([chunk, side[16:]])
    through = dot_halved(left, weight_ref[...], 1, 1)
    slow = dot_halved(left, side, 1, 1)
    wide = chunk.astype(jnp.float32)
    square = jnp.zeros((128, 128), jnp.float32)
    for at in range(0, chunk.shape[1], 128):
        square = square + wide[:, at : at + 128] * wide[:, at : at + 128]

    @pl.when(step == 0)
    def _():
        slow_ref[...] = jnp.zeros(slow_ref.shape, jnp.float32)
        through_ref[...] = through
        slow_ref[:144, :32] = slow
        square_ref[...] = square

    @pl.when(step > 0)
    def _():
        through_ref[...] += through
        slow_ref[:144, :32] += slow
        square_ref[...] += square

    @pl.when(step == pl.num_programs(0) - 1)
    def _():
        width = chunk.shape[1] * pl.num_programs(0)
        length_own = lens_ref[0]
        root = 1.0 / math.sqrt(HEAD_SIZE)
        slow = slow_ref[...]
        slow_turned = slow.T
        square = square_ref[...]
        inverse = lax.rsqrt(lane_sum(square) / width + NORM_EPS)
        inverse_turned = lax.rsqrt(row_sum(square.T) / width + NORM_EPS)
        each = 1.0 / jnp.broadcast_to(length_own, (1, 1)).astype(jnp.float32)
        share = jnp.where(
            lax.broadcasted_iota(jnp.int32, (128, 1), 0) < length_own, each, 0.0
        )
        share_turned = jnp.where(
            lax.broadcasted_iota(jnp.int32, (1, 128), 1) < length_own, each, 0.0
        )
        logits = inverse * slow[:128, 16:32]
        lead = share * inverse
        pulled = lead * inverse * logits / width
        lead_turned = share_turned * inverse_turned
        pulled_turned = (
            lead_turned * inverse_turned * inverse_turned * slow_turned[16:32, :128] / width
        )
        low_turned = slow_turned[:16, :128]
        rewards_ref[...] = jnp.zeros(rewards_ref.shape, jnp.float32)
        rewards_ref[:1, :16] = row_sum(share * logits)
        down = down_ref[...]
        through = through_ref[...] + ADAPTER_SCALE * dot_halved(
            flat(rounded_parts(slow[:144, :16], 2)), tall([down, down]), 1, 0
        )
        narrow_ref[...] = jnp.zeros(narrow_ref.shape, jnp.float32)
        context = context_ref[...]
        context_rows = stack(context)
        probs = prob_ref[...]
        capped = capped_ref[...]
        slope = probs * (1.0 - capped * capped) * root
        probs_turned = tall(rounded_parts(probs.T, 2))
        query_turned = tall(rounded_parts(stack(query_ref[...]).T, 2))
        keys = keys_ref[...]
        values = values_ref[...]
        low = [tall(rounded_parts(low_ref[16 * at : 16 * at + 16], 2)) for at in range(3)]
        up_query = up_query_ref[...]
        context_low = context_low_ref[...]
        cot_low = []
        for obj in range(OBJ):
            lead_row = through[128 + obj : 129 + obj]
            cot = stack(lead * lead_row - pulled[:, obj : obj + 1] * through[:128])
            cot_prob = product(cot, values, 1)
            cot_score = slope * (cot_prob - lane_sum(cot * context_rows))
            cot_query = unstack(product(cot_score, keys, 0))
            cot_keys = corners(
                dot_halved(query_turned, flat(rounded_parts(cot_score, 2)), 1, 0), 128, 128
            )
            cot_values = corners(
                dot_halved(probs_turned, flat(rounded_parts(cot, 2)), 1, 0), 128, 128
            )
            query_parts = rounded_parts(cot_query, 2)
            keys_parts = rounded_parts(cot_keys, 2)
            values_parts = rounded_parts(cot_values, 2)
            factor_query = dot_halved(up_query, tall(query_parts), 1, 1)
            factor_keys = dot_halved(up_kv_ref[0], flat(keys_parts), 1, 0)
            factor_values = dot_halved(up_kv_ref[1], tall(values_parts), 1, 1)
            rows = [
                ADAPTER_SCALE * (factor[:, :128] + factor[:, 128:])
                for factor in (factor_query, factor_keys, factor_values)
            ] + [context_low]
            for piece in range(4):
                for half in range(2):
                    factors_ref[pl.ds(20 * half + 5 * piece + obj, 8, stride=40), :] = rows[
                        piece
                    ][8 * half : 8 * half + 8]
            jac_query = corners(dot_halved(low[0], flat(query_parts), 1, 0), 16, 512)
            jac_keys = corners(dot_halved(low[1], tall(keys_parts), 1, 1), 16, 128)
            jac_values = corners(dot_halved(low[2], flat(values_parts), 1, 0), 16, 128)
            blocks = [jac_query[:, at : at + 128] for at in range(0, 512, 128)]
            spots = [(obj, 0), (obj, 1), (obj, 2), (obj, 3), (10 + obj, 0), (10 + obj, 1)]
            for (row, tile), block in zip(spots, blocks + [jac_keys, jac_values]):
                for half in range(2):
                    narrow_ref[tile, pl.ds(128 * half + row, 8, stride=16), :] = (
                        ADAPTER_SCALE * block[8 * half : 8 * half + 8]
                    )
            cot_low.append(
                slow_turned[:16, 128 + obj : 129 + obj] * lead_turned
                - pulled_turned[obj : obj + 1] * low_turned
            )
        jac_down = ADAPTER_SCALE * product(tall(cot_low), context, 0)
        for obj in range(OBJ):
            for half in range(2):
                start = 16 * obj + 8 * half
                for tile in range(4):
                    narrow_ref[tile, pl.ds(128 * half + 5 + obj, 8, stride=16), :] = jac_down[
                        start : start + 8, 128 * tile : 128 * tile + 128
                    ]
        blank = jnp.zeros((15, 128), jnp.float32)
        repeated_ref[0] = jnp.concatenate([blank, pulled_turned[:5]] * 2, 0)
        repeated_ref[1] = jnp.broadcast_to(lead_turned, (40, 128))


def cotangents(lens, spots, shards, output_weight, side, *others):
    width = shards[0].shape[1]
    query_cols = output_weight.shape[0]
    steps = width // CHUNK

    def chunked(rows):
        return pl.BlockSpec((rows, CHUNK), lambda step: (0, step))

    shapes = [
        jax.ShapeDtypeStruct((128, width), jnp.bfloat16),
        jax.ShapeDtypeStruct((320, 128), jnp.float32),
        jax.ShapeDtypeStruct((4, 256, 128), jnp.float32),
        jax.ShapeDtypeStruct((8, 128), jnp.float32),
        jax.ShapeDtypeStruct((2, 40, 128), jnp.float32),
    ]
    return pl.pallas_call(
        cotangents_body,
        grid=(steps,),
        in_specs=[pl.BlockSpec(memory_space=pltpu.SMEM)] * 2
        + shard_specs(steps - 1)
        + [chunked(query_cols), chunked(32)]
        + [fixed(array) for array in others],
        out_specs=[chunked(128)] + [fixed(shape) for shape in shapes[1:]],
        out_shape=shapes,
        scratch_shapes=[
            pltpu.VMEM((144, query_cols), jnp.float32),
            pltpu.VMEM((256, 128), jnp.float32),
            pltpu.VMEM((128, 128), jnp.float32),
        ],
        compiler_params=pltpu.CompilerParams(vmem_limit_bytes=20 * 2**20),
        name="cotangents",
    )(lens, spots, *shards, output_weight, side, *others)


def jacobian_body(
    factors_ref, tokens_ref, resid_ref, side_ref, repeated_ref, narrow_ref, payload_ref
):
    factors = jnp.sum(factors_ref[...], axis=0)
    row = lax.broadcasted_iota(jnp.int32, (40, 1), 0) % 20
    last = row >= 15
    left = flat([jnp.where(last, 0.0, factors), jnp.where(last, -factors * repeated_ref[0], 0.0)])
    lane = lax.broadcasted_iota(jnp.int32, (40, 16), 1)
    lead = jnp.where(lane == row - 15, lane_sum(factors * repeated_ref[1]), 0.0)

    def both(rows):
        upper = rows.astype(jnp.bfloat16).astype(jnp.float32)
        return tall([upper, rows - upper]).astype(jnp.bfloat16)

    left = both(left)
    lead = both(lead)

    def place(group, _):
        lanes = pl.ds(pl.multiple_of(group * LANES, LANES), LANES)
        right = tall([tokens_ref[:, lanes], resid_ref[:, lanes]])
        pair = dot_halved(left, right, 1, 0) + dot_halved(lead, side_ref[16:, lanes], 1, 0)
        below = flat(
            [narrow_ref[tile, pl.ds(pl.multiple_of(group * 16, 16), 16), :] for tile in range(4)]
        )
        payload_ref[group] = tall([pair[:40] + pair[40:], below]).astype(jnp.bfloat16)
        return 0

    lax.fori_loop(0, 16, place, 0, unroll=4)


def jacobian(*arrays):
    return pl.pallas_call(
        jacobian_body,
        in_specs=whole(len(arrays)),
        out_specs=pl.BlockSpec(memory_space=pltpu.VMEM),
        out_shape=jax.ShapeDtypeStruct((16, PIECE_ROWS, LANES), jnp.bfloat16),
        compiler_params=pltpu.CompilerParams(vmem_limit_bytes=12 * 2**20),
        name="jacobian",
    )(*arrays)


def assemble(part, every, start_a, start_bq, start_bkv, start_ao, start_bo):
    steps = 8
    shapes = [start_a, start_bq, start_bkv, start_ao, start_bo]
    blocks = [
        pl.BlockSpec((3, 16, 2 * LANES), lambda step: (0, 0, step)),
        pl.BlockSpec((16, LANES), lambda step: (0, step)),
        pl.BlockSpec((2, 16, HEAD_SIZE), lambda step: (0, 0, step)),
        pl.BlockSpec((16, LANES), lambda step: (0, step)),
        pl.BlockSpec((16, 2 * LANES), lambda step: (0, step)),
    ]
    return pl.pallas_call(
        assemble_body,
        grid=(steps,),
        in_specs=[
            pl.BlockSpec(memory_space=pltpu.SMEM),
            pl.BlockSpec(every.shape, lambda step: (0, 0, 0)),
        ]
        + blocks,
        out_specs=blocks,
        out_shape=[jax.ShapeDtypeStruct(shape.shape, jnp.float32) for shape in shapes],
        compiler_params=pltpu.CompilerParams(vmem_limit_bytes=14 * 2**20),
        name="assemble",
    )(part, every, start_a, start_bq, start_bkv, start_ao, start_bo)


def local(
    hidden,
    query_weight,
    key_value_weight,
    output_weight,
    head,
    lens,
    partner,
    adapter_down_qkv,
    adapter_up_query,
    adapter_up_key_value,
    adapter_down_output,
    adapter_up_output,
    initial_down_qkv,
    initial_up_query,
    initial_up_key_value,
    initial_down_output,
    initial_up_output,
):
    _, part_length, width = hidden.shape
    shards = lax.axis_size("tensor")
    groups = lax.axis_size("dp")
    tensor_rank = lax.axis_index("tensor")
    group_rank = lax.axis_index("dp")
    query_cols = query_weight.shape[1]
    length = part_length * shards

    down_rows = jnp.transpose(adapter_down_qkv, (0, 2, 1)).reshape(48, width)
    down_output = adapter_down_output.T
    head_rows = head.T
    spots = shard_spots()
    side = jnp.concatenate([adapter_up_output, head_rows, jnp.zeros((11, width), head.dtype)], 0)
    (
        tokens,
        out_terms,
        query,
        keys,
        values,
        probabilities,
        capped,
        context,
        low,
        context_low,
    ) = forward(
        spots,
        gather_by_relays(hidden[0]),
        query_weight,
        key_value_weight,
        down_rows,
        output_weight,
        adapter_up_output,
        down_output,
        adapter_up_query,
        adapter_up_key_value,
    )
    out_pieces = lax.all_to_all(out_terms, "tensor", 0, 0)
    resid_own = hidden[0].astype(jnp.float32) + jnp.sum(out_pieces.astype(jnp.float32), 0)
    resid, factors, narrow, rewards, repeated = cotangents(
        lens,
        spots,
        gather_by_relays(resid_own.astype(jnp.bfloat16)),
        output_weight,
        side,
        query,
        keys,
        values,
        probabilities,
        capped,
        context,
        low,
        context_low,
        down_output,
        adapter_up_query,
        adapter_up_key_value,
    )
    factors = lax.all_to_all(factors.reshape(shards, 8 * OBJ, length), "tensor", 0, 0)
    payload = jacobian(factors, tokens, resid, side, repeated, narrow)
    spread = lax.all_to_all(payload, "dp", 0, 0)
    jac = (
        spread[:, : PIECES * OBJ]
        .reshape(groups, PIECES, OBJ, LANES)
        .transpose(0, 2, 1, 3)
        .reshape(groups * OBJ, PIECES * LANES)
    )

    own_a = lax.dynamic_slice(
        jnp.transpose(initial_down_qkv, (0, 2, 1)).reshape(3, 2, shards, width),
        (0, 0, tensor_rank, group_rank * LANES),
        (3, 2, 1, LANES),
    ).reshape(3, 2, LANES)
    own_bo = lax.dynamic_slice(
        initial_up_output.reshape(2, shards, width),
        (0, tensor_rank, group_rank * LANES),
        (2, 1, LANES),
    ).reshape(2, LANES)
    own_bq = lax.dynamic_slice(
        initial_up_query, (group_rank, tensor_rank * query_cols), (1, query_cols)
    )
    own_ao = lax.dynamic_slice(
        initial_down_output.T, (group_rank, tensor_rank * query_cols), (1, query_cols)
    )
    own_bkv = lax.dynamic_slice(
        initial_up_key_value, (0, group_rank, tensor_rank * HEAD_SIZE), (2, 1, HEAD_SIZE)
    )
    own_start = jnp.concatenate(
        [
            jnp.concatenate([own_a.transpose(1, 0, 2), own_bo[:, None]], 1).reshape(8, LANES),
            own_bq,
            own_ao,
            jnp.concatenate(
                [own_bkv.reshape(1, 2 * HEAD_SIZE), jnp.zeros((1, LANES - 2 * HEAD_SIZE))], 1
            ),
        ],
        0,
    ).reshape(1, PIECES * LANES)
    own_start = own_start.astype(jnp.float32)
    sequences = jnp.arange(groups)
    leads = sequences < partner
    order = jnp.sum((sequences[None, :] < sequences[:, None]) & leads[None, :], 1)
    chosen = (
        leads[None, :] & (order[None, :] == jnp.arange(groups // 2)[:, None])
    ).astype(jnp.float32)
    differences = chosen - jnp.take(chosen, partner, axis=1)
    pairs = (
        differences[:, None, :, None] * jnp.eye(OBJ, dtype=jnp.float32)[None, :, None, :]
    ).reshape(PAIR_ROWS, groups * OBJ)
    pairs = jnp.pad(pairs, ((0, PACK_ROWS - PAIR_ROWS), (0, 128 - groups * OBJ)))
    packed = pl.pallas_call(
        gram_body,
        in_specs=[pl.BlockSpec(memory_space=pltpu.SMEM)] + whole(4),
        out_specs=pl.BlockSpec(memory_space=pltpu.VMEM),
        out_shape=jax.ShapeDtypeStruct((16, 128), jnp.float32),
        compiler_params=pltpu.CompilerParams(vmem_limit_bytes=6 * 2**20),
        name="gram",
    )(
        jnp.stack([group_rank, tensor_rank]).astype(jnp.int32),
        jac,
        own_start,
        pairs,
        rewards,
    )
    packed = jnp.sum(gather_by_exchange(packed, "dp"), 0)
    packed = gather_by_exchange(packed, "tensor")
    own_result, part = pl.pallas_call(
        lanczos_body,
        in_specs=whole(3),
        out_specs=whole(2),
        out_shape=[
            jax.ShapeDtypeStruct((8, RESULT_LANES), jnp.bfloat16),
            jax.ShapeDtypeStruct((1, 128), jnp.float32),
        ],
        compiler_params=pltpu.CompilerParams(vmem_limit_bytes=6 * 2**20),
        name="lanczos",
    )(packed, pairs, jac)
    every = lax.all_to_all(
        jnp.broadcast_to(own_result[None], (groups * shards,) + own_result.shape),
        ("dp", "tensor"),
        0,
        0,
    )
    next_a, next_bq, next_bkv, next_ao, next_bo = assemble(
        part,
        every,
        jnp.transpose(initial_down_qkv, (0, 2, 1)),
        initial_up_query,
        initial_up_key_value,
        initial_down_output.T,
        initial_up_output,
    )
    return jnp.transpose(next_a, (0, 2, 1)), next_bq, next_bkv, next_ao.T, next_bo


def solution(mesh):
    in_specs = (
        P("dp", "tensor", None),
        P(None, "tensor"),
        P(None, None, "tensor"),
        P("tensor", None),
        P(),
        P("dp"),
        P(),
        P(),
        P(None, "tensor"),
        P(None, None, "tensor"),
        P("tensor", None),
        P(),
        P(),
        P(),
        P(),
        P(),
        P(),
    )
    out_specs = (P(), P(), P(), P(), P())
    return jax.shard_map(local, mesh=mesh, in_specs=in_specs, out_specs=out_specs, check_vma=False)
```

```python
import math

import jax
import jax.numpy as jnp
from jax import lax
from jax.experimental import pallas as pl
from jax.experimental.pallas import tpu as pltpu
from jax.sharding import PartitionSpec as P

HEAD_SIZE = 128
NPARAM = 688128
ADAPTER_SCALE = 2.0
NORM_EPS = 1e-05
LANCZOS_EPS = 1e-06
SCORE_CAP = 30.0
PRECISE = lax.Precision.HIGHEST
OBJ = 5
PIECES = 11
PIECE_ROWS = 56
LANES = 512


def dot_halved(left_side, right_side, left_dim, right_dim):
    return lax.dot_general(
        left_side,
        right_side,
        (((left_dim,), (right_dim,)), ((), ())),
        preferred_element_type=jnp.float32,
    )


def dot_entire(left_side, right_side, left_dim, right_dim):
    return lax.dot_general(
        left_side,
        right_side,
        (((left_dim,), (right_dim,)), ((), ())),
        precision=PRECISE,
        preferred_element_type=jnp.float32,
    )


def gather_by_exchange(block, axis):
    count = lax.axis_size(axis)
    copies = jnp.broadcast_to(block[None], (count,) + block.shape)
    return lax.all_to_all(copies, axis, 0, 0)


PAIR_ROWS = 40
PACK_ROWS = 48
PACK_LANES = 42
RESULT_LANES = 768


def rounded_parts(entire, count):
    parts = []
    for _ in range(count):
        part = entire.astype(jnp.bfloat16)
        parts.append(part)
        entire = entire - part.astype(jnp.float32)
    return parts


def lane_sum(values):
    return jnp.sum(values, axis=1, keepdims=True)


def row_sum(values):
    return jnp.sum(values, axis=0, keepdims=True)


def gram_body(rank_ref, jac_ref, start_ref, pairs_ref, rewards_ref, packed_ref):
    jac = jac_ref[...]
    start = start_ref[...]
    pairs = pairs_ref[...]
    rows = jac.shape[0]
    gram = dot_halved(jac, jac, 1, 1)
    starts = jnp.concatenate(rounded_parts(start, 3), 0)
    along = lane_sum(dot_halved(jac, starts, 1, 1))
    own_pairs = pairs[:, :rows]
    gram = dot_entire(dot_entire(own_pairs, gram, 1, 0), own_pairs, 1, 1)
    along = dot_entire(own_pairs, jnp.broadcast_to(along, (rows, 128)), 1, 0)
    rewards = pltpu.roll(rewards_ref[...], OBJ * rank_ref[0], axis=1)[:1]
    rewards = jnp.where(rank_ref[1] == 0, rewards, 0.0)
    apart = lane_sum(pairs * rewards)
    square = jnp.sum(start * start)
    lane = lax.broadcasted_iota(jnp.int32, (PACK_ROWS, 128), 1)
    row = lax.broadcasted_iota(jnp.int32, (PACK_ROWS, 128), 0)
    wide = jnp.concatenate([gram, jnp.zeros((PACK_ROWS, 128 - PACK_ROWS), jnp.float32)], 1)
    wide = jnp.where(lane < PAIR_ROWS, wide, 0.0)
    wide = jnp.where(lane == PAIR_ROWS, along, wide)
    wide = jnp.where(lane == PAIR_ROWS + 1, apart, wide)
    wide = jnp.where((row == PAIR_ROWS) & (lane == 0), square, wide)
    packed_ref[...] = (
        wide[:16]
        + pltpu.roll(wide[16:32], PACK_LANES, axis=1)
        + pltpu.roll(wide[32:], 2 * PACK_LANES, axis=1)
    )


def lanczos_body(packed_ref, pairs_ref, jac_ref, result_ref, part_ref):
    packed = jnp.sum(packed_ref[...], axis=0)
    wide = jnp.concatenate(
        [
            packed,
            pltpu.roll(packed, 128 - PACK_LANES, axis=1),
            pltpu.roll(packed, 128 - 2 * PACK_LANES, axis=1),
        ],
        0,
    )
    lane = lax.broadcasted_iota(jnp.int32, (PACK_ROWS, 128), 1)
    row = lax.broadcasted_iota(jnp.int32, (PACK_ROWS, 128), 0)
    inside = row < PAIR_ROWS
    gram = jnp.where(inside & (lane < PAIR_ROWS), wide, 0.0)
    along = lane_sum(jnp.where(inside & (lane == PAIR_ROWS), wide, 0.0))
    apart = lane_sum(jnp.where(inside & (lane == PAIR_ROWS + 1), wide, 0.0))
    picked = jnp.where((row == PAIR_ROWS) & (lane == 0), wide, 0.0)
    start_square = lane_sum(row_sum(picked)) / NPARAM
    diagonal = row == lane

    def gram_times(column):
        across = row_sum(jnp.where(diagonal, column, 0.0))
        return lane_sum(gram * across)

    def inner(left_side, right_side):
        return row_sum(left_side * right_side) / NPARAM

    decayed = jnp.exp(-jnp.abs(apart))
    curvature = decayed / ((1.0 + decayed) * (1.0 + decayed)) / (16 // 2)
    start_scale = lax.rsqrt(start_square + LANCZOS_EPS)
    first_square = start_square * start_scale * start_scale
    along_one = along * start_scale
    pull_one = curvature * along_one
    alpha_one = inner(pull_one, along_one)
    gram_pull = gram_times(pull_one)
    beta_one = jnp.sqrt(
        inner(pull_one, gram_pull) - alpha_one * alpha_one * (2.0 - first_square) + LANCZOS_EPS
    )
    along_two = (gram_pull - alpha_one * along_one) / beta_one
    pull_two = curvature * along_two
    first_second = alpha_one * (1.0 - first_square) / beta_one
    alpha_two = inner(pull_two, along_two) - beta_one * first_second
    mixed = pull_two - (alpha_two / beta_one) * pull_one
    first_part = alpha_two * alpha_one / beta_one - beta_one
    beta_two = jnp.sqrt(
        inner(mixed, gram_times(mixed))
        + 2.0 * first_part * inner(mixed, along_one)
        + first_part * first_part * first_square
        + LANCZOS_EPS
    )
    part_ref[...] = jnp.broadcast_to(first_part * start_scale / beta_two, part_ref.shape)
    across = row_sum(pairs_ref[...] * (mixed / beta_two))
    jac = jac_ref[...]
    rows = jac.shape[0]
    parts = rounded_parts(jnp.broadcast_to(across[:, :rows], (8, rows)), 3)
    result = sum(dot_halved(part, jac, 1, 0) for part in parts)[:1]
    spare = jnp.zeros((6, 128), jnp.float32)

    def chunks(start, count, size):
        return [result[:, start + size * step : start + size * (step + 1)] for step in range(count)]

    main = jnp.concatenate(chunks(0, 8, LANES), 0)
    middle = jnp.concatenate(chunks(8 * LANES, 8, 128), 0)
    last = jnp.concatenate(chunks(10 * LANES, 2, 128) + [spare], 0)
    result_ref[...] = jnp.concatenate([main, middle, last], 1).astype(jnp.bfloat16)


def assemble_body(
    part_ref,
    every_ref,
    a_ref,
    bq_ref,
    bkv_ref,
    ao_ref,
    bo_ref,
    out_a_ref,
    out_bq_ref,
    out_bkv_ref,
    out_ao_ref,
    out_bo_ref,
):
    step = pl.program_id(0)
    part = part_ref[0, 0]

    def one_hot(size, first, second):
        row = lax.broadcasted_iota(jnp.int32, (size, size), 0)
        lane = lax.broadcasted_iota(jnp.int32, (size, size), 1)
        wanted = (row % second) * first + row // second
        return jnp.where(lane == wanted, 1.0, 0.0).astype(jnp.bfloat16)

    row = lax.broadcasted_iota(jnp.int32, (64, 64), 0)
    lane = lax.broadcasted_iota(jnp.int32, (64, 64), 1)
    wanted = (row % 8) * 8 + ((row % 16) // 8) * 4 + row // 16
    moved = jnp.where(lane == wanted, 1.0, 0.0).astype(jnp.bfloat16)
    for half in range(2):
        group = 2 * step + half
        block = every_ref[pl.ds(8 * group, 8), :, :LANES].reshape(64, LANES)
        placed = dot_halved(moved, block, 1, 0).reshape(4, 16, LANES)
        lanes = slice(half * LANES, (half + 1) * LANES)
        out_a_ref[:, :, lanes] = placed[:3] + part * a_ref[:, :, lanes]
        out_bo_ref[:, lanes] = placed[3] + part * bo_ref[:, lanes]
    block = jnp.concatenate(
        [every_ref[8 * group + step, :, LANES:] for group in range(16)], 0
    )
    placed = dot_halved(one_hot(128, 8, 16), block, 1, 0)
    for chunk in range(4):
        lanes = slice(chunk * 128, (chunk + 1) * 128)
        out_bq_ref[:, lanes] = placed[16 * chunk : 16 * chunk + 16, :128] + part * bq_ref[:, lanes]
        out_ao_ref[:, lanes] = (
            placed[64 + 16 * chunk : 80 + 16 * chunk, :128] + part * ao_ref[:, lanes]
        )
    out_bkv_ref[0] = placed[:16, 128:] + part * bkv_ref[0]
    out_bkv_ref[1] = placed[16:32, 128:] + part * bkv_ref[1]


def whole(count):
    return [pl.BlockSpec(memory_space=pltpu.VMEM)] * count


def product(left, right, right_dim):
    left_both = jnp.concatenate(rounded_parts(left, 2), 1)
    upper, lower = rounded_parts(right, 2)
    if right_dim == 0:
        rows = jnp.concatenate([upper, lower], 1)
        both = dot_halved(left_both, jnp.concatenate([rows, rows], 0), 1, 0)
    else:
        rows = jnp.concatenate([upper, lower], 0)
        both = dot_halved(left_both, jnp.concatenate([rows, rows], 1), 1, 1)
    size = right.shape[1 - right_dim]
    return both[:, :size] + both[:, size:]


def tall(parts):
    return jnp.concatenate(parts, 0)


def flat(parts):
    return jnp.concatenate(parts, 1)


def corners(both, rows, lanes):
    upper = both[:rows] + both[rows:]
    return upper[:, :lanes] + upper[:, lanes:]


def stack(rows):
    return tall([rows[:, at : at + 128] for at in range(0, rows.shape[1], 128)])


def unstack(rows):
    return flat([rows[at : at + 128] for at in range(0, rows.shape[0], 128)])


def place_shards(spots_ref, whole_ref, shards, first_half):
    for at in range(6):
        rows = pl.ds(pl.multiple_of(spots_ref[at] * 16, 16), 16)
        whole_ref[rows, :] = shards[at][...]
    for at in range(2):
        rows = pl.ds(pl.multiple_of(spots_ref[6 + at] * 16, 16), 16)
        whole_ref[rows, :] = jnp.where(
            first_half, shards[6 + 2 * at][...], shards[7 + 2 * at][...]
        )


def shard_specs(last_step):
    half = last_step // 2
    full = pl.BlockSpec((16, CHUNK), lambda step: (0, jnp.minimum(step, last_step)))
    early = pl.BlockSpec((16, CHUNK), lambda step: (0, jnp.minimum(step, half)))
    late = pl.BlockSpec(
        (16, CHUNK), lambda step: (0, jnp.clip(step - half - 1, 0, last_step - half - 1))
    )
    return [full] * 6 + [early, late] * 2


def gather_by_relays(block):
    half = block.shape[1] // 2

    def permute(array, y_step, z_step):
        pairs = [
            (at, ((at // 4 + y_step) % 2) * 4 + (at % 4 + z_step) % 4) for at in range(8)
        ]
        return lax.ppermute(array, "tensor", pairs)

    across = permute(block, 1, 0)
    below = permute(block, 0, 1)
    above = permute(block, 0, 3)
    across_below = permute(across, 0, 1)
    across_above = permute(across, 0, 3)
    far = [permute(below[:, :half], 0, 1), permute(above[:, half:], 0, 3)]
    across_far = [
        permute(across_below[:, :half], 0, 1),
        permute(across_above[:, half:], 0, 3),
    ]
    return [block, across, below, above, across_below, across_above] + far + across_far


def shard_spots():
    rank = lax.axis_index("tensor").astype(jnp.int32)
    y, z = rank // 4 * 4, rank % 4
    other = 4 - y
    return jnp.stack(
        [
            y + z,
            other + z,
            y + (z + 3) % 4,
            y + (z + 1) % 4,
            other + (z + 3) % 4,
            other + (z + 1) % 4,
            y + (z + 2) % 4,
            other + (z + 2) % 4,
        ]
    )


CHUNK = 2048


def forward_body(
    spots_ref,
    shard_0,
    shard_1,
    shard_2,
    shard_3,
    shard_4,
    shard_5,
    shard_6,
    shard_7,
    shard_8,
    shard_9,
    query_weight_ref,
    kv_weight_ref,
    down_ref,
    output_weight_ref,
    up_output_ref,
    down_output_ref,
    up_query_ref,
    up_kv_ref,
    tokens_ref,
    out_ref,
    query_ref,
    keys_ref,
    values_ref,
    prob_ref,
    capped_ref,
    context_ref,
    low_ref,
    context_low_ref,
    query_sum,
    kv_sum,
    low_sum,
    halved_ref,
    halved_low_ref,
):
    step = pl.program_id(0)
    steps = pl.num_programs(0) // 2
    shards = [
        shard_0,
        shard_1,
        shard_2,
        shard_3,
        shard_4,
        shard_5,
        shard_6,
        shard_7,
        shard_8,
        shard_9,
    ]

    @pl.when(step < steps)
    def _():
        place_shards(spots_ref, tokens_ref, shards, step < steps // 2)
        tokens = tokens_ref[...]
        query = dot_halved(tokens, query_weight_ref[...], 1, 0)
        kv = dot_halved(tokens, flat([kv_weight_ref[0], kv_weight_ref[1]]), 1, 0)
        low = dot_halved(down_ref[...], tokens, 1, 1)

        @pl.when(step == 0)
        def _():
            query_sum[...] = query
            kv_sum[...] = kv
            low_sum[...] = jnp.zeros(low_sum.shape, jnp.float32)
            low_sum[:48] = low

        @pl.when(step > 0)
        def _():
            query_sum[...] += query
            kv_sum[...] += kv
            low_sum[:48] += low

    @pl.when(step == steps - 1)
    def _():
        low_turned = low_sum[...]
        low = low_turned.T
        low_ref[...] = low_turned[:48]
        root = 1.0 / math.sqrt(HEAD_SIZE)

        def adapted(total, piece, up):
            parts = rounded_parts(low[:, 16 * piece : 16 * piece + 16], 2)
            return total + ADAPTER_SCALE * dot_halved(flat(parts), tall([up, up]), 1, 0)

        query = adapted(query_sum[...], 0, up_query_ref[...])
        keys = adapted(kv_sum[:, :128], 1, up_kv_ref[0])
        values = adapted(kv_sum[:, 128:], 2, up_kv_ref[1])
        capped = jnp.tanh(product(stack(query), keys, 1) * (root / SCORE_CAP))
        row = lax.broadcasted_iota(jnp.int32, (512, 128), 0) % 128
        lane = lax.broadcasted_iota(jnp.int32, (512, 128), 1)
        weights = jnp.where(row >= lane, jnp.exp(SCORE_CAP * capped), 0.0)
        probs = weights / lane_sum(weights)
        context = unstack(product(probs, values, 0))
        low_pair = dot_halved(down_output_ref[...], tall(rounded_parts(context, 2)), 1, 1)
        context_low = ADAPTER_SCALE * (low_pair[:, :128] + low_pair[:, 128:])
        query_ref[...] = query
        keys_ref[...] = keys
        values_ref[...] = values
        prob_ref[...] = probs
        capped_ref[...] = capped
        context_ref[...] = context
        context_low_ref[...] = context_low
        halved_ref[...] = context.astype(jnp.bfloat16)
        turned = tall([context_low, jnp.zeros((112, 128), jnp.float32)]).T[:, :16]
        halved_low_ref[...] = flat(rounded_parts(turned, 2))

    @pl.when(step >= steps)
    def _():
        up = up_output_ref[...]
        terms = dot_halved(halved_ref[...], output_weight_ref[...], 1, 0) + dot_halved(
            halved_low_ref[...], tall([up, up]), 1, 0
        )
        out_ref[...] = terms.astype(jnp.bfloat16).reshape(out_ref.shape)


def fixed(array):
    zeros = (0,) * array.ndim
    return pl.BlockSpec(array.shape, lambda step: zeros)


def forward(
    spots,
    shards,
    query_weight,
    key_value_weight,
    down_rows,
    output_weight,
    up_output,
    down_output,
    up_query,
    up_key_value,
):
    width = shards[0].shape[1]
    steps = width // CHUNK
    last = steps - 1
    query_cols = query_weight.shape[1]

    def first_part(step):
        return jnp.minimum(step, last)

    def second_part(step):
        return jnp.maximum(step - steps, 0)

    shapes = [
        jax.ShapeDtypeStruct((128, width), jnp.bfloat16),
        jax.ShapeDtypeStruct((8, 16, width), jnp.bfloat16),
        jax.ShapeDtypeStruct((128, query_cols), jnp.float32),
        jax.ShapeDtypeStruct((128, 128), jnp.float32),
        jax.ShapeDtypeStruct((128, 128), jnp.float32),
        jax.ShapeDtypeStruct((512, 128), jnp.float32),
        jax.ShapeDtypeStruct((512, 128), jnp.float32),
        jax.ShapeDtypeStruct((128, query_cols), jnp.float32),
        jax.ShapeDtypeStruct((48, 128), jnp.float32),
        jax.ShapeDtypeStruct((16, 128), jnp.float32),
    ]
    return pl.pallas_call(
        forward_body,
        grid=(2 * steps,),
        in_specs=[pl.BlockSpec(memory_space=pltpu.SMEM)]
        + shard_specs(last)
        + [
            pl.BlockSpec((CHUNK, query_cols), lambda step: (first_part(step), 0)),
            pl.BlockSpec((2, CHUNK, 128), lambda step: (0, first_part(step), 0)),
            pl.BlockSpec((48, CHUNK), lambda step: (0, first_part(step))),
            pl.BlockSpec((query_cols, CHUNK), lambda step: (0, second_part(step))),
            pl.BlockSpec((16, CHUNK), lambda step: (0, second_part(step))),
            fixed(down_output),
            fixed(up_query),
            fixed(up_key_value),
        ],
        out_specs=[
            pl.BlockSpec((128, CHUNK), lambda step: (0, first_part(step))),
            pl.BlockSpec((8, 16, CHUNK), lambda step: (0, 0, second_part(step))),
        ]
        + [fixed(shape) for shape in shapes[2:]],
        out_shape=shapes,
        scratch_shapes=[
            pltpu.VMEM((128, query_cols), jnp.float32),
            pltpu.VMEM((128, 256), jnp.float32),
            pltpu.VMEM((128, 128), jnp.float32),
            pltpu.VMEM((128, query_cols), jnp.bfloat16),
            pltpu.VMEM((128, 32), jnp.bfloat16),
        ],
        compiler_params=pltpu.CompilerParams(vmem_limit_bytes=60 * 2**20),
        name="forward",
    )(
        spots,
        *shards,
        query_weight,
        key_value_weight,
        down_rows,
        output_weight,
        up_output,
        down_output,
        up_query,
        up_key_value,
    )


def cotangents_body(
    lens_ref,
    spots_ref,
    shard_0,
    shard_1,
    shard_2,
    shard_3,
    shard_4,
    shard_5,
    shard_6,
    shard_7,
    shard_8,
    shard_9,
    weight_ref,
    side_ref,
    query_ref,
    keys_ref,
    values_ref,
    prob_ref,
    capped_ref,
    context_ref,
    low_ref,
    context_low_ref,
    down_ref,
    up_query_ref,
    up_kv_ref,
    resid_ref,
    factors_ref,
    narrow_ref,
    rewards_ref,
    repeated_ref,
    through_ref,
    slow_ref,
    square_ref,
):
    step = pl.program_id(0)
    shards = [
        shard_0,
        shard_1,
        shard_2,
        shard_3,
        shard_4,
        shard_5,
        shard_6,
        shard_7,
        shard_8,
        shard_9,
    ]
    place_shards(spots_ref, resid_ref, shards, step < pl.num_programs(0) // 2)
    chunk = resid_ref[...]
    side = side_ref[...]
    left = tall([chunk, side[16:]])
    through = dot_halved(left, weight_ref[...], 1, 1)
    slow = dot_halved(left, side, 1, 1)
    wide = chunk.astype(jnp.float32)
    square = jnp.zeros((128, 128), jnp.float32)
    for at in range(0, chunk.shape[1], 128):
        square = square + wide[:, at : at + 128] * wide[:, at : at + 128]

    @pl.when(step == 0)
    def _():
        slow_ref[...] = jnp.zeros(slow_ref.shape, jnp.float32)
        through_ref[...] = through
        slow_ref[:144, :32] = slow
        square_ref[...] = square

    @pl.when(step > 0)
    def _():
        through_ref[...] += through
        slow_ref[:144, :32] += slow
        square_ref[...] += square

    @pl.when(step == pl.num_programs(0) - 1)
    def _():
        width = chunk.shape[1] * pl.num_programs(0)
        length_own = lens_ref[0]
        root = 1.0 / math.sqrt(HEAD_SIZE)
        slow = slow_ref[...]
        slow_turned = slow.T
        square = square_ref[...]
        inverse = lax.rsqrt(lane_sum(square) / width + NORM_EPS)
        inverse_turned = lax.rsqrt(row_sum(square.T) / width + NORM_EPS)
        each = 1.0 / jnp.broadcast_to(length_own, (1, 1)).astype(jnp.float32)
        share = jnp.where(
            lax.broadcasted_iota(jnp.int32, (128, 1), 0) < length_own, each, 0.0
        )
        share_turned = jnp.where(
            lax.broadcasted_iota(jnp.int32, (1, 128), 1) < length_own, each, 0.0
        )
        logits = inverse * slow[:128, 16:32]
        lead = share * inverse
        pulled = lead * inverse * logits / width
        lead_turned = share_turned * inverse_turned
        pulled_turned = (
            lead_turned * inverse_turned * inverse_turned * slow_turned[16:32, :128] / width
        )
        low_turned = slow_turned[:16, :128]
        rewards_ref[...] = jnp.zeros(rewards_ref.shape, jnp.float32)
        rewards_ref[:1, :16] = row_sum(share * logits)
        down = down_ref[...]
        through = through_ref[...] + ADAPTER_SCALE * dot_halved(
            flat(rounded_parts(slow[:144, :16], 2)), tall([down, down]), 1, 0
        )
        narrow_ref[...] = jnp.zeros(narrow_ref.shape, jnp.float32)
        context = context_ref[...]
        context_rows = stack(context)
        probs = prob_ref[...]
        capped = capped_ref[...]
        slope = probs * (1.0 - capped * capped) * root
        probs_turned = tall(rounded_parts(probs.T, 2))
        query_turned = tall(rounded_parts(stack(query_ref[...]).T, 2))
        keys = keys_ref[...]
        values = values_ref[...]
        low = [tall(rounded_parts(low_ref[16 * at : 16 * at + 16], 2)) for at in range(3)]
        up_query = up_query_ref[...]
        context_low = context_low_ref[...]
        cot_low = []
        for obj in range(OBJ):
            lead_row = through[128 + obj : 129 + obj]
            cot = stack(lead * lead_row - pulled[:, obj : obj + 1] * through[:128])
            cot_prob = product(cot, values, 1)
            cot_score = slope * (cot_prob - lane_sum(cot * context_rows))
            cot_query = unstack(product(cot_score, keys, 0))
            cot_keys = corners(
                dot_halved(query_turned, flat(rounded_parts(cot_score, 2)), 1, 0), 128, 128
            )
            cot_values = corners(
                dot_halved(probs_turned, flat(rounded_parts(cot, 2)), 1, 0), 128, 128
            )
            query_parts = rounded_parts(cot_query, 2)
            keys_parts = rounded_parts(cot_keys, 2)
            values_parts = rounded_parts(cot_values, 2)
            factor_query = dot_halved(up_query, tall(query_parts), 1, 1)
            factor_keys = dot_halved(up_kv_ref[0], flat(keys_parts), 1, 0)
            factor_values = dot_halved(up_kv_ref[1], tall(values_parts), 1, 1)
            rows = [
                ADAPTER_SCALE * (factor[:, :128] + factor[:, 128:])
                for factor in (factor_query, factor_keys, factor_values)
            ] + [context_low]
            for piece in range(4):
                for half in range(2):
                    factors_ref[pl.ds(20 * half + 5 * piece + obj, 8, stride=40), :] = rows[
                        piece
                    ][8 * half : 8 * half + 8]
            jac_query = corners(dot_halved(low[0], flat(query_parts), 1, 0), 16, 512)
            jac_keys = corners(dot_halved(low[1], tall(keys_parts), 1, 1), 16, 128)
            jac_values = corners(dot_halved(low[2], flat(values_parts), 1, 0), 16, 128)
            blocks = [jac_query[:, at : at + 128] for at in range(0, 512, 128)]
            spots = [(obj, 0), (obj, 1), (obj, 2), (obj, 3), (10 + obj, 0), (10 + obj, 1)]
            for (row, tile), block in zip(spots, blocks + [jac_keys, jac_values]):
                for half in range(2):
                    narrow_ref[tile, pl.ds(128 * half + row, 8, stride=16), :] = (
                        ADAPTER_SCALE * block[8 * half : 8 * half + 8]
                    )
            cot_low.append(
                slow_turned[:16, 128 + obj : 129 + obj] * lead_turned
                - pulled_turned[obj : obj + 1] * low_turned
            )
        jac_down = ADAPTER_SCALE * product(tall(cot_low), context, 0)
        for obj in range(OBJ):
            for half in range(2):
                start = 16 * obj + 8 * half
                for tile in range(4):
                    narrow_ref[tile, pl.ds(128 * half + 5 + obj, 8, stride=16), :] = jac_down[
                        start : start + 8, 128 * tile : 128 * tile + 128
                    ]
        blank = jnp.zeros((15, 128), jnp.float32)
        repeated_ref[0] = jnp.concatenate([blank, pulled_turned[:5]] * 2, 0)
        repeated_ref[1] = jnp.broadcast_to(lead_turned, (40, 128))


def cotangents(lens, spots, shards, output_weight, side, *others):
    width = shards[0].shape[1]
    query_cols = output_weight.shape[0]
    steps = width // CHUNK

    def chunked(rows):
        return pl.BlockSpec((rows, CHUNK), lambda step: (0, step))

    shapes = [
        jax.ShapeDtypeStruct((128, width), jnp.bfloat16),
        jax.ShapeDtypeStruct((320, 128), jnp.float32),
        jax.ShapeDtypeStruct((4, 256, 128), jnp.float32),
        jax.ShapeDtypeStruct((8, 128), jnp.float32),
        jax.ShapeDtypeStruct((2, 40, 128), jnp.float32),
    ]
    return pl.pallas_call(
        cotangents_body,
        grid=(steps,),
        in_specs=[pl.BlockSpec(memory_space=pltpu.SMEM)] * 2
        + shard_specs(steps - 1)
        + [chunked(query_cols), chunked(32)]
        + [fixed(array) for array in others],
        out_specs=[chunked(128)] + [fixed(shape) for shape in shapes[1:]],
        out_shape=shapes,
        scratch_shapes=[
            pltpu.VMEM((144, query_cols), jnp.float32),
            pltpu.VMEM((256, 128), jnp.float32),
            pltpu.VMEM((128, 128), jnp.float32),
        ],
        compiler_params=pltpu.CompilerParams(vmem_limit_bytes=60 * 2**20),
        name="cotangents",
    )(lens, spots, *shards, output_weight, side, *others)


def jacobian_body(
    factors_ref, tokens_ref, resid_ref, side_ref, repeated_ref, narrow_ref, payload_ref
):
    factors = jnp.sum(factors_ref[...], axis=0)
    row = lax.broadcasted_iota(jnp.int32, (40, 1), 0) % 20
    last = row >= 15
    left = flat([jnp.where(last, 0.0, factors), jnp.where(last, -factors * repeated_ref[0], 0.0)])
    lane = lax.broadcasted_iota(jnp.int32, (40, 16), 1)
    lead = jnp.where(lane == row - 15, lane_sum(factors * repeated_ref[1]), 0.0)

    def both(rows):
        upper = rows.astype(jnp.bfloat16).astype(jnp.float32)
        return tall([upper, rows - upper]).astype(jnp.bfloat16)

    left = both(left)
    lead = both(lead)

    def place(group, _):
        lanes = pl.ds(pl.multiple_of(group * LANES, LANES), LANES)
        right = tall([tokens_ref[:, lanes], resid_ref[:, lanes]])
        pair = dot_halved(left, right, 1, 0) + dot_halved(lead, side_ref[16:, lanes], 1, 0)
        below = flat(
            [narrow_ref[tile, pl.ds(pl.multiple_of(group * 16, 16), 16), :] for tile in range(4)]
        )
        payload_ref[group] = tall([pair[:40] + pair[40:], below]).astype(jnp.bfloat16)
        return 0

    lax.fori_loop(0, 16, place, 0, unroll=4)


def jacobian(*arrays):
    return pl.pallas_call(
        jacobian_body,
        in_specs=whole(len(arrays)),
        out_specs=pl.BlockSpec(memory_space=pltpu.VMEM),
        out_shape=jax.ShapeDtypeStruct((16, PIECE_ROWS, LANES), jnp.bfloat16),
        compiler_params=pltpu.CompilerParams(vmem_limit_bytes=60 * 2**20),
        name="jacobian",
    )(*arrays)


def assemble(part, every, start_a, start_bq, start_bkv, start_ao, start_bo):
    steps = 8
    shapes = [start_a, start_bq, start_bkv, start_ao, start_bo]
    blocks = [
        pl.BlockSpec((3, 16, 2 * LANES), lambda step: (0, 0, step)),
        pl.BlockSpec((16, LANES), lambda step: (0, step)),
        pl.BlockSpec((2, 16, HEAD_SIZE), lambda step: (0, 0, step)),
        pl.BlockSpec((16, LANES), lambda step: (0, step)),
        pl.BlockSpec((16, 2 * LANES), lambda step: (0, step)),
    ]
    return pl.pallas_call(
        assemble_body,
        grid=(steps,),
        in_specs=[
            pl.BlockSpec(memory_space=pltpu.SMEM),
            pl.BlockSpec(every.shape, lambda step: (0, 0, 0)),
        ]
        + blocks,
        out_specs=blocks,
        out_shape=[jax.ShapeDtypeStruct(shape.shape, jnp.float32) for shape in shapes],
        compiler_params=pltpu.CompilerParams(vmem_limit_bytes=14 * 2**20),
        name="assemble",
    )(part, every, start_a, start_bq, start_bkv, start_ao, start_bo)


def local(
    hidden,
    query_weight,
    key_value_weight,
    output_weight,
    head,
    lens,
    partner,
    adapter_down_qkv,
    adapter_up_query,
    adapter_up_key_value,
    adapter_down_output,
    adapter_up_output,
    initial_down_qkv,
    initial_up_query,
    initial_up_key_value,
    initial_down_output,
    initial_up_output,
):
    _, part_length, width = hidden.shape
    shards = lax.axis_size("tensor")
    groups = lax.axis_size("dp")
    tensor_rank = lax.axis_index("tensor")
    group_rank = lax.axis_index("dp")
    query_cols = query_weight.shape[1]
    length = part_length * shards

    down_rows = jnp.transpose(adapter_down_qkv, (0, 2, 1)).reshape(48, width)
    down_output = adapter_down_output.T
    head_rows = head.T
    spots = shard_spots()
    side = jnp.concatenate([adapter_up_output, head_rows, jnp.zeros((11, width), head.dtype)], 0)
    (
        tokens,
        out_terms,
        query,
        keys,
        values,
        probabilities,
        capped,
        context,
        low,
        context_low,
    ) = forward(
        spots,
        gather_by_relays(hidden[0]),
        query_weight,
        key_value_weight,
        down_rows,
        output_weight,
        adapter_up_output,
        down_output,
        adapter_up_query,
        adapter_up_key_value,
    )
    out_pieces = lax.all_to_all(out_terms, "tensor", 0, 0)
    resid_own = hidden[0].astype(jnp.float32) + jnp.sum(out_pieces.astype(jnp.float32), 0)
    resid, factors, narrow, rewards, repeated = cotangents(
        lens,
        spots,
        gather_by_relays(resid_own.astype(jnp.bfloat16)),
        output_weight,
        side,
        query,
        keys,
        values,
        probabilities,
        capped,
        context,
        low,
        context_low,
        down_output,
        adapter_up_query,
        adapter_up_key_value,
    )
    factors = lax.all_to_all(factors.reshape(shards, 8 * OBJ, length), "tensor", 0, 0)
    payload = jacobian(factors, tokens, resid, side, repeated, narrow)
    spread = lax.all_to_all(payload, "dp", 0, 0)
    jac = (
        spread[:, : PIECES * OBJ]
        .reshape(groups, PIECES, OBJ, LANES)
        .transpose(0, 2, 1, 3)
        .reshape(groups * OBJ, PIECES * LANES)
    )

    own_a = lax.dynamic_slice(
        jnp.transpose(initial_down_qkv, (0, 2, 1)).reshape(3, 2, shards, width),
        (0, 0, tensor_rank, group_rank * LANES),
        (3, 2, 1, LANES),
    ).reshape(3, 2, LANES)
    own_bo = lax.dynamic_slice(
        initial_up_output.reshape(2, shards, width),
        (0, tensor_rank, group_rank * LANES),
        (2, 1, LANES),
    ).reshape(2, LANES)
    own_bq = lax.dynamic_slice(
        initial_up_query, (group_rank, tensor_rank * query_cols), (1, query_cols)
    )
    own_ao = lax.dynamic_slice(
        initial_down_output.T, (group_rank, tensor_rank * query_cols), (1, query_cols)
    )
    own_bkv = lax.dynamic_slice(
        initial_up_key_value, (0, group_rank, tensor_rank * HEAD_SIZE), (2, 1, HEAD_SIZE)
    )
    own_start = jnp.concatenate(
        [
            jnp.concatenate([own_a.transpose(1, 0, 2), own_bo[:, None]], 1).reshape(8, LANES),
            own_bq,
            own_ao,
            jnp.concatenate(
                [own_bkv.reshape(1, 2 * HEAD_SIZE), jnp.zeros((1, LANES - 2 * HEAD_SIZE))], 1
            ),
        ],
        0,
    ).reshape(1, PIECES * LANES)
    own_start = own_start.astype(jnp.float32)
    sequences = jnp.arange(groups)
    leads = sequences < partner
    order = jnp.sum((sequences[None, :] < sequences[:, None]) & leads[None, :], 1)
    chosen = (
        leads[None, :] & (order[None, :] == jnp.arange(groups // 2)[:, None])
    ).astype(jnp.float32)
    differences = chosen - jnp.take(chosen, partner, axis=1)
    pairs = (
        differences[:, None, :, None] * jnp.eye(OBJ, dtype=jnp.float32)[None, :, None, :]
    ).reshape(PAIR_ROWS, groups * OBJ)
    pairs = jnp.pad(pairs, ((0, PACK_ROWS - PAIR_ROWS), (0, 128 - groups * OBJ)))
    packed = pl.pallas_call(
        gram_body,
        in_specs=[pl.BlockSpec(memory_space=pltpu.SMEM)] + whole(4),
        out_specs=pl.BlockSpec(memory_space=pltpu.VMEM),
        out_shape=jax.ShapeDtypeStruct((16, 128), jnp.float32),
        compiler_params=pltpu.CompilerParams(vmem_limit_bytes=6 * 2**20),
        name="gram",
    )(
        jnp.stack([group_rank, tensor_rank]).astype(jnp.int32),
        jac,
        own_start,
        pairs,
        rewards,
    )
    packed = jnp.sum(gather_by_exchange(packed, "dp"), 0)
    packed = gather_by_exchange(packed, "tensor")
    own_result, part = pl.pallas_call(
        lanczos_body,
        in_specs=whole(3),
        out_specs=whole(2),
        out_shape=[
            jax.ShapeDtypeStruct((8, RESULT_LANES), jnp.bfloat16),
            jax.ShapeDtypeStruct((1, 128), jnp.float32),
        ],
        compiler_params=pltpu.CompilerParams(vmem_limit_bytes=6 * 2**20),
        name="lanczos",
    )(packed, pairs, jac)
    every = lax.all_to_all(
        jnp.broadcast_to(own_result[None], (groups * shards,) + own_result.shape),
        ("dp", "tensor"),
        0,
        0,
    )
    next_a, next_bq, next_bkv, next_ao, next_bo = assemble(
        part,
        every,
        jnp.transpose(initial_down_qkv, (0, 2, 1)),
        initial_up_query,
        initial_up_key_value,
        initial_down_output.T,
        initial_up_output,
    )
    return jnp.transpose(next_a, (0, 2, 1)), next_bq, next_bkv, next_ao.T, next_bo


def solution(mesh):
    in_specs = (
        P("dp", "tensor", None),
        P(None, "tensor"),
        P(None, None, "tensor"),
        P("tensor", None),
        P(),
        P("dp"),
        P(),
        P(),
        P(None, "tensor"),
        P(None, None, "tensor"),
        P("tensor", None),
        P(),
        P(),
        P(),
        P(),
        P(),
        P(),
    )
    out_specs = (P(), P(), P(), P(), P())
    return jax.shard_map(local, mesh=mesh, in_specs=in_specs, out_specs=out_specs, check_vma=False)
```

```python
import math

import jax
import jax.numpy as jnp
from jax import lax
from jax.experimental import pallas as pl
from jax.experimental.pallas import tpu as pltpu
from jax.sharding import PartitionSpec as P

HEAD_SIZE = 128
NPARAM = 688128
ADAPTER_SCALE = 2.0
NORM_EPS = 1e-05
LANCZOS_EPS = 1e-06
SCORE_CAP = 30.0
PRECISE = lax.Precision.HIGHEST
OBJ = 5
PIECES = 11
PIECE_ROWS = 56
LANES = 512


def dot_halved(left_side, right_side, left_dim, right_dim):
    return lax.dot_general(
        left_side,
        right_side,
        (((left_dim,), (right_dim,)), ((), ())),
        preferred_element_type=jnp.float32,
    )


def dot_entire(left_side, right_side, left_dim, right_dim):
    return lax.dot_general(
        left_side,
        right_side,
        (((left_dim,), (right_dim,)), ((), ())),
        precision=PRECISE,
        preferred_element_type=jnp.float32,
    )


def gather_by_exchange(block, axis):
    count = lax.axis_size(axis)
    copies = jnp.broadcast_to(block[None], (count,) + block.shape)
    return lax.all_to_all(copies, axis, 0, 0)


PAIR_ROWS = 40
PACK_ROWS = 48
PACK_LANES = 42
RESULT_LANES = 768


def rounded_parts(entire, count):
    parts = []
    for _ in range(count):
        part = entire.astype(jnp.bfloat16)
        parts.append(part)
        entire = entire - part.astype(jnp.float32)
    return parts


def lane_sum(values):
    return jnp.sum(values, axis=1, keepdims=True)


def row_sum(values):
    return jnp.sum(values, axis=0, keepdims=True)


def gram_body(rank_ref, jac_ref, start_ref, pairs_ref, rewards_ref, packed_ref):
    jac = jac_ref[...]
    start = start_ref[...]
    pairs = pairs_ref[...]
    rows = jac.shape[0]
    gram = dot_halved(jac, jac, 1, 1)
    starts = jnp.concatenate(rounded_parts(start, 3), 0)
    along = lane_sum(dot_halved(jac, starts, 1, 1))
    own_pairs = pairs[:, :rows]
    gram = dot_entire(dot_entire(own_pairs, gram, 1, 0), own_pairs, 1, 1)
    along = dot_entire(own_pairs, jnp.broadcast_to(along, (rows, 128)), 1, 0)
    rewards = pltpu.roll(rewards_ref[...], OBJ * rank_ref[0], axis=1)[:1]
    rewards = jnp.where(rank_ref[1] == 0, rewards, 0.0)
    apart = lane_sum(pairs * rewards)
    square = jnp.sum(start * start)
    lane = lax.broadcasted_iota(jnp.int32, (PACK_ROWS, 128), 1)
    row = lax.broadcasted_iota(jnp.int32, (PACK_ROWS, 128), 0)
    wide = jnp.concatenate([gram, jnp.zeros((PACK_ROWS, 128 - PACK_ROWS), jnp.float32)], 1)
    wide = jnp.where(lane < PAIR_ROWS, wide, 0.0)
    wide = jnp.where(lane == PAIR_ROWS, along, wide)
    wide = jnp.where(lane == PAIR_ROWS + 1, apart, wide)
    wide = jnp.where((row == PAIR_ROWS) & (lane == 0), square, wide)
    packed_ref[...] = (
        wide[:16]
        + pltpu.roll(wide[16:32], PACK_LANES, axis=1)
        + pltpu.roll(wide[32:], 2 * PACK_LANES, axis=1)
    )


def lanczos_body(packed_ref, pairs_ref, jac_ref, result_ref, part_ref):
    packed = jnp.sum(packed_ref[...], axis=0)
    wide = jnp.concatenate(
        [
            packed,
            pltpu.roll(packed, 128 - PACK_LANES, axis=1),
            pltpu.roll(packed, 128 - 2 * PACK_LANES, axis=1),
        ],
        0,
    )
    lane = lax.broadcasted_iota(jnp.int32, (PACK_ROWS, 128), 1)
    row = lax.broadcasted_iota(jnp.int32, (PACK_ROWS, 128), 0)
    inside = row < PAIR_ROWS
    gram = jnp.where(inside & (lane < PAIR_ROWS), wide, 0.0)
    along = lane_sum(jnp.where(inside & (lane == PAIR_ROWS), wide, 0.0))
    apart = lane_sum(jnp.where(inside & (lane == PAIR_ROWS + 1), wide, 0.0))
    picked = jnp.where((row == PAIR_ROWS) & (lane == 0), wide, 0.0)
    start_square = lane_sum(row_sum(picked)) / NPARAM
    diagonal = row == lane

    def gram_times(column):
        across = row_sum(jnp.where(diagonal, column, 0.0))
        return lane_sum(gram * across)

    def inner(left_side, right_side):
        return row_sum(left_side * right_side) / NPARAM

    decayed = jnp.exp(-jnp.abs(apart))
    curvature = decayed / ((1.0 + decayed) * (1.0 + decayed)) / (16 // 2)
    start_scale = lax.rsqrt(start_square + LANCZOS_EPS)
    first_square = start_square * start_scale * start_scale
    along_one = along * start_scale
    pull_one = curvature * along_one
    alpha_one = inner(pull_one, along_one)
    gram_pull = gram_times(pull_one)
    beta_one = jnp.sqrt(
        inner(pull_one, gram_pull) - alpha_one * alpha_one * (2.0 - first_square) + LANCZOS_EPS
    )
    along_two = (gram_pull - alpha_one * along_one) / beta_one
    pull_two = curvature * along_two
    first_second = alpha_one * (1.0 - first_square) / beta_one
    alpha_two = inner(pull_two, along_two) - beta_one * first_second
    mixed = pull_two - (alpha_two / beta_one) * pull_one
    first_part = alpha_two * alpha_one / beta_one - beta_one
    beta_two = jnp.sqrt(
        inner(mixed, gram_times(mixed))
        + 2.0 * first_part * inner(mixed, along_one)
        + first_part * first_part * first_square
        + LANCZOS_EPS
    )
    part_ref[...] = jnp.broadcast_to(first_part * start_scale / beta_two, part_ref.shape)
    across = row_sum(pairs_ref[...] * (mixed / beta_two))
    jac = jac_ref[...]
    rows = jac.shape[0]
    parts = rounded_parts(jnp.broadcast_to(across[:, :rows], (8, rows)), 3)
    result = sum(dot_halved(part, jac, 1, 0) for part in parts)[:1]
    spare = jnp.zeros((6, 128), jnp.float32)

    def chunks(start, count, size):
        return [result[:, start + size * step : start + size * (step + 1)] for step in range(count)]

    main = jnp.concatenate(chunks(0, 8, LANES), 0)
    middle = jnp.concatenate(chunks(8 * LANES, 8, 128), 0)
    last = jnp.concatenate(chunks(10 * LANES, 2, 128) + [spare], 0)
    result_ref[...] = jnp.concatenate([main, middle, last], 1).astype(jnp.bfloat16)


def assemble_body(
    core_ref,
    part_ref,
    own_ref,
    other_ref,
    a_ref,
    bq_ref,
    bkv_ref,
    ao_ref,
    bo_ref,
    out_a_ref,
    out_bq_ref,
    out_bkv_ref,
    out_ao_ref,
    out_bo_ref,
):
    step = pl.program_id(0)
    part = part_ref[0, 0]

    def one_hot(size, first, second):
        row = lax.broadcasted_iota(jnp.int32, (size, size), 0)
        lane = lax.broadcasted_iota(jnp.int32, (size, size), 1)
        wanted = (row % second) * first + row // second
        return jnp.where(lane == wanted, 1.0, 0.0).astype(jnp.bfloat16)

    row = lax.broadcasted_iota(jnp.int32, (64, 64), 0)
    lane = lax.broadcasted_iota(jnp.int32, (64, 64), 1)
    wanted = (row % 8) * 8 + ((row % 16) // 8) * 4 + row // 16
    moved = jnp.where(lane == wanted, 1.0, 0.0).astype(jnp.bfloat16)

    def pick(core, spot, lanes):
        return jnp.where(
            core_ref[0] == core, own_ref[spot, :, lanes], other_ref[spot, :, lanes]
        )

    for half in range(2):
        spot = pl.ds(pl.multiple_of(8 * step, 8), 8)
        block = pick(half, spot, slice(0, LANES)).reshape(64, LANES)
        placed = dot_halved(moved, block, 1, 0).reshape(4, 16, LANES)
        lanes = slice(half * LANES, (half + 1) * LANES)
        out_a_ref[:, :, lanes] = placed[:3] + part * a_ref[:, :, lanes]
        out_bo_ref[:, lanes] = placed[3] + part * bo_ref[:, lanes]
    block = jnp.concatenate(
        [pick(at % 2, 8 * (at // 2) + step, slice(LANES, None)) for at in range(16)], 0
    )
    placed = dot_halved(one_hot(128, 8, 16), block, 1, 0)
    for chunk in range(4):
        lanes = slice(chunk * 128, (chunk + 1) * 128)
        out_bq_ref[:, lanes] = placed[16 * chunk : 16 * chunk + 16, :128] + part * bq_ref[:, lanes]
        out_ao_ref[:, lanes] = (
            placed[64 + 16 * chunk : 80 + 16 * chunk, :128] + part * ao_ref[:, lanes]
        )
    out_bkv_ref[0] = placed[:16, 128:] + part * bkv_ref[0]
    out_bkv_ref[1] = placed[16:32, 128:] + part * bkv_ref[1]


def whole(count):
    return [pl.BlockSpec(memory_space=pltpu.VMEM)] * count


def product(left, right, right_dim):
    left_both = jnp.concatenate(rounded_parts(left, 2), 1)
    upper, lower = rounded_parts(right, 2)
    if right_dim == 0:
        rows = jnp.concatenate([upper, lower], 1)
        both = dot_halved(left_both, jnp.concatenate([rows, rows], 0), 1, 0)
    else:
        rows = jnp.concatenate([upper, lower], 0)
        both = dot_halved(left_both, jnp.concatenate([rows, rows], 1), 1, 1)
    size = right.shape[1 - right_dim]
    return both[:, :size] + both[:, size:]


def tall(parts):
    return jnp.concatenate(parts, 0)


def flat(parts):
    return jnp.concatenate(parts, 1)


def corners(both, rows, lanes):
    upper = both[:rows] + both[rows:]
    return upper[:, :lanes] + upper[:, lanes:]


def stack(rows):
    return tall([rows[:, at : at + 128] for at in range(0, rows.shape[1], 128)])


def unstack(rows):
    return flat([rows[at : at + 128] for at in range(0, rows.shape[0], 128)])


def place_shards(spots_ref, whole_ref, shards, semaphores):
    half = whole_ref.shape[1] // 2
    copies = []
    for at, shard in enumerate(shards):
        spot = at if at < 6 else 6 + (at - 6) // 2
        rows = pl.ds(pl.multiple_of(spots_ref[spot] * 16, 16), 16)
        if at < 6:
            target = whole_ref.at[rows, :]
        else:
            target = whole_ref.at[rows, pl.ds((at % 2) * half, half)]
        copies.append(pltpu.make_async_copy(shard, target, semaphores.at[at]))
    for copy in copies:
        copy.start()
    return copies


def launch(pairs, semaphores, first):
    copies = prepared(pairs, semaphores, first)
    begin(copies)
    return copies


def finish(copies):
    for copy in copies:
        copy.wait()


def prepared(pairs, semaphores, first):
    return [
        pltpu.make_async_copy(source, target, semaphores.at[first + at])
        for at, (source, target) in enumerate(pairs)
    ]


def begin(copies):
    for copy in copies:
        copy.start()


def span_of(step):
    if isinstance(step, int):
        return pl.ds(step * CHUNK, CHUNK)
    return pl.ds(pl.multiple_of(step * CHUNK, CHUNK), CHUNK)


ANYWHERE = pl.BlockSpec(memory_space=pl.ANY)
LARGE = 60 * 2**20


def gather_by_relays(block):
    half = block.shape[1] // 2

    def permute(array, y_step, z_step):
        pairs = [
            (at, ((at // 4 + y_step) % 2) * 4 + (at % 4 + z_step) % 4) for at in range(8)
        ]
        return lax.ppermute(array, "tensor", pairs)

    across = permute(block, 1, 0)
    below = permute(block, 0, 1)
    above = permute(block, 0, 3)
    across_below = permute(across, 0, 1)
    across_above = permute(across, 0, 3)
    far = [permute(below[:, :half], 0, 1), permute(above[:, half:], 0, 3)]
    across_far = [
        permute(across_below[:, :half], 0, 1),
        permute(across_above[:, half:], 0, 3),
    ]
    return [block, across, below, above, across_below, across_above] + far + across_far


def shard_spots():
    rank = lax.axis_index("tensor").astype(jnp.int32)
    y, z = rank // 4 * 4, rank % 4
    other = 4 - y
    return jnp.stack(
        [
            y + z,
            other + z,
            y + (z + 3) % 4,
            y + (z + 1) % 4,
            other + (z + 3) % 4,
            other + (z + 1) % 4,
            y + (z + 2) % 4,
            other + (z + 2) % 4,
        ]
    )


CHUNK = 2048
STATE_ROWS = 2368


def forward_body(
    spots_ref,
    shard_0,
    shard_1,
    shard_2,
    shard_3,
    shard_4,
    shard_5,
    shard_6,
    shard_7,
    shard_8,
    shard_9,
    query_weight_hbm,
    kv_weight_hbm,
    down_hbm,
    output_weight_hbm,
    up_output_hbm,
    small_hbm,
    tokens_hbm,
    out_hbm,
    state_hbm,
    tokens_ref,
    query_weight_ref,
    kv_weight_ref,
    down_ref,
    output_weight_ref,
    up_output_ref,
    small_ref,
    out_ref,
    state_ref,
    query_sum,
    kv_sum,
    low_sum,
    semaphores,
):
    shards = [
        shard_0,
        shard_1,
        shard_2,
        shard_3,
        shard_4,
        shard_5,
        shard_6,
        shard_7,
        shard_8,
        shard_9,
    ]
    placed = place_shards(spots_ref, tokens_ref, shards, semaphores)
    count = tokens_ref.shape[1] // CHUNK

    def early(step):
        span = span_of(step)
        pairs = [
            (query_weight_hbm.at[span, :], query_weight_ref.at[span, :]),
            (kv_weight_hbm.at[:, span, :], kv_weight_ref.at[:, span, :]),
            (down_hbm.at[:, span], down_ref.at[:, span]),
        ]
        return prepared(pairs, semaphores, 10 + 3 * step)

    def late(step):
        span = span_of(step)
        pairs = [
            (output_weight_hbm.at[:, span], output_weight_ref.at[:, span]),
            (up_output_hbm.at[:, span], up_output_ref.at[:, span]),
        ]
        return prepared(pairs, semaphores, 10 + 3 * count + 2 * step)

    def departing(step):
        span = span_of(step)
        pairs = [(out_ref.at[:, :, span], out_hbm.at[:, :, span])]
        return prepared(pairs, semaphores, 10 + 5 * count + step)

    for step in range(count):
        begin(early(step))
    small_copy = launch([(small_hbm, small_ref)], semaphores, 10 + 6 * count)
    for step in range(count):
        begin(late(step))
    finish(placed)
    leaving = launch([(tokens_ref, tokens_hbm)], semaphores, 11 + 6 * count)
    query_sum[...] = jnp.zeros(query_sum.shape, jnp.float32)
    kv_sum[...] = jnp.zeros(kv_sum.shape, jnp.float32)
    low_sum[...] = jnp.zeros(low_sum.shape, jnp.float32)

    def project(step, _):
        finish(early(step))
        span = span_of(step)
        tokens = tokens_ref[:, span]
        query_sum[...] += dot_halved(tokens, query_weight_ref[span, :], 1, 0)
        kv_sum[...] += dot_halved(
            tokens, flat([kv_weight_ref[0, span, :], kv_weight_ref[1, span, :]]), 1, 0
        )
        low_sum[:48] += dot_halved(down_ref[:, span], tokens, 1, 1)
        return 0

    lax.fori_loop(0, count, project, 0)
    finish(small_copy)
    low_turned = low_sum[...]
    low = low_turned.T
    root = 1.0 / math.sqrt(HEAD_SIZE)

    def adapted(total, piece, up):
        parts = rounded_parts(low[:, 16 * piece : 16 * piece + 16], 2)
        return total + ADAPTER_SCALE * dot_halved(flat(parts), tall([up, up]), 1, 0)

    query = stack(adapted(query_sum[...], 0, small_ref[:, 512:1024]))
    keys = adapted(kv_sum[:, :128], 1, small_ref[:, 1024:1152])
    values = adapted(kv_sum[:, 128:], 2, small_ref[:, 1152:])
    capped = jnp.tanh(product(query, keys, 1) * (root / SCORE_CAP))
    row = lax.broadcasted_iota(jnp.int32, (512, 128), 0) % 128
    lane = lax.broadcasted_iota(jnp.int32, (512, 128), 1)
    weights = jnp.where(row >= lane, jnp.exp(SCORE_CAP * capped), 0.0)
    probs = weights / lane_sum(weights)
    context_rows = product(probs, values, 0)
    context = unstack(context_rows)
    low_pair = dot_halved(small_ref[:, :512], tall(rounded_parts(context, 2)), 1, 1)
    context_low = ADAPTER_SCALE * (low_pair[:, :128] + low_pair[:, 128:])
    state_ref[0:512] = query
    state_ref[512:1024] = context_rows
    state_ref[1024:1536] = probs
    state_ref[1536:2048] = capped
    state_ref[2048:2176] = keys
    state_ref[2176:2304] = values
    state_ref[2304:2352] = low_turned[:48]
    state_ref[2352:2368] = context_low
    halved = context.astype(jnp.bfloat16)
    turned = tall([context_low, jnp.zeros((112, 128), jnp.float32)]).T[:, :16]
    halved_low = flat(rounded_parts(turned, 2))
    leaving += launch([(state_ref, state_hbm)], semaphores, 12 + 6 * count)

    def write(step, _):
        finish(late(step))
        span = span_of(step)
        up = up_output_ref[:, span]
        terms = dot_halved(halved, output_weight_ref[:, span], 1, 0) + dot_halved(
            halved_low, tall([up, up]), 1, 0
        )
        out_ref[:, :, span] = terms.astype(jnp.bfloat16).reshape(8, 16, CHUNK)
        begin(departing(step))
        return 0

    lax.fori_loop(0, count, write, 0)
    for step in range(count):
        finish(departing(step))
    finish(leaving)


def forward(
    spots, shards, query_weight, key_value_weight, down_rows, output_weight, up_output, small
):
    width = shards[0].shape[1]
    query_cols = query_weight.shape[1]
    arrays = (query_weight, key_value_weight, down_rows, output_weight, up_output, small)
    results = [
        jax.ShapeDtypeStruct((128, width), jnp.bfloat16),
        jax.ShapeDtypeStruct((8, 16, width), jnp.bfloat16),
        jax.ShapeDtypeStruct((STATE_ROWS, 128), jnp.float32),
    ]
    scratch = [results[0], *arrays, results[1], results[2]]
    return pl.pallas_call(
        forward_body,
        in_specs=[pl.BlockSpec(memory_space=pltpu.SMEM)]
        + [ANYWHERE] * (len(shards) + len(arrays)),
        out_specs=[ANYWHERE] * 3,
        out_shape=results,
        scratch_shapes=[pltpu.VMEM(array.shape, array.dtype) for array in scratch]
        + [
            pltpu.VMEM((128, query_cols), jnp.float32),
            pltpu.VMEM((128, 256), jnp.float32),
            pltpu.VMEM((128, 128), jnp.float32),
            pltpu.SemaphoreType.DMA((13 + 6 * (width // CHUNK),)),
        ],
        compiler_params=pltpu.CompilerParams(vmem_limit_bytes=LARGE),
        name="forward",
    )(spots, *shards, *arrays)


def cotangents_body(
    lens_ref,
    spots_ref,
    shard_0,
    shard_1,
    shard_2,
    shard_3,
    shard_4,
    shard_5,
    shard_6,
    shard_7,
    shard_8,
    shard_9,
    weight_hbm,
    side_hbm,
    state_hbm,
    small_hbm,
    resid_hbm,
    factors_ref,
    narrow_ref,
    scalars_ref,
    resid_ref,
    weight_ref,
    side_ref,
    state_ref,
    small_ref,
    through_ref,
    slow_ref,
    square_ref,
    semaphores,
):
    shards = [
        shard_0,
        shard_1,
        shard_2,
        shard_3,
        shard_4,
        shard_5,
        shard_6,
        shard_7,
        shard_8,
        shard_9,
    ]
    placed = place_shards(spots_ref, resid_ref, shards, semaphores)
    count = resid_ref.shape[1] // CHUNK

    def early(step):
        span = span_of(step)
        pairs = [
            (weight_hbm.at[:, span], weight_ref.at[:, span]),
            (side_hbm.at[:, span], side_ref.at[:, span]),
        ]
        return prepared(pairs, semaphores, 10 + 2 * step)

    for step in range(count):
        begin(early(step))
    first = 10 + 2 * count
    others = launch([(state_hbm, state_ref), (small_hbm, small_ref)], semaphores, first)
    slow_ref[...] = jnp.zeros(slow_ref.shape, jnp.float32)
    through_ref[...] = jnp.zeros(through_ref.shape, jnp.float32)
    square_ref[...] = jnp.zeros(square_ref.shape, jnp.float32)
    narrow_ref[...] = jnp.zeros(narrow_ref.shape, jnp.float32)
    width = resid_ref.shape[1]
    finish(placed)
    leaving = launch([(resid_ref, resid_hbm)], semaphores, first + 2)

    def project(step, _):
        finish(early(step))
        span = span_of(step)
        chunk = resid_ref[:, span]
        side = side_ref[:, span]
        left = tall([chunk, side[16:]])
        through_ref[...] += dot_halved(left, weight_ref[:, span], 1, 1)
        slow_ref[:144, :32] += dot_halved(left, side, 1, 1)
        wide = chunk.astype(jnp.float32)
        square = jnp.zeros((128, 128), jnp.float32)
        for lanes in range(0, CHUNK, 128):
            square = square + wide[:, lanes : lanes + 128] * wide[:, lanes : lanes + 128]
        square_ref[...] += square
        return 0

    lax.fori_loop(0, count, project, 0)
    finish(others)
    finish_cotangents(
        lens_ref,
        width,
        state_ref,
        small_ref,
        factors_ref,
        narrow_ref,
        scalars_ref,
        through_ref,
        slow_ref,
        square_ref,
    )
    finish(leaving)


def finish_cotangents(
    lens_ref,
    width,
    state_ref,
    small_ref,
    factors_ref,
    narrow_ref,
    scalars_ref,
    through_ref,
    slow_ref,
    square_ref,
):
    if True:
        length_own = lens_ref[0]
        root = 1.0 / math.sqrt(HEAD_SIZE)
        slow = slow_ref[...]
        slow_turned = slow.T
        square = square_ref[...]
        inverse = lax.rsqrt(lane_sum(square) / width + NORM_EPS)
        inverse_turned = lax.rsqrt(row_sum(square.T) / width + NORM_EPS)
        each = 1.0 / jnp.broadcast_to(length_own, (1, 1)).astype(jnp.float32)
        share = jnp.where(
            lax.broadcasted_iota(jnp.int32, (128, 1), 0) < length_own, each, 0.0
        )
        share_turned = jnp.where(
            lax.broadcasted_iota(jnp.int32, (1, 128), 1) < length_own, each, 0.0
        )
        logits = inverse * slow[:128, 16:32]
        lead = share * inverse
        pulled = lead * inverse * logits / width
        lead_turned = share_turned * inverse_turned
        pulled_turned = (
            lead_turned * inverse_turned * inverse_turned * slow_turned[16:32, :128] / width
        )
        low_turned = slow_turned[:16, :128]
        scalars_ref[:8] = jnp.zeros((8, 128), jnp.float32)
        scalars_ref[:1, :16] = row_sum(share * logits)
        down = small_ref[:, :512]
        through = through_ref[...] + ADAPTER_SCALE * dot_halved(
            flat(rounded_parts(slow[:144, :16], 2)), tall([down, down]), 1, 0
        )
        context_rows = state_ref[512:1024]
        context = unstack(context_rows)
        probs = state_ref[1024:1536]
        capped = state_ref[1536:2048]
        slope = probs * (1.0 - capped * capped) * root
        probs_turned = tall(rounded_parts(probs.T, 2))
        query_turned = tall(rounded_parts(state_ref[0:512].T, 2))
        keys = state_ref[2048:2176]
        values = state_ref[2176:2304]
        low = [
            tall(rounded_parts(state_ref[2304 + 16 * at : 2320 + 16 * at], 2)) for at in range(3)
        ]
        up_query = small_ref[:, 512:1024]
        up_keys = small_ref[:, 1024:1152]
        up_values = small_ref[:, 1152:]
        context_low = state_ref[2352:2368]
        through_ref[...] = through
        through_tokens = through[:128]
        heads_low = slow_turned[:16, 128:]
        lane_pulled = lax.broadcasted_iota(jnp.int32, pulled.shape, 1)
        lane_low = lax.broadcasted_iota(jnp.int32, heads_low.shape, 1)
        row_pulled = lax.broadcasted_iota(jnp.int32, pulled_turned.shape, 0)

        def objective(obj, _):
            pulled_own = lane_sum(jnp.where(lane_pulled == obj, pulled, 0.0))
            lead_row = through_ref[pl.ds(128 + obj, 1), :]
            cot = stack(lead * lead_row - pulled_own * through_tokens)
            cot_prob = product(cot, values, 1)
            cot_score = slope * (cot_prob - lane_sum(cot * context_rows))
            cot_query = unstack(product(cot_score, keys, 0))
            cot_keys = corners(
                dot_halved(query_turned, flat(rounded_parts(cot_score, 2)), 1, 0), 128, 128
            )
            cot_values = corners(
                dot_halved(probs_turned, flat(rounded_parts(cot, 2)), 1, 0), 128, 128
            )
            query_parts = rounded_parts(cot_query, 2)
            keys_parts = rounded_parts(cot_keys, 2)
            values_parts = rounded_parts(cot_values, 2)
            factor_query = dot_halved(up_query, tall(query_parts), 1, 1)
            factor_keys = dot_halved(up_keys, flat(keys_parts), 1, 0)
            factor_values = dot_halved(up_values, tall(values_parts), 1, 1)
            rows = [
                ADAPTER_SCALE * (factor[:, :128] + factor[:, 128:])
                for factor in (factor_query, factor_keys, factor_values)
            ] + [context_low]
            for piece in range(4):
                for half in range(2):
                    factors_ref[pl.ds(20 * half + 5 * piece + obj, 8, stride=40), :] = rows[
                        piece
                    ][8 * half : 8 * half + 8]
            jac_query = corners(dot_halved(low[0], flat(query_parts), 1, 0), 16, 512)
            jac_keys = corners(dot_halved(low[1], tall(keys_parts), 1, 1), 16, 128)
            jac_values = corners(dot_halved(low[2], flat(values_parts), 1, 0), 16, 128)
            pulled_row = row_sum(jnp.where(row_pulled == obj, pulled_turned, 0.0))
            head_low = lane_sum(jnp.where(lane_low == obj, heads_low, 0.0))
            jac_down = product(head_low * lead_turned - pulled_row * low_turned, context, 0)
            blocks = [jac_query[:, at : at + 128] for at in range(0, 512, 128)]
            blocks += [jac_down[:, at : at + 128] for at in range(0, 512, 128)]
            spots = [(0, 0), (0, 1), (0, 2), (0, 3), (5, 0), (5, 1), (5, 2), (5, 3)]
            spots += [(10, 0), (10, 1)]
            for (row, tile), block in zip(spots, blocks + [jac_keys, jac_values]):
                for half in range(2):
                    narrow_ref[tile, pl.ds(128 * half + row + obj, 8, stride=16), :] = (
                        ADAPTER_SCALE * block[8 * half : 8 * half + 8]
                    )
            return 0

        lax.fori_loop(0, OBJ, objective, 0, unroll=True)
        blank = jnp.zeros((15, 128), jnp.float32)
        scalars_ref[8:48] = jnp.concatenate([blank, pulled_turned[:5]] * 2, 0)
        scalars_ref[48:] = jnp.broadcast_to(lead_turned, (40, 128))


def cotangents(lens, spots, shards, output_weight, side, state, small):
    width = shards[0].shape[1]
    query_cols = output_weight.shape[0]
    arrays = (output_weight, side, state, small)
    results = [
        jax.ShapeDtypeStruct((128, width), jnp.bfloat16),
        jax.ShapeDtypeStruct((320, 128), jnp.float32),
        jax.ShapeDtypeStruct((4, 256, 128), jnp.float32),
        jax.ShapeDtypeStruct((88, 128), jnp.float32),
    ]
    return pl.pallas_call(
        cotangents_body,
        in_specs=[pl.BlockSpec(memory_space=pltpu.SMEM)] * 2
        + [ANYWHERE] * (len(shards) + len(arrays)),
        out_specs=[ANYWHERE] + whole(3),
        out_shape=results,
        scratch_shapes=[pltpu.VMEM(array.shape, array.dtype) for array in (results[0], *arrays)]
        + [
            pltpu.VMEM((144, query_cols), jnp.float32),
            pltpu.VMEM((256, 128), jnp.float32),
            pltpu.VMEM((128, 128), jnp.float32),
            pltpu.SemaphoreType.DMA((13 + 2 * (width // CHUNK),)),
        ],
        compiler_params=pltpu.CompilerParams(vmem_limit_bytes=LARGE),
        name="cotangents",
    )(lens, spots, *shards, *arrays)


def jacobian_body(
    factors_hbm,
    tokens_hbm,
    resid_hbm,
    side_hbm,
    scalars_hbm,
    narrow_hbm,
    payload_hbm,
    factors_ref,
    tokens_ref,
    resid_ref,
    side_ref,
    scalars_ref,
    narrow_ref,
    payload_ref,
    semaphores,
):
    early = launch([(factors_hbm, factors_ref), (scalars_hbm, scalars_ref)], semaphores, 0)
    count = tokens_ref.shape[1] // CHUNK
    per_step = CHUNK // LANES

    def arriving(step):
        span = span_of(step)
        pairs = [
            (tokens_hbm.at[:, span], tokens_ref.at[:, span]),
            (resid_hbm.at[:, span], resid_ref.at[:, span]),
            (side_hbm.at[:, span], side_ref.at[:, span]),
        ]
        return prepared(pairs, semaphores, 3 + 3 * step)

    def departing(step):
        groups = pl.ds(step * per_step, per_step)
        pairs = [(payload_ref.at[groups], payload_hbm.at[groups])]
        return prepared(pairs, semaphores, 3 + 3 * count + step)

    begin(arriving(0))
    early += launch([(narrow_hbm, narrow_ref)], semaphores, 2)
    for step in range(1, count):
        begin(arriving(step))
    finish(early)
    factors = jnp.sum(factors_ref[...], axis=0)
    row = lax.broadcasted_iota(jnp.int32, (40, 1), 0) % 20
    last = row >= 15
    left = flat(
        [jnp.where(last, 0.0, factors), jnp.where(last, -factors * scalars_ref[8:48], 0.0)]
    )
    lane = lax.broadcasted_iota(jnp.int32, (40, 16), 1)
    lead = jnp.where(lane == row - 15, lane_sum(factors * scalars_ref[48:]), 0.0)

    def both(rows):
        upper = rows.astype(jnp.bfloat16).astype(jnp.float32)
        return tall([upper, rows - upper]).astype(jnp.bfloat16)

    left = both(left)
    lead = both(lead)

    def place(step, _):
        finish(arriving(step))
        span = span_of(step)
        right = tall([tokens_ref[:, span], resid_ref[:, span]])
        pair = dot_halved(left, right, 1, 0) + dot_halved(lead, side_ref[16:, span], 1, 0)
        rows = pair[:40] + pair[40:]
        for inner in range(per_step):
            group = step * per_step + inner
            below = flat(
                [
                    narrow_ref[tile, pl.ds(pl.multiple_of(group * 16, 16), 16), :]
                    for tile in range(4)
                ]
            )
            block = tall([rows[:, inner * LANES : (inner + 1) * LANES], below])
            payload_ref[group] = block.astype(jnp.bfloat16)
        begin(departing(step))
        return 0

    lax.fori_loop(0, count, place, 0)
    for step in range(count):
        finish(departing(step))


def jacobian(*arrays):
    result = jax.ShapeDtypeStruct((16, PIECE_ROWS, LANES), jnp.bfloat16)
    steps = arrays[1].shape[1] // CHUNK
    return pl.pallas_call(
        jacobian_body,
        in_specs=[ANYWHERE] * len(arrays),
        out_specs=ANYWHERE,
        out_shape=result,
        scratch_shapes=[pltpu.VMEM(array.shape, array.dtype) for array in (*arrays, result)]
        + [pltpu.SemaphoreType.DMA((3 + 4 * steps,))],
        compiler_params=pltpu.CompilerParams(vmem_limit_bytes=LARGE),
        name="jacobian",
    )(*arrays)


def assemble(core, part, own, other, start_a, start_bq, start_bkv, start_ao, start_bo):
    steps = 8
    shapes = [start_a, start_bq, start_bkv, start_ao, start_bo]
    blocks = [
        pl.BlockSpec((3, 16, 2 * LANES), lambda step: (0, 0, step)),
        pl.BlockSpec((16, LANES), lambda step: (0, step)),
        pl.BlockSpec((2, 16, HEAD_SIZE), lambda step: (0, 0, step)),
        pl.BlockSpec((16, LANES), lambda step: (0, step)),
        pl.BlockSpec((16, 2 * LANES), lambda step: (0, step)),
    ]
    return pl.pallas_call(
        assemble_body,
        grid=(steps,),
        in_specs=[
            pl.BlockSpec(memory_space=pltpu.SMEM),
            pl.BlockSpec(memory_space=pltpu.SMEM),
            pl.BlockSpec(own.shape, lambda step: (0, 0, 0)),
            pl.BlockSpec(other.shape, lambda step: (0, 0, 0)),
        ]
        + blocks,
        out_specs=blocks,
        out_shape=[jax.ShapeDtypeStruct(shape.shape, jnp.float32) for shape in shapes],
        compiler_params=pltpu.CompilerParams(vmem_limit_bytes=14 * 2**20),
        name="assemble",
    )(core, part, own, other, *(pltpu.with_memory_space_constraint(x, pltpu.HBM) for x in shapes))


def local(
    hidden,
    query_weight,
    key_value_weight,
    output_weight,
    head,
    lens,
    partner,
    adapter_down_qkv,
    adapter_up_query,
    adapter_up_key_value,
    adapter_down_output,
    adapter_up_output,
    initial_down_qkv,
    initial_up_query,
    initial_up_key_value,
    initial_down_output,
    initial_up_output,
):
    _, part_length, width = hidden.shape
    shards = lax.axis_size("tensor")
    groups = lax.axis_size("dp")
    tensor_rank = lax.axis_index("tensor")
    group_rank = lax.axis_index("dp")
    query_cols = query_weight.shape[1]
    length = part_length * shards

    down_rows = jnp.transpose(adapter_down_qkv, (0, 2, 1)).reshape(48, width)
    down_output = adapter_down_output.T
    head_rows = head.T
    spots = shard_spots()
    side = jnp.concatenate([adapter_up_output, head_rows, jnp.zeros((11, width), head.dtype)], 0)
    small = jnp.concatenate(
        [down_output, adapter_up_query, adapter_up_key_value[0], adapter_up_key_value[1]], 1
    )
    tokens, out_terms, state = forward(
        spots,
        gather_by_relays(hidden[0]),
        query_weight,
        key_value_weight,
        down_rows,
        output_weight,
        adapter_up_output,
        small,
    )
    out_pieces = lax.all_to_all(out_terms, "tensor", 0, 0)
    resid_own = hidden[0].astype(jnp.float32) + jnp.sum(out_pieces.astype(jnp.float32), 0)
    resid, factors, narrow, scalars = cotangents(
        lens,
        spots,
        gather_by_relays(resid_own.astype(jnp.bfloat16)),
        output_weight,
        side,
        state,
        small,
    )
    factors = lax.all_to_all(factors.reshape(shards, 8 * OBJ, length), "tensor", 0, 0)
    payload = jacobian(factors, tokens, resid, side, scalars, narrow)
    spread = lax.all_to_all(payload, "dp", 0, 0)
    jac = (
        spread[:, : PIECES * OBJ]
        .reshape(groups, PIECES, OBJ, LANES)
        .transpose(0, 2, 1, 3)
        .reshape(groups * OBJ, PIECES * LANES)
    )

    own_a = lax.dynamic_slice(
        jnp.transpose(initial_down_qkv, (0, 2, 1)).reshape(3, 2, shards, width),
        (0, 0, tensor_rank, group_rank * LANES),
        (3, 2, 1, LANES),
    ).reshape(3, 2, LANES)
    own_bo = lax.dynamic_slice(
        initial_up_output.reshape(2, shards, width),
        (0, tensor_rank, group_rank * LANES),
        (2, 1, LANES),
    ).reshape(2, LANES)
    own_bq = lax.dynamic_slice(
        initial_up_query, (group_rank, tensor_rank * query_cols), (1, query_cols)
    )
    own_ao = lax.dynamic_slice(
        initial_down_output.T, (group_rank, tensor_rank * query_cols), (1, query_cols)
    )
    own_bkv = lax.dynamic_slice(
        initial_up_key_value, (0, group_rank, tensor_rank * HEAD_SIZE), (2, 1, HEAD_SIZE)
    )
    own_start = jnp.concatenate(
        [
            jnp.concatenate([own_a.transpose(1, 0, 2), own_bo[:, None]], 1).reshape(8, LANES),
            own_bq,
            own_ao,
            jnp.concatenate(
                [own_bkv.reshape(1, 2 * HEAD_SIZE), jnp.zeros((1, LANES - 2 * HEAD_SIZE))], 1
            ),
        ],
        0,
    ).reshape(1, PIECES * LANES)
    own_start = own_start.astype(jnp.float32)
    sequences = jnp.arange(groups)
    leads = sequences < partner
    order = jnp.sum((sequences[None, :] < sequences[:, None]) & leads[None, :], 1)
    chosen = (
        leads[None, :] & (order[None, :] == jnp.arange(groups // 2)[:, None])
    ).astype(jnp.float32)
    differences = chosen - jnp.take(chosen, partner, axis=1)
    pairs = (
        differences[:, None, :, None] * jnp.eye(OBJ, dtype=jnp.float32)[None, :, None, :]
    ).reshape(PAIR_ROWS, groups * OBJ)
    pairs = jnp.pad(pairs, ((0, PACK_ROWS - PAIR_ROWS), (0, 128 - groups * OBJ)))
    packed = pl.pallas_call(
        gram_body,
        in_specs=[pl.BlockSpec(memory_space=pltpu.SMEM)] + whole(4),
        out_specs=pl.BlockSpec(memory_space=pltpu.VMEM),
        out_shape=jax.ShapeDtypeStruct((16, 128), jnp.float32),
        compiler_params=pltpu.CompilerParams(vmem_limit_bytes=6 * 2**20),
        name="gram",
    )(
        jnp.stack([group_rank, tensor_rank]).astype(jnp.int32),
        jac,
        own_start,
        pairs,
        scalars[:8],
    )
    packed = jnp.sum(gather_by_exchange(packed, "dp"), 0)
    packed = gather_by_exchange(packed, "tensor")
    own_result, part = pl.pallas_call(
        lanczos_body,
        in_specs=whole(3),
        out_specs=whole(2),
        out_shape=[
            jax.ShapeDtypeStruct((8, RESULT_LANES), jnp.bfloat16),
            jax.ShapeDtypeStruct((1, 128), jnp.float32),
        ],
        compiler_params=pltpu.CompilerParams(vmem_limit_bytes=6 * 2**20),
        name="lanczos",
    )(packed, pairs, jac)
    half = groups * shards // 2
    same_core = [
        [at for at in range(2 * half) if (at // shards) % 2 == core] for core in range(2)
    ]
    own_half = lax.all_to_all(
        jnp.broadcast_to(own_result[None], (half,) + own_result.shape),
        ("dp", "tensor"),
        0,
        0,
        axis_index_groups=same_core,
    )
    other_half = lax.ppermute(own_half, "dp", [(at, at ^ 1) for at in range(groups)])
    next_a, next_bq, next_bkv, next_ao, next_bo = assemble(
        (group_rank % 2).astype(jnp.int32).reshape(1),
        part,
        own_half,
        other_half,
        jnp.transpose(initial_down_qkv, (0, 2, 1)),
        initial_up_query,
        initial_up_key_value,
        initial_down_output.T,
        initial_up_output,
    )
    return jnp.transpose(next_a, (0, 2, 1)), next_bq, next_bkv, next_ao.T, next_bo


def solution(mesh):
    in_specs = (
        P("dp", "tensor", None),
        P(None, "tensor"),
        P(None, None, "tensor"),
        P("tensor", None),
        P(),
        P("dp"),
        P(),
        P(),
        P(None, "tensor"),
        P(None, None, "tensor"),
        P("tensor", None),
        P(),
        P(),
        P(),
        P(),
        P(),
        P(),
    )
    out_specs = (P(), P(), P(), P(), P())
    return jax.shard_map(local, mesh=mesh, in_specs=in_specs, out_specs=out_specs, check_vma=False)
```

```python
import math

import jax
import jax.numpy as jnp
from jax import lax
from jax.experimental import pallas as pl
from jax.experimental.pallas import tpu as pltpu
from jax.sharding import PartitionSpec as P

HEAD_SIZE = 128
NPARAM = 688128
ADAPTER_SCALE = 2.0
NORM_EPS = 1e-05
LANCZOS_EPS = 1e-06
SCORE_CAP = 30.0
PRECISE = lax.Precision.HIGHEST
OBJ = 5
PIECES = 11
PIECE_ROWS = 56
LANES = 512


def dot_halved(left_side, right_side, left_dim, right_dim):
    return lax.dot_general(
        left_side,
        right_side,
        (((left_dim,), (right_dim,)), ((), ())),
        preferred_element_type=jnp.float32,
    )


def dot_entire(left_side, right_side, left_dim, right_dim):
    return lax.dot_general(
        left_side,
        right_side,
        (((left_dim,), (right_dim,)), ((), ())),
        precision=PRECISE,
        preferred_element_type=jnp.float32,
    )


def gather_by_exchange(block, axis):
    count = lax.axis_size(axis)
    copies = jnp.broadcast_to(block[None], (count,) + block.shape)
    return lax.all_to_all(copies, axis, 0, 0)


PAIR_ROWS = 40
PACK_ROWS = 48
PACK_LANES = 42
RESULT_LANES = 768


def rounded_parts(entire, count):
    parts = []
    for _ in range(count):
        part = entire.astype(jnp.bfloat16)
        parts.append(part)
        entire = entire - part.astype(jnp.float32)
    return parts


def lane_sum(values):
    return jnp.sum(values, axis=1, keepdims=True)


def row_sum(values):
    return jnp.sum(values, axis=0, keepdims=True)


def gram_body(
    jac_ref,
    pairs_ref,
    rewards_ref,
    a_hbm,
    bq_hbm,
    bkv_hbm,
    ao_hbm,
    bo_hbm,
    packed_ref,
    a_ref,
    bq_ref,
    bkv_ref,
    ao_ref,
    bo_ref,
    semaphores,
):
    group = lax.axis_index("dp").astype(jnp.int32)
    rank = lax.axis_index("tensor").astype(jnp.int32)
    by_group = pl.ds(pl.multiple_of(group * LANES, LANES), LANES)
    by_rank = pl.ds(pl.multiple_of(rank * LANES, LANES), LANES)
    narrow = pl.ds(pl.multiple_of(rank * HEAD_SIZE, HEAD_SIZE), HEAD_SIZE)
    pairs = [
        (a_hbm.at[:, :, by_group], a_ref),
        (bq_hbm.at[:, by_rank], bq_ref),
        (bkv_hbm.at[:, :, narrow], bkv_ref),
        (ao_hbm.at[:, by_rank], ao_ref),
        (bo_hbm.at[:, by_group], bo_ref),
    ]
    copies = launch(pairs, semaphores, 0)
    jac = jac_ref[...]
    pairs = pairs_ref[...]
    rows = jac.shape[0]
    gram = dot_halved(jac, jac, 1, 1)
    finish(copies)
    blocks = []
    for row in (rank, rank + 8):
        blocks += [a_ref[piece, pl.ds(row, 1), :] for piece in range(3)]
        blocks.append(bo_ref[pl.ds(row, 1), :])
    blocks += [bq_ref[pl.ds(group, 1), :], ao_ref[pl.ds(group, 1), :]]
    blocks += [bkv_ref[piece, pl.ds(group, 1), :] for piece in range(2)]
    start = flat(blocks + [jnp.zeros((1, LANES - 2 * HEAD_SIZE), jnp.float32)])
    starts = jnp.concatenate(rounded_parts(start, 3), 0)
    along = lane_sum(dot_halved(jac, starts, 1, 1))
    own_pairs = pairs[:, :rows]
    gram = dot_entire(dot_entire(own_pairs, gram, 1, 0), own_pairs, 1, 1)
    along = dot_entire(own_pairs, jnp.broadcast_to(along, (rows, 128)), 1, 0)
    rewards = pltpu.roll(rewards_ref[...], OBJ * group, axis=1)[:1]
    rewards = jnp.where(rank == 0, rewards, 0.0)
    apart = lane_sum(pairs * rewards)
    square = jnp.sum(start * start)
    lane = lax.broadcasted_iota(jnp.int32, (PACK_ROWS, 128), 1)
    row = lax.broadcasted_iota(jnp.int32, (PACK_ROWS, 128), 0)
    wide = jnp.concatenate([gram, jnp.zeros((PACK_ROWS, 128 - PACK_ROWS), jnp.float32)], 1)
    wide = jnp.where(lane < PAIR_ROWS, wide, 0.0)
    wide = jnp.where(lane == PAIR_ROWS, along, wide)
    wide = jnp.where(lane == PAIR_ROWS + 1, apart, wide)
    wide = jnp.where((row == PAIR_ROWS) & (lane == 0), square, wide)
    packed_ref[...] = (
        wide[:16]
        + pltpu.roll(wide[16:32], PACK_LANES, axis=1)
        + pltpu.roll(wide[32:], 2 * PACK_LANES, axis=1)
    )


def lanczos_body(packed_ref, pairs_ref, jac_ref, result_ref, part_ref):
    packed = jnp.sum(packed_ref[...], axis=0)
    wide = jnp.concatenate(
        [
            packed,
            pltpu.roll(packed, 128 - PACK_LANES, axis=1),
            pltpu.roll(packed, 128 - 2 * PACK_LANES, axis=1),
        ],
        0,
    )
    lane = lax.broadcasted_iota(jnp.int32, (PACK_ROWS, 128), 1)
    row = lax.broadcasted_iota(jnp.int32, (PACK_ROWS, 128), 0)
    inside = row < PAIR_ROWS
    gram = jnp.where(inside & (lane < PAIR_ROWS), wide, 0.0)
    along = lane_sum(jnp.where(inside & (lane == PAIR_ROWS), wide, 0.0))
    apart = lane_sum(jnp.where(inside & (lane == PAIR_ROWS + 1), wide, 0.0))
    picked = jnp.where((row == PAIR_ROWS) & (lane == 0), wide, 0.0)
    start_square = lane_sum(row_sum(picked)) / NPARAM
    diagonal = row == lane

    def gram_times(column):
        across = row_sum(jnp.where(diagonal, column, 0.0))
        return lane_sum(gram * across)

    def inner(left_side, right_side):
        return row_sum(left_side * right_side) / NPARAM

    decayed = jnp.exp(-jnp.abs(apart))
    curvature = decayed / ((1.0 + decayed) * (1.0 + decayed)) / (16 // 2)
    start_scale = lax.rsqrt(start_square + LANCZOS_EPS)
    first_square = start_square * start_scale * start_scale
    along_one = along * start_scale
    pull_one = curvature * along_one
    alpha_one = inner(pull_one, along_one)
    gram_pull = gram_times(pull_one)
    beta_one = jnp.sqrt(
        inner(pull_one, gram_pull) - alpha_one * alpha_one * (2.0 - first_square) + LANCZOS_EPS
    )
    along_two = (gram_pull - alpha_one * along_one) / beta_one
    pull_two = curvature * along_two
    first_second = alpha_one * (1.0 - first_square) / beta_one
    alpha_two = inner(pull_two, along_two) - beta_one * first_second
    mixed = pull_two - (alpha_two / beta_one) * pull_one
    first_part = alpha_two * alpha_one / beta_one - beta_one
    beta_two = jnp.sqrt(
        inner(mixed, gram_times(mixed))
        + 2.0 * first_part * inner(mixed, along_one)
        + first_part * first_part * first_square
        + LANCZOS_EPS
    )
    part_ref[...] = jnp.broadcast_to(first_part * start_scale / beta_two, part_ref.shape)
    across = row_sum(pairs_ref[...] * (mixed / beta_two))
    jac = jac_ref[...]
    rows = jac.shape[0]
    parts = rounded_parts(jnp.broadcast_to(across[:, :rows], (8, rows)), 3)
    result = sum(dot_halved(part, jac, 1, 0) for part in parts)[:1]
    spare = jnp.zeros((6, 128), jnp.float32)

    def chunks(start, count, size):
        return [result[:, start + size * step : start + size * (step + 1)] for step in range(count)]

    main = jnp.concatenate(chunks(0, 8, LANES), 0)
    middle = jnp.concatenate(chunks(8 * LANES, 8, 128), 0)
    last = jnp.concatenate(chunks(10 * LANES, 2, 128) + [spare], 0)
    result_ref[...] = jnp.concatenate([main, middle, last], 1).astype(jnp.bfloat16)


def assemble_body(
    part_ref,
    own_ref,
    other_ref,
    a_ref,
    bq_ref,
    bkv_ref,
    ao_ref,
    bo_ref,
    out_a_ref,
    out_bq_ref,
    out_bkv_ref,
    out_ao_ref,
    out_bo_ref,
):
    step = pl.program_id(0)
    part = part_ref[0, 0]

    def one_hot(size, first, second):
        row = lax.broadcasted_iota(jnp.int32, (size, size), 0)
        lane = lax.broadcasted_iota(jnp.int32, (size, size), 1)
        wanted = (row % second) * first + row // second
        return jnp.where(lane == wanted, 1.0, 0.0).astype(jnp.bfloat16)

    row = lax.broadcasted_iota(jnp.int32, (64, 64), 0)
    lane = lax.broadcasted_iota(jnp.int32, (64, 64), 1)
    wanted = (row % 8) * 8 + ((row % 16) // 8) * 4 + row // 16
    moved = jnp.where(lane == wanted, 1.0, 0.0).astype(jnp.bfloat16)

    mine = lax.axis_index("dp").astype(jnp.int32) % 2

    def pick(core, spot, lanes):
        return jnp.where(
            mine == core, own_ref[spot, :, lanes], other_ref[spot, :, lanes]
        )

    for half in range(4):
        spot = pl.ds(pl.multiple_of(16 * step + 8 * (half // 2), 8), 8)
        block = pick(half % 2, spot, slice(0, LANES)).reshape(64, LANES)
        placed = dot_halved(moved, block, 1, 0).reshape(4, 16, LANES)
        lanes = slice(half * LANES, (half + 1) * LANES)
        out_a_ref[:, :, lanes] = placed[:3] + part * a_ref[:, :, lanes]
        out_bo_ref[:, lanes] = placed[3] + part * bo_ref[:, lanes]
    turned = one_hot(128, 8, 16)
    for sub in range(2):
        block = jnp.concatenate(
            [
                pick(at % 2, 8 * (at // 2) + 2 * step + sub, slice(LANES, None))
                for at in range(16)
            ],
            0,
        )
        placed = dot_halved(turned, block, 1, 0)
        for chunk in range(4):
            lanes = slice(sub * LANES + chunk * 128, sub * LANES + (chunk + 1) * 128)
            rows = slice(16 * chunk, 16 * chunk + 16)
            out_bq_ref[:, lanes] = placed[rows, :128] + part * bq_ref[:, lanes]
            rows = slice(64 + 16 * chunk, 80 + 16 * chunk)
            out_ao_ref[:, lanes] = placed[rows, :128] + part * ao_ref[:, lanes]
        lanes = slice(sub * HEAD_SIZE, (sub + 1) * HEAD_SIZE)
        out_bkv_ref[0, :, lanes] = placed[:16, 128:] + part * bkv_ref[0, :, lanes]
        out_bkv_ref[1, :, lanes] = placed[16:32, 128:] + part * bkv_ref[1, :, lanes]


def whole(count):
    return [pl.BlockSpec(memory_space=pltpu.VMEM)] * count


def product(left, right, right_dim):
    left_both = jnp.concatenate(rounded_parts(left, 2), 1)
    upper, lower = rounded_parts(right, 2)
    if right_dim == 0:
        rows = jnp.concatenate([upper, lower], 1)
        both = dot_halved(left_both, jnp.concatenate([rows, rows], 0), 1, 0)
    else:
        rows = jnp.concatenate([upper, lower], 0)
        both = dot_halved(left_both, jnp.concatenate([rows, rows], 1), 1, 1)
    size = right.shape[1 - right_dim]
    return both[:, :size] + both[:, size:]


def tall(parts):
    return jnp.concatenate(parts, 0)


def flat(parts):
    return jnp.concatenate(parts, 1)


def corners(both, rows, lanes):
    upper = both[:rows] + both[rows:]
    return upper[:, :lanes] + upper[:, lanes:]


def stack(rows):
    return tall([rows[:, at : at + 128] for at in range(0, rows.shape[1], 128)])


def unstack(rows):
    return flat([rows[at : at + 128] for at in range(0, rows.shape[0], 128)])


def place_shards(whole_ref, shards, semaphores):
    spots = shard_spots()
    half = whole_ref.shape[1] // 2
    copies = []
    for at, shard in enumerate(shards):
        spot = at if at < 6 else 6 + (at - 6) // 2
        rows = pl.ds(pl.multiple_of(spots[spot] * 16, 16), 16)
        if at < 6:
            target = whole_ref.at[rows, :]
        else:
            target = whole_ref.at[rows, pl.ds((at % 2) * half, half)]
        copies.append(pltpu.make_async_copy(shard, target, semaphores.at[at]))
    for copy in copies:
        copy.start()
    return copies


def launch(pairs, semaphores, first):
    copies = prepared(pairs, semaphores, first)
    begin(copies)
    return copies


def finish(copies):
    for copy in copies:
        copy.wait()


def prepared(pairs, semaphores, first):
    return [
        pltpu.make_async_copy(source, target, semaphores.at[first + at])
        for at, (source, target) in enumerate(pairs)
    ]


def begin(copies):
    for copy in copies:
        copy.start()


def span_of(step):
    if isinstance(step, int):
        return pl.ds(step * CHUNK, CHUNK)
    return pl.ds(pl.multiple_of(step * CHUNK, CHUNK), CHUNK)


ANYWHERE = pl.BlockSpec(memory_space=pl.ANY)
LARGE = 60 * 2**20


def gather_by_relays(block):
    half = block.shape[1] // 2

    def permute(array, y_step, z_step):
        pairs = [
            (at, ((at // 4 + y_step) % 2) * 4 + (at % 4 + z_step) % 4) for at in range(8)
        ]
        return lax.ppermute(array, "tensor", pairs)

    across = permute(block, 1, 0)
    below = permute(block, 0, 1)
    above = permute(block, 0, 3)
    across_below = permute(across, 0, 1)
    across_above = permute(across, 0, 3)
    far = [permute(below[:, :half], 0, 1), permute(above[:, half:], 0, 3)]
    across_far = [
        permute(across_below[:, :half], 0, 1),
        permute(across_above[:, half:], 0, 3),
    ]
    return [block, across, below, above, across_below, across_above] + far + across_far


def shard_spots():
    rank = lax.axis_index("tensor").astype(jnp.int32)
    y, z = rank // 4 * 4, rank % 4
    other = 4 - y
    return [
        y + z,
        other + z,
        y + (z + 3) % 4,
        y + (z + 1) % 4,
        other + (z + 3) % 4,
        other + (z + 1) % 4,
        y + (z + 2) % 4,
        other + (z + 2) % 4,
    ]


def small_pairs(down_hbm, up_query_hbm, up_kv_hbm, small_ref):
    return [
        (down_hbm, small_ref.at[:, 0:512]),
        (up_query_hbm, small_ref.at[:, 512:1024]),
        (up_kv_hbm.at[0], small_ref.at[:, 1024:1152]),
        (up_kv_hbm.at[1], small_ref.at[:, 1152:1280]),
    ]


CHUNK = 2048
STATE_ROWS = 2368


def forward_body(
    shard_0,
    shard_1,
    shard_2,
    shard_3,
    shard_4,
    shard_5,
    shard_6,
    shard_7,
    shard_8,
    shard_9,
    query_weight_hbm,
    kv_weight_hbm,
    down_hbm,
    output_weight_hbm,
    up_output_hbm,
    small_down_hbm,
    small_query_hbm,
    small_kv_hbm,
    tokens_hbm,
    out_hbm,
    state_hbm,
    tokens_ref,
    query_weight_ref,
    kv_weight_ref,
    down_ref,
    output_weight_ref,
    up_output_ref,
    small_ref,
    out_ref,
    state_ref,
    query_sum,
    kv_sum,
    low_sum,
    semaphores,
):
    shards = [
        shard_0,
        shard_1,
        shard_2,
        shard_3,
        shard_4,
        shard_5,
        shard_6,
        shard_7,
        shard_8,
        shard_9,
    ]
    placed = place_shards(tokens_ref, shards, semaphores)
    count = tokens_ref.shape[1] // CHUNK

    def early(step):
        span = span_of(step)
        pairs = [
            (query_weight_hbm.at[span, :], query_weight_ref.at[span, :]),
            (kv_weight_hbm.at[:, span, :], kv_weight_ref.at[:, span, :]),
            (down_hbm.at[:, span], down_ref.at[:, span]),
        ]
        return prepared(pairs, semaphores, 10 + 3 * step)

    def late(step):
        span = span_of(step)
        pairs = [
            (output_weight_hbm.at[:, span], output_weight_ref.at[:, span]),
            (up_output_hbm.at[:, span], up_output_ref.at[:, span]),
        ]
        return prepared(pairs, semaphores, 10 + 3 * count + 2 * step)

    def departing(step):
        span = span_of(step)
        pairs = [(out_ref.at[:, :, span], out_hbm.at[:, :, span])]
        return prepared(pairs, semaphores, 10 + 5 * count + step)

    for step in range(count):
        begin(early(step))
    pairs = small_pairs(small_down_hbm, small_query_hbm, small_kv_hbm, small_ref)
    small_copy = launch(pairs, semaphores, 12 + 6 * count)
    finish(placed)
    leaving = launch([(tokens_ref, tokens_hbm)], semaphores, 10 + 6 * count)
    query_sum[...] = jnp.zeros(query_sum.shape, jnp.float32)
    kv_sum[...] = jnp.zeros(kv_sum.shape, jnp.float32)
    low_sum[...] = jnp.zeros(low_sum.shape, jnp.float32)

    def project(step, _):
        finish(early(step))
        begin(late(step))
        span = span_of(step)
        tokens = tokens_ref[:, span]
        query_sum[...] += dot_halved(tokens, query_weight_ref[span, :], 1, 0)
        kv_sum[...] += dot_halved(
            tokens, flat([kv_weight_ref[0, span, :], kv_weight_ref[1, span, :]]), 1, 0
        )
        low_sum[:48] += dot_halved(down_ref[:, span], tokens, 1, 1)
        return 0

    lax.fori_loop(0, count, project, 0)
    finish(small_copy)
    low_turned = low_sum[...]
    low = low_turned.T
    root = 1.0 / math.sqrt(HEAD_SIZE)

    def adapted(total, piece, up):
        parts = rounded_parts(low[:, 16 * piece : 16 * piece + 16], 2)
        return total + ADAPTER_SCALE * dot_halved(flat(parts), tall([up, up]), 1, 0)

    query = stack(adapted(query_sum[...], 0, small_ref[:, 512:1024]))
    keys = adapted(kv_sum[:, :128], 1, small_ref[:, 1024:1152])
    values = adapted(kv_sum[:, 128:], 2, small_ref[:, 1152:])
    capped = jnp.tanh(product(query, keys, 1) * (root / SCORE_CAP))
    row = lax.broadcasted_iota(jnp.int32, (512, 128), 0) % 128
    lane = lax.broadcasted_iota(jnp.int32, (512, 128), 1)
    weights = jnp.where(row >= lane, jnp.exp(SCORE_CAP * capped), 0.0)
    probs = weights / lane_sum(weights)
    context_rows = product(probs, values, 0)
    context = unstack(context_rows)
    low_pair = dot_halved(small_ref[:, :512], tall(rounded_parts(context, 2)), 1, 1)
    context_low = ADAPTER_SCALE * (low_pair[:, :128] + low_pair[:, 128:])
    state_ref[0:512] = query
    state_ref[512:1024] = context_rows
    state_ref[1024:1536] = probs
    state_ref[1536:2048] = capped
    state_ref[2048:2176] = keys
    state_ref[2176:2304] = values
    state_ref[2304:2352] = low_turned[:48]
    state_ref[2352:2368] = context_low
    halved = context.astype(jnp.bfloat16)
    turned = tall([context_low, jnp.zeros((112, 128), jnp.float32)]).T[:, :16]
    halved_low = flat(rounded_parts(turned, 2))
    leaving += launch([(state_ref, state_hbm)], semaphores, 11 + 6 * count)

    def write(step, _):
        finish(late(step))
        span = span_of(step)
        up = up_output_ref[:, span]
        terms = dot_halved(halved, output_weight_ref[:, span], 1, 0) + dot_halved(
            halved_low, tall([up, up]), 1, 0
        )
        out_ref[:, :, span] = terms.astype(jnp.bfloat16).reshape(8, 16, CHUNK)
        begin(departing(step))
        return 0

    lax.fori_loop(0, count, write, 0)
    for step in range(count):
        finish(departing(step))
    finish(leaving)


def forward(
    shards, query_weight, key_value_weight, down_rows, output_weight, up_output, *adapters
):
    width = shards[0].shape[1]
    query_cols = query_weight.shape[1]
    weights = (query_weight, key_value_weight, down_rows, output_weight, up_output)
    arrays = (*weights, *adapters)
    small = jax.ShapeDtypeStruct((16, 1280), jnp.bfloat16)
    results = [
        jax.ShapeDtypeStruct((128, width), jnp.bfloat16),
        jax.ShapeDtypeStruct((8, 16, width), jnp.bfloat16),
        jax.ShapeDtypeStruct((STATE_ROWS, 128), jnp.float32),
    ]
    scratch = [results[0], *weights, small, results[1], results[2]]
    return pl.pallas_call(
        forward_body,
        in_specs=[ANYWHERE] * (len(shards) + len(arrays)),
        out_specs=[ANYWHERE] * 3,
        out_shape=results,
        scratch_shapes=[pltpu.VMEM(array.shape, array.dtype) for array in scratch]
        + [
            pltpu.VMEM((128, query_cols), jnp.float32),
            pltpu.VMEM((128, 256), jnp.float32),
            pltpu.VMEM((128, 128), jnp.float32),
            pltpu.SemaphoreType.DMA((16 + 6 * (width // CHUNK),)),
        ],
        compiler_params=pltpu.CompilerParams(vmem_limit_bytes=LARGE),
        name="forward",
    )(*shards, *arrays)


def cotangents_body(
    lens_ref,
    shard_0,
    shard_1,
    shard_2,
    shard_3,
    shard_4,
    shard_5,
    shard_6,
    shard_7,
    shard_8,
    shard_9,
    weight_hbm,
    side_hbm,
    state_hbm,
    small_down_hbm,
    small_query_hbm,
    small_kv_hbm,
    resid_hbm,
    factors_ref,
    narrow_ref,
    scalars_ref,
    resid_ref,
    weight_ref,
    side_ref,
    state_ref,
    small_ref,
    through_ref,
    slow_ref,
    square_ref,
    semaphores,
):
    shards = [
        shard_0,
        shard_1,
        shard_2,
        shard_3,
        shard_4,
        shard_5,
        shard_6,
        shard_7,
        shard_8,
        shard_9,
    ]
    placed = place_shards(resid_ref, shards, semaphores)
    count = resid_ref.shape[1] // CHUNK

    def early(step):
        span = span_of(step)
        pairs = [
            (weight_hbm.at[:, span], weight_ref.at[:, span]),
            (side_hbm.at[:, span], side_ref.at[:, span]),
        ]
        return prepared(pairs, semaphores, 10 + 2 * step)

    for step in range(count):
        begin(early(step))
    first = 10 + 2 * count
    pairs = small_pairs(small_down_hbm, small_query_hbm, small_kv_hbm, small_ref)
    others = launch([(state_hbm, state_ref)] + pairs, semaphores, first)
    slow_ref[...] = jnp.zeros(slow_ref.shape, jnp.float32)
    through_ref[...] = jnp.zeros(through_ref.shape, jnp.float32)
    square_ref[...] = jnp.zeros(square_ref.shape, jnp.float32)
    narrow_ref[...] = jnp.zeros(narrow_ref.shape, jnp.float32)
    width = resid_ref.shape[1]
    finish(placed)
    leaving = launch([(resid_ref, resid_hbm)], semaphores, first + 5)

    def project(step, _):
        finish(early(step))
        span = span_of(step)
        chunk = resid_ref[:, span]
        side = side_ref[:, span]
        left = tall([chunk, side[16:]])
        through_ref[...] += dot_halved(left, weight_ref[:, span], 1, 1)
        slow_ref[:144, :32] += dot_halved(left, side, 1, 1)
        wide = chunk.astype(jnp.float32)
        square = jnp.zeros((128, 128), jnp.float32)
        for lanes in range(0, CHUNK, 128):
            square = square + wide[:, lanes : lanes + 128] * wide[:, lanes : lanes + 128]
        square_ref[...] += square
        return 0

    lax.fori_loop(0, count, project, 0)
    finish(others)
    finish_cotangents(
        lens_ref,
        width,
        state_ref,
        small_ref,
        factors_ref,
        narrow_ref,
        scalars_ref,
        through_ref,
        slow_ref,
        square_ref,
    )
    finish(leaving)


def finish_cotangents(
    lens_ref,
    width,
    state_ref,
    small_ref,
    factors_ref,
    narrow_ref,
    scalars_ref,
    through_ref,
    slow_ref,
    square_ref,
):
    if True:
        length_own = lens_ref[0]
        root = 1.0 / math.sqrt(HEAD_SIZE)
        slow = slow_ref[...]
        slow_turned = slow.T
        square = square_ref[...]
        inverse = lax.rsqrt(lane_sum(square) / width + NORM_EPS)
        inverse_turned = lax.rsqrt(row_sum(square.T) / width + NORM_EPS)
        each = 1.0 / jnp.broadcast_to(length_own, (1, 1)).astype(jnp.float32)
        share = jnp.where(
            lax.broadcasted_iota(jnp.int32, (128, 1), 0) < length_own, each, 0.0
        )
        share_turned = jnp.where(
            lax.broadcasted_iota(jnp.int32, (1, 128), 1) < length_own, each, 0.0
        )
        logits = inverse * slow[:128, 16:32]
        lead = share * inverse
        pulled = lead * inverse * logits / width
        lead_turned = share_turned * inverse_turned
        pulled_turned = (
            lead_turned * inverse_turned * inverse_turned * slow_turned[16:32, :128] / width
        )
        low_turned = slow_turned[:16, :128]
        scalars_ref[:8] = jnp.zeros((8, 128), jnp.float32)
        scalars_ref[:1, :16] = row_sum(share * logits)
        down = small_ref[:, :512]
        through = through_ref[...] + ADAPTER_SCALE * dot_halved(
            flat(rounded_parts(slow[:144, :16], 2)), tall([down, down]), 1, 0
        )
        context_rows = state_ref[512:1024]
        context = unstack(context_rows)
        probs = state_ref[1024:1536]
        capped = state_ref[1536:2048]
        slope = probs * (1.0 - capped * capped) * root
        probs_turned = tall(rounded_parts(probs.T, 2))
        query_turned = tall(rounded_parts(state_ref[0:512].T, 2))
        keys = state_ref[2048:2176]
        values = state_ref[2176:2304]
        low = [
            tall(rounded_parts(state_ref[2304 + 16 * at : 2320 + 16 * at], 2)) for at in range(3)
        ]
        up_query = small_ref[:, 512:1024]
        up_keys = small_ref[:, 1024:1152]
        up_values = small_ref[:, 1152:]
        context_low = state_ref[2352:2368]
        through_ref[...] = through
        through_tokens = through[:128]
        heads_low = slow_turned[:16, 128:]
        lane_pulled = lax.broadcasted_iota(jnp.int32, pulled.shape, 1)
        lane_low = lax.broadcasted_iota(jnp.int32, heads_low.shape, 1)
        row_pulled = lax.broadcasted_iota(jnp.int32, pulled_turned.shape, 0)

        def objective(obj, _):
            pulled_own = lane_sum(jnp.where(lane_pulled == obj, pulled, 0.0))
            lead_row = through_ref[pl.ds(128 + obj, 1), :]
            cot = stack(lead * lead_row - pulled_own * through_tokens)
            cot_prob = product(cot, values, 1)
            cot_score = slope * (cot_prob - lane_sum(cot * context_rows))
            cot_query = unstack(product(cot_score, keys, 0))
            cot_keys = corners(
                dot_halved(query_turned, flat(rounded_parts(cot_score, 2)), 1, 0), 128, 128
            )
            cot_values = corners(
                dot_halved(probs_turned, flat(rounded_parts(cot, 2)), 1, 0), 128, 128
            )
            query_parts = rounded_parts(cot_query, 2)
            keys_parts = rounded_parts(cot_keys, 2)
            values_parts = rounded_parts(cot_values, 2)
            factor_query = dot_halved(up_query, tall(query_parts), 1, 1)
            factor_keys = dot_halved(up_keys, flat(keys_parts), 1, 0)
            factor_values = dot_halved(up_values, tall(values_parts), 1, 1)
            rows = [
                ADAPTER_SCALE * (factor[:, :128] + factor[:, 128:])
                for factor in (factor_query, factor_keys, factor_values)
            ] + [context_low]
            for piece in range(4):
                for half in range(2):
                    factors_ref[pl.ds(20 * half + 5 * piece + obj, 8, stride=40), :] = rows[
                        piece
                    ][8 * half : 8 * half + 8]
            jac_query = corners(dot_halved(low[0], flat(query_parts), 1, 0), 16, 512)
            jac_keys = corners(dot_halved(low[1], tall(keys_parts), 1, 1), 16, 128)
            jac_values = corners(dot_halved(low[2], flat(values_parts), 1, 0), 16, 128)
            pulled_row = row_sum(jnp.where(row_pulled == obj, pulled_turned, 0.0))
            head_low = lane_sum(jnp.where(lane_low == obj, heads_low, 0.0))
            jac_down = product(head_low * lead_turned - pulled_row * low_turned, context, 0)
            blocks = [jac_query[:, at : at + 128] for at in range(0, 512, 128)]
            blocks += [jac_down[:, at : at + 128] for at in range(0, 512, 128)]
            spots = [(0, 0), (0, 1), (0, 2), (0, 3), (5, 0), (5, 1), (5, 2), (5, 3)]
            spots += [(10, 0), (10, 1)]
            for (row, tile), block in zip(spots, blocks + [jac_keys, jac_values]):
                for half in range(2):
                    narrow_ref[tile, pl.ds(128 * half + row + obj, 8, stride=16), :] = (
                        ADAPTER_SCALE * block[8 * half : 8 * half + 8]
                    )
            return 0

        lax.fori_loop(0, OBJ, objective, 0, unroll=True)
        blank = jnp.zeros((15, 128), jnp.float32)
        scalars_ref[8:48] = jnp.concatenate([blank, pulled_turned[:5]] * 2, 0)
        scalars_ref[48:] = jnp.broadcast_to(lead_turned, (40, 128))


def cotangents(lens, shards, output_weight, side, state, *adapters):
    width = shards[0].shape[1]
    query_cols = output_weight.shape[0]
    arrays = (output_weight, side, state, *adapters)
    small = jax.ShapeDtypeStruct((16, 1280), jnp.bfloat16)
    scratch = [output_weight, side, state, small]
    results = [
        jax.ShapeDtypeStruct((128, width), jnp.bfloat16),
        jax.ShapeDtypeStruct((320, 128), jnp.float32),
        jax.ShapeDtypeStruct((4, 256, 128), jnp.float32),
        jax.ShapeDtypeStruct((88, 128), jnp.float32),
    ]
    return pl.pallas_call(
        cotangents_body,
        in_specs=[pl.BlockSpec(memory_space=pltpu.SMEM)]
        + [ANYWHERE] * (len(shards) + len(arrays)),
        out_specs=[ANYWHERE] + whole(3),
        out_shape=results,
        scratch_shapes=[pltpu.VMEM(array.shape, array.dtype) for array in (results[0], *scratch)]
        + [
            pltpu.VMEM((144, query_cols), jnp.float32),
            pltpu.VMEM((256, 128), jnp.float32),
            pltpu.VMEM((128, 128), jnp.float32),
            pltpu.SemaphoreType.DMA((16 + 2 * (width // CHUNK),)),
        ],
        compiler_params=pltpu.CompilerParams(vmem_limit_bytes=LARGE),
        name="cotangents",
    )(lens, *shards, *arrays)


def jacobian_body(
    factors_hbm,
    tokens_hbm,
    resid_hbm,
    heads_hbm,
    scalars_hbm,
    narrow_hbm,
    payload_hbm,
    factors_ref,
    tokens_ref,
    resid_ref,
    heads_ref,
    scalars_ref,
    narrow_ref,
    payload_ref,
    semaphores,
):
    early = launch([(factors_hbm, factors_ref), (scalars_hbm, scalars_ref)], semaphores, 0)
    count = tokens_ref.shape[1] // CHUNK
    per_step = CHUNK // LANES

    def arriving(step):
        span = span_of(step)
        pairs = [
            (tokens_hbm.at[:, span], tokens_ref.at[:, span]),
            (resid_hbm.at[:, span], resid_ref.at[:, span]),
            (heads_hbm.at[:, span], heads_ref.at[:, span]),
        ]
        return prepared(pairs, semaphores, 3 + 3 * step)

    def departing(step):
        groups = pl.ds(step * per_step, per_step)
        pairs = [(payload_ref.at[groups], payload_hbm.at[groups])]
        return prepared(pairs, semaphores, 3 + 3 * count + step)

    begin(arriving(0))
    early += launch([(narrow_hbm, narrow_ref)], semaphores, 2)
    for step in range(1, count):
        begin(arriving(step))
    finish(early)
    factors = jnp.sum(factors_ref[...], axis=0)
    row = lax.broadcasted_iota(jnp.int32, (40, 1), 0) % 20
    last = row >= 15
    left = flat(
        [jnp.where(last, 0.0, factors), jnp.where(last, -factors * scalars_ref[8:48], 0.0)]
    )
    lead = lane_sum(factors * scalars_ref[48:])

    def both(rows):
        upper = rows.astype(jnp.bfloat16).astype(jnp.float32)
        return tall([upper, rows - upper]).astype(jnp.bfloat16)

    left = both(left)

    def place(step, _):
        finish(arriving(step))
        span = span_of(step)
        right = tall([tokens_ref[:, span], resid_ref[:, span]])
        pair = dot_halved(left, right, 1, 0)
        rows = pair[:40] + pair[40:] + lead * heads_ref[:40, span].astype(jnp.float32)
        for inner in range(per_step):
            group = step * per_step + inner
            below = flat(
                [
                    narrow_ref[tile, pl.ds(pl.multiple_of(group * 16, 16), 16), :]
                    for tile in range(4)
                ]
            )
            block = tall([rows[:, inner * LANES : (inner + 1) * LANES], below])
            payload_ref[group] = block.astype(jnp.bfloat16)
        begin(departing(step))
        return 0

    lax.fori_loop(0, count, place, 0)
    for step in range(count):
        finish(departing(step))


def jacobian(*arrays):
    result = jax.ShapeDtypeStruct((16, PIECE_ROWS, LANES), jnp.bfloat16)
    steps = arrays[1].shape[1] // CHUNK
    return pl.pallas_call(
        jacobian_body,
        in_specs=[ANYWHERE] * len(arrays),
        out_specs=ANYWHERE,
        out_shape=result,
        scratch_shapes=[pltpu.VMEM(array.shape, array.dtype) for array in (*arrays, result)]
        + [pltpu.SemaphoreType.DMA((3 + 4 * steps,))],
        compiler_params=pltpu.CompilerParams(vmem_limit_bytes=LARGE),
        name="jacobian",
    )(*arrays)


def assemble(part, own, other, *shapes):
    steps = 4
    blocks = [
        pl.BlockSpec((3, 16, 4 * LANES), lambda step: (0, 0, step)),
        pl.BlockSpec((16, 2 * LANES), lambda step: (0, step)),
        pl.BlockSpec((2, 16, 2 * HEAD_SIZE), lambda step: (0, 0, step)),
        pl.BlockSpec((16, 2 * LANES), lambda step: (0, step)),
        pl.BlockSpec((16, 4 * LANES), lambda step: (0, step)),
    ]
    return pl.pallas_call(
        assemble_body,
        grid=(steps,),
        in_specs=[
            pl.BlockSpec(memory_space=pltpu.SMEM),
            pl.BlockSpec(own.shape, lambda step: (0, 0, 0)),
            pl.BlockSpec(other.shape, lambda step: (0, 0, 0)),
        ]
        + blocks,
        out_specs=blocks,
        out_shape=[jax.ShapeDtypeStruct(shape.shape, jnp.float32) for shape in shapes],
        compiler_params=pltpu.CompilerParams(vmem_limit_bytes=14 * 2**20),
        name="assemble",
    )(part, own, other, *shapes)


def local(
    hidden,
    query_weight,
    key_value_weight,
    output_weight,
    head,
    lens,
    partner,
    adapter_down_qkv,
    adapter_up_query,
    adapter_up_key_value,
    adapter_down_output,
    adapter_up_output,
    initial_down_qkv,
    initial_up_query,
    initial_up_key_value,
    initial_down_output,
    initial_up_output,
):
    _, part_length, width = hidden.shape
    shards = lax.axis_size("tensor")
    groups = lax.axis_size("dp")
    tensor_rank = lax.axis_index("tensor")
    group_rank = lax.axis_index("dp")
    query_cols = query_weight.shape[1]
    length = part_length * shards

    down_rows = jnp.transpose(adapter_down_qkv, (0, 2, 1)).reshape(48, width)
    down_output = adapter_down_output.T
    head_rows = head.T
    side = jnp.concatenate([adapter_up_output, head_rows, jnp.zeros((11, width), head.dtype)], 0)
    heads = jnp.pad(head_rows, ((15, 0), (0, 0)))
    heads = jnp.pad(jnp.concatenate([heads, heads], 0), ((0, 8), (0, 0)))
    adapters = (down_output, adapter_up_query, adapter_up_key_value)
    tokens, out_terms, state = forward(
        gather_by_relays(hidden[0]),
        query_weight,
        key_value_weight,
        down_rows,
        output_weight,
        adapter_up_output,
        *adapters,
    )
    out_pieces = lax.all_to_all(out_terms, "tensor", 0, 0)
    resid_own = hidden[0].astype(jnp.float32) + jnp.sum(out_pieces.astype(jnp.float32), 0)
    resid, factors, narrow, scalars = cotangents(
        lens,
        gather_by_relays(resid_own.astype(jnp.bfloat16)),
        output_weight,
        side,
        state,
        *adapters,
    )
    factors = lax.all_to_all(factors.reshape(shards, 8 * OBJ, length), "tensor", 0, 0)
    payload = jacobian(factors, tokens, resid, heads, scalars, narrow)
    spread = lax.all_to_all(payload, "dp", 0, 0)
    jac = (
        spread[:, : PIECES * OBJ]
        .reshape(groups, PIECES, OBJ, LANES)
        .transpose(0, 2, 1, 3)
        .reshape(groups * OBJ, PIECES * LANES)
    )

    starts = (
        jnp.transpose(initial_down_qkv, (0, 2, 1)),
        initial_up_query,
        initial_up_key_value,
        initial_down_output.T,
        initial_up_output,
    )
    starts = [pltpu.with_memory_space_constraint(start, pltpu.HBM) for start in starts]
    sequences = jnp.arange(groups)
    leads = sequences < partner
    order = jnp.sum((sequences[None, :] < sequences[:, None]) & leads[None, :], 1)
    chosen = (
        leads[None, :] & (order[None, :] == jnp.arange(groups // 2)[:, None])
    ).astype(jnp.float32)
    differences = chosen - jnp.take(chosen, partner, axis=1)
    pairs = (
        differences[:, None, :, None] * jnp.eye(OBJ, dtype=jnp.float32)[None, :, None, :]
    ).reshape(PAIR_ROWS, groups * OBJ)
    pairs = jnp.pad(pairs, ((0, PACK_ROWS - PAIR_ROWS), (0, 128 - groups * OBJ)))
    packed = pl.pallas_call(
        gram_body,
        in_specs=whole(3) + [ANYWHERE] * 5,
        out_specs=pl.BlockSpec(memory_space=pltpu.VMEM),
        out_shape=jax.ShapeDtypeStruct((16, 128), jnp.float32),
        scratch_shapes=[
            pltpu.VMEM((3, 16, LANES), jnp.float32),
            pltpu.VMEM((16, LANES), jnp.float32),
            pltpu.VMEM((2, 16, HEAD_SIZE), jnp.float32),
            pltpu.VMEM((16, LANES), jnp.float32),
            pltpu.VMEM((16, LANES), jnp.float32),
            pltpu.SemaphoreType.DMA((5,)),
        ],
        compiler_params=pltpu.CompilerParams(vmem_limit_bytes=6 * 2**20),
        name="gram",
    )(jac, pairs, scalars[:8], *starts)
    packed = jnp.sum(gather_by_exchange(packed, "dp"), 0)
    packed = gather_by_exchange(packed, "tensor")
    own_result, part = pl.pallas_call(
        lanczos_body,
        in_specs=whole(3),
        out_specs=whole(2),
        out_shape=[
            jax.ShapeDtypeStruct((8, RESULT_LANES), jnp.bfloat16),
            jax.ShapeDtypeStruct((1, 128), jnp.float32),
        ],
        compiler_params=pltpu.CompilerParams(vmem_limit_bytes=6 * 2**20),
        name="lanczos",
    )(packed, pairs, jac)
    half = groups * shards // 2
    same_core = [
        [at for at in range(2 * half) if (at // shards) % 2 == core] for core in range(2)
    ]
    own_half = lax.all_to_all(
        jnp.broadcast_to(own_result[None], (half,) + own_result.shape),
        ("dp", "tensor"),
        0,
        0,
        axis_index_groups=same_core,
    )
    other_half = lax.ppermute(own_half, "dp", [(at, at ^ 1) for at in range(groups)])
    next_a, next_bq, next_bkv, next_ao, next_bo = assemble(part, own_half, other_half, *starts)
    return jnp.transpose(next_a, (0, 2, 1)), next_bq, next_bkv, next_ao.T, next_bo


def solution(mesh):
    in_specs = (
        P("dp", "tensor", None),
        P(None, "tensor"),
        P(None, None, "tensor"),
        P("tensor", None),
        P(),
        P("dp"),
        P(),
        P(),
        P(None, "tensor"),
        P(None, None, "tensor"),
        P("tensor", None),
        P(),
        P(),
        P(),
        P(),
        P(),
        P(),
    )
    out_specs = (P(), P(), P(), P(), P())
    return jax.shard_map(local, mesh=mesh, in_specs=in_specs, out_specs=out_specs, check_vma=False)
```

```python
import math

import jax
import jax.numpy as jnp
from jax import lax
from jax.experimental import pallas as pl
from jax.experimental.pallas import tpu as pltpu
from jax.sharding import PartitionSpec as P

HEAD_SIZE = 128
NPARAM = 688128
ADAPTER_SCALE = 2.0
NORM_EPS = 1e-05
LANCZOS_EPS = 1e-06
SCORE_CAP = 30.0
PRECISE = lax.Precision.HIGHEST
OBJ = 5
PIECES = 11
PIECE_ROWS = 56
LANES = 512


def dot_halved(left_side, right_side, left_dim, right_dim):
    return lax.dot_general(
        left_side,
        right_side,
        (((left_dim,), (right_dim,)), ((), ())),
        preferred_element_type=jnp.float32,
    )


def dot_entire(left_side, right_side, left_dim, right_dim):
    return lax.dot_general(
        left_side,
        right_side,
        (((left_dim,), (right_dim,)), ((), ())),
        precision=PRECISE,
        preferred_element_type=jnp.float32,
    )


def gather_by_exchange(block, axis):
    count = lax.axis_size(axis)
    copies = jnp.broadcast_to(block[None], (count,) + block.shape)
    return lax.all_to_all(copies, axis, 0, 0)


PAIR_ROWS = 40
PACK_ROWS = 48
PACK_LANES = 42
RESULT_LANES = 768


def rounded_parts(entire, count):
    parts = []
    for _ in range(count):
        part = entire.astype(jnp.bfloat16)
        parts.append(part)
        entire = entire - part.astype(jnp.float32)
    return parts


def lane_sum(values):
    return jnp.sum(values, axis=1, keepdims=True)


def row_sum(values):
    return jnp.sum(values, axis=0, keepdims=True)


def gram_body(
    jac_ref,
    pairs_ref,
    rewards_ref,
    a_hbm,
    bq_hbm,
    bkv_hbm,
    ao_hbm,
    bo_hbm,
    packed_ref,
    a_ref,
    bq_ref,
    bkv_ref,
    ao_ref,
    bo_ref,
    semaphores,
):
    group = lax.axis_index("dp").astype(jnp.int32)
    rank = lax.axis_index("tensor").astype(jnp.int32)
    by_group = pl.ds(pl.multiple_of(group * LANES, LANES), LANES)
    by_rank = pl.ds(pl.multiple_of(rank * LANES, LANES), LANES)
    narrow = pl.ds(pl.multiple_of(rank * HEAD_SIZE, HEAD_SIZE), HEAD_SIZE)
    pairs = [
        (a_hbm.at[:, :, by_group], a_ref),
        (bq_hbm.at[:, by_rank], bq_ref),
        (bkv_hbm.at[:, :, narrow], bkv_ref),
        (ao_hbm.at[:, by_rank], ao_ref),
        (bo_hbm.at[:, by_group], bo_ref),
    ]
    copies = launch(pairs, semaphores, 0)
    jac = jac_ref[...]
    pairs = pairs_ref[...]
    rows = jac.shape[0]
    gram = dot_halved(jac, jac, 1, 1)
    finish(copies)
    blocks = []
    for row in (rank, rank + 8):
        blocks += [a_ref[piece, pl.ds(row, 1), :] for piece in range(3)]
        blocks.append(bo_ref[pl.ds(row, 1), :])
    blocks += [bq_ref[pl.ds(group, 1), :], ao_ref[pl.ds(group, 1), :]]
    blocks += [bkv_ref[piece, pl.ds(group, 1), :] for piece in range(2)]
    start = flat(blocks + [jnp.zeros((1, LANES - 2 * HEAD_SIZE), jnp.float32)])
    starts = jnp.concatenate(rounded_parts(start, 3), 0)
    along = lane_sum(dot_halved(jac, starts, 1, 1))
    own_pairs = pairs[:, :rows]
    gram = dot_entire(dot_entire(own_pairs, gram, 1, 0), own_pairs, 1, 1)
    along = dot_entire(own_pairs, jnp.broadcast_to(along, (rows, 128)), 1, 0)
    rewards = pltpu.roll(rewards_ref[...], OBJ * group, axis=1)[:1]
    rewards = jnp.where(rank == 0, rewards, 0.0)
    apart = lane_sum(pairs * rewards)
    square = jnp.sum(start * start)
    lane = lax.broadcasted_iota(jnp.int32, (PACK_ROWS, 128), 1)
    row = lax.broadcasted_iota(jnp.int32, (PACK_ROWS, 128), 0)
    wide = jnp.concatenate([gram, jnp.zeros((PACK_ROWS, 128 - PACK_ROWS), jnp.float32)], 1)
    wide = jnp.where(lane < PAIR_ROWS, wide, 0.0)
    wide = jnp.where(lane == PAIR_ROWS, along, wide)
    wide = jnp.where(lane == PAIR_ROWS + 1, apart, wide)
    wide = jnp.where((row == PAIR_ROWS) & (lane == 0), square, wide)
    packed_ref[...] = (
        wide[:16]
        + pltpu.roll(wide[16:32], PACK_LANES, axis=1)
        + pltpu.roll(wide[32:], 2 * PACK_LANES, axis=1)
    )


def lanczos_body(packed_ref, pairs_ref, jac_ref, result_ref, part_ref):
    packed = jnp.sum(packed_ref[...], axis=0)
    wide = jnp.concatenate(
        [
            packed,
            pltpu.roll(packed, 128 - PACK_LANES, axis=1),
            pltpu.roll(packed, 128 - 2 * PACK_LANES, axis=1),
        ],
        0,
    )
    lane = lax.broadcasted_iota(jnp.int32, (PACK_ROWS, 128), 1)
    row = lax.broadcasted_iota(jnp.int32, (PACK_ROWS, 128), 0)
    inside = row < PAIR_ROWS
    gram = jnp.where(inside & (lane < PAIR_ROWS), wide, 0.0)
    along = lane_sum(jnp.where(inside & (lane == PAIR_ROWS), wide, 0.0))
    apart = lane_sum(jnp.where(inside & (lane == PAIR_ROWS + 1), wide, 0.0))
    picked = jnp.where((row == PAIR_ROWS) & (lane == 0), wide, 0.0)
    start_square = lane_sum(row_sum(picked)) / NPARAM
    diagonal = row == lane

    def gram_times(column):
        across = row_sum(jnp.where(diagonal, column, 0.0))
        return lane_sum(gram * across)

    def inner(left_side, right_side):
        return row_sum(left_side * right_side) / NPARAM

    decayed = jnp.exp(-jnp.abs(apart))
    curvature = decayed / ((1.0 + decayed) * (1.0 + decayed)) / (16 // 2)
    start_scale = lax.rsqrt(start_square + LANCZOS_EPS)
    first_square = start_square * start_scale * start_scale
    along_one = along * start_scale
    pull_one = curvature * along_one
    alpha_one = inner(pull_one, along_one)
    gram_pull = gram_times(pull_one)
    beta_one = jnp.sqrt(
        inner(pull_one, gram_pull) - alpha_one * alpha_one * (2.0 - first_square) + LANCZOS_EPS
    )
    along_two = (gram_pull - alpha_one * along_one) / beta_one
    pull_two = curvature * along_two
    first_second = alpha_one * (1.0 - first_square) / beta_one
    alpha_two = inner(pull_two, along_two) - beta_one * first_second
    mixed = pull_two - (alpha_two / beta_one) * pull_one
    first_part = alpha_two * alpha_one / beta_one - beta_one
    beta_two = jnp.sqrt(
        inner(mixed, gram_times(mixed))
        + 2.0 * first_part * inner(mixed, along_one)
        + first_part * first_part * first_square
        + LANCZOS_EPS
    )
    part_ref[...] = jnp.broadcast_to(first_part * start_scale / beta_two, part_ref.shape)
    across = row_sum(pairs_ref[...] * (mixed / beta_two))
    jac = jac_ref[...]
    rows = jac.shape[0]
    parts = rounded_parts(jnp.broadcast_to(across[:, :rows], (8, rows)), 3)
    result = sum(dot_halved(part, jac, 1, 0) for part in parts)[:1]
    spare = jnp.zeros((6, 128), jnp.float32)

    def chunks(start, count, size):
        return [result[:, start + size * step : start + size * (step + 1)] for step in range(count)]

    main = jnp.concatenate(chunks(0, 8, LANES), 0)
    middle = jnp.concatenate(chunks(8 * LANES, 8, 128), 0)
    last = jnp.concatenate(chunks(10 * LANES, 2, 128) + [spare], 0)
    result_ref[...] = jnp.concatenate([main, middle, last], 1).astype(jnp.bfloat16)


def assemble_body(
    part_ref,
    own_ref,
    other_ref,
    a_ref,
    bq_ref,
    bkv_ref,
    ao_ref,
    bo_ref,
    out_a_ref,
    out_bq_ref,
    out_bkv_ref,
    out_ao_ref,
    out_bo_ref,
):
    step = pl.program_id(0)
    part = part_ref[0, 0]

    def one_hot(size, first, second):
        row = lax.broadcasted_iota(jnp.int32, (size, size), 0)
        lane = lax.broadcasted_iota(jnp.int32, (size, size), 1)
        wanted = (row % second) * first + row // second
        return jnp.where(lane == wanted, 1.0, 0.0).astype(jnp.bfloat16)

    row = lax.broadcasted_iota(jnp.int32, (64, 64), 0)
    lane = lax.broadcasted_iota(jnp.int32, (64, 64), 1)
    wanted = (row % 8) * 8 + ((row % 16) // 8) * 4 + row // 16
    moved = jnp.where(lane == wanted, 1.0, 0.0).astype(jnp.bfloat16)

    mine = lax.axis_index("dp").astype(jnp.int32) % 2

    def pick(core, spot, lanes):
        return jnp.where(
            mine == core, own_ref[spot, :, lanes], other_ref[spot, :, lanes]
        )

    for half in range(4):
        spot = pl.ds(pl.multiple_of(16 * step + 8 * (half // 2), 8), 8)
        block = pick(half % 2, spot, slice(0, LANES)).reshape(64, LANES)
        placed = dot_halved(moved, block, 1, 0).reshape(4, 16, LANES)
        lanes = slice(half * LANES, (half + 1) * LANES)
        out_a_ref[:, :, lanes] = placed[:3] + part * a_ref[:, :, lanes]
        out_bo_ref[:, lanes] = placed[3] + part * bo_ref[:, lanes]
    turned = one_hot(128, 8, 16)
    for sub in range(2):
        block = jnp.concatenate(
            [
                pick(at % 2, 8 * (at // 2) + 2 * step + sub, slice(LANES, None))
                for at in range(16)
            ],
            0,
        )
        placed = dot_halved(turned, block, 1, 0)
        for chunk in range(4):
            lanes = slice(sub * LANES + chunk * 128, sub * LANES + (chunk + 1) * 128)
            rows = slice(16 * chunk, 16 * chunk + 16)
            out_bq_ref[:, lanes] = placed[rows, :128] + part * bq_ref[:, lanes]
            rows = slice(64 + 16 * chunk, 80 + 16 * chunk)
            out_ao_ref[:, lanes] = placed[rows, :128] + part * ao_ref[:, lanes]
        lanes = slice(sub * HEAD_SIZE, (sub + 1) * HEAD_SIZE)
        out_bkv_ref[0, :, lanes] = placed[:16, 128:] + part * bkv_ref[0, :, lanes]
        out_bkv_ref[1, :, lanes] = placed[16:32, 128:] + part * bkv_ref[1, :, lanes]


def whole(count):
    return [pl.BlockSpec(memory_space=pltpu.VMEM)] * count


def product(left, right, right_dim):
    left_both = jnp.concatenate(rounded_parts(left, 2), 1)
    upper, lower = rounded_parts(right, 2)
    if right_dim == 0:
        rows = jnp.concatenate([upper, lower], 1)
        both = dot_halved(left_both, jnp.concatenate([rows, rows], 0), 1, 0)
    else:
        rows = jnp.concatenate([upper, lower], 0)
        both = dot_halved(left_both, jnp.concatenate([rows, rows], 1), 1, 1)
    size = right.shape[1 - right_dim]
    return both[:, :size] + both[:, size:]


def tall(parts):
    return jnp.concatenate(parts, 0)


def flat(parts):
    return jnp.concatenate(parts, 1)


def stack(rows):
    return tall([rows[:, at : at + 128] for at in range(0, rows.shape[1], 128)])


def unstack(rows):
    return flat([rows[at : at + 128] for at in range(0, rows.shape[0], 128)])


def place_shards(whole_ref, shards, semaphores):
    spots = shard_spots()
    half = whole_ref.shape[1] // 2
    copies = []
    for at, shard in enumerate(shards):
        spot = at if at < 6 else 6 + (at - 6) // 2
        rows = pl.ds(pl.multiple_of(spots[spot] * 16, 16), 16)
        if at < 6:
            target = whole_ref.at[rows, :]
        else:
            target = whole_ref.at[rows, pl.ds((at % 2) * half, half)]
        copies.append(pltpu.make_async_copy(shard, target, semaphores.at[at]))
    for copy in copies:
        copy.start()
    return copies


def launch(pairs, semaphores, first):
    copies = prepared(pairs, semaphores, first)
    begin(copies)
    return copies


def finish(copies):
    for copy in copies:
        copy.wait()


def prepared(pairs, semaphores, first):
    return [
        pltpu.make_async_copy(source, target, semaphores.at[first + at])
        for at, (source, target) in enumerate(pairs)
    ]


def begin(copies):
    for copy in copies:
        copy.start()


def span_of(step):
    if isinstance(step, int):
        return pl.ds(step * CHUNK, CHUNK)
    return pl.ds(pl.multiple_of(step * CHUNK, CHUNK), CHUNK)


ANYWHERE = pl.BlockSpec(memory_space=pl.ANY)
LARGE = 60 * 2**20


def gather_by_relays(block):
    half = block.shape[1] // 2

    def permute(array, y_step, z_step):
        pairs = [
            (at, ((at // 4 + y_step) % 2) * 4 + (at % 4 + z_step) % 4) for at in range(8)
        ]
        return lax.ppermute(array, "tensor", pairs)

    across = permute(block, 1, 0)
    below = permute(block, 0, 1)
    above = permute(block, 0, 3)
    across_below = permute(across, 0, 1)
    across_above = permute(across, 0, 3)
    far = [permute(below[:, :half], 0, 1), permute(above[:, half:], 0, 3)]
    across_far = [
        permute(across_below[:, :half], 0, 1),
        permute(across_above[:, half:], 0, 3),
    ]
    return [block, across, below, above, across_below, across_above] + far + across_far


def shard_spots():
    rank = lax.axis_index("tensor").astype(jnp.int32)
    y, z = rank // 4 * 4, rank % 4
    other = 4 - y
    return [
        y + z,
        other + z,
        y + (z + 3) % 4,
        y + (z + 1) % 4,
        other + (z + 3) % 4,
        other + (z + 1) % 4,
        y + (z + 2) % 4,
        other + (z + 2) % 4,
    ]


def small_pairs(down_hbm, up_query_hbm, up_kv_hbm, small_ref):
    return [
        (down_hbm, small_ref.at[:, 0:512]),
        (up_query_hbm, small_ref.at[:, 512:1024]),
        (up_kv_hbm.at[0], small_ref.at[:, 1024:1152]),
        (up_kv_hbm.at[1], small_ref.at[:, 1152:1280]),
    ]


CHUNK = 2048
STATE_ROWS = 2368


def forward_body(
    shard_0,
    shard_1,
    shard_2,
    shard_3,
    shard_4,
    shard_5,
    shard_6,
    shard_7,
    shard_8,
    shard_9,
    query_weight_hbm,
    kv_weight_hbm,
    down_hbm,
    output_weight_hbm,
    up_output_hbm,
    small_down_hbm,
    small_query_hbm,
    small_kv_hbm,
    tokens_hbm,
    out_hbm,
    state_hbm,
    tokens_ref,
    query_weight_ref,
    kv_weight_ref,
    down_ref,
    output_weight_ref,
    up_output_ref,
    small_ref,
    out_ref,
    state_ref,
    query_sum,
    kv_sum,
    low_sum,
    semaphores,
):
    shards = [
        shard_0,
        shard_1,
        shard_2,
        shard_3,
        shard_4,
        shard_5,
        shard_6,
        shard_7,
        shard_8,
        shard_9,
    ]
    placed = place_shards(tokens_ref, shards, semaphores)
    count = tokens_ref.shape[1] // CHUNK

    def early(step):
        span = span_of(step)
        pairs = [
            (query_weight_hbm.at[span, :], query_weight_ref.at[span, :]),
            (kv_weight_hbm.at[:, span, :], kv_weight_ref.at[:, span, :]),
            (down_hbm.at[:, span], down_ref.at[:, span]),
        ]
        return prepared(pairs, semaphores, 10 + 3 * step)

    def late(step):
        span = span_of(step)
        pairs = [
            (output_weight_hbm.at[:, span], output_weight_ref.at[:, span]),
            (up_output_hbm.at[:, span], up_output_ref.at[:, span]),
        ]
        return prepared(pairs, semaphores, 10 + 3 * count + 2 * step)

    def departing(step):
        span = span_of(step)
        pairs = [(out_ref.at[:, :, span], out_hbm.at[:, :, span])]
        return prepared(pairs, semaphores, 10 + 5 * count + step)

    for step in range(count):
        begin(early(step))
    pairs = small_pairs(small_down_hbm, small_query_hbm, small_kv_hbm, small_ref)
    small_copy = launch(pairs, semaphores, 12 + 6 * count)
    finish(placed)
    leaving = launch([(tokens_ref, tokens_hbm)], semaphores, 10 + 6 * count)
    query_sum[...] = jnp.zeros(query_sum.shape, jnp.float32)
    kv_sum[...] = jnp.zeros(kv_sum.shape, jnp.float32)
    low_sum[...] = jnp.zeros(low_sum.shape, jnp.float32)

    def project(step, _):
        finish(early(step))
        begin(late(step))
        span = span_of(step)
        tokens = tokens_ref[:, span]
        query_sum[...] += dot_halved(tokens, query_weight_ref[span, :], 1, 0)
        kv_sum[...] += dot_halved(
            tokens, flat([kv_weight_ref[0, span, :], kv_weight_ref[1, span, :]]), 1, 0
        )
        low_sum[:48] += dot_halved(down_ref[:, span], tokens, 1, 1)
        return 0

    lax.fori_loop(0, count, project, 0)
    finish(small_copy)
    low_turned = low_sum[...]
    low = low_turned.T
    root = 1.0 / math.sqrt(HEAD_SIZE)

    def adapted(total, piece, up):
        parts = rounded_parts(low[:, 16 * piece : 16 * piece + 16], 2)
        return total + ADAPTER_SCALE * dot_halved(flat(parts), tall([up, up]), 1, 0)

    query = stack(adapted(query_sum[...], 0, small_ref[:, 512:1024]))
    keys = adapted(kv_sum[:, :128], 1, small_ref[:, 1024:1152])
    values = adapted(kv_sum[:, 128:], 2, small_ref[:, 1152:])
    capped = jnp.tanh(product(query, keys, 1) * (root / SCORE_CAP))
    row = lax.broadcasted_iota(jnp.int32, (512, 128), 0) % 128
    lane = lax.broadcasted_iota(jnp.int32, (512, 128), 1)
    weights = jnp.where(row >= lane, jnp.exp(SCORE_CAP * capped), 0.0)
    probs = weights / lane_sum(weights)
    context_rows = product(probs, values, 0)
    context = unstack(context_rows)
    low_pair = dot_halved(small_ref[:, :512], tall(rounded_parts(context, 2)), 1, 1)
    context_low = ADAPTER_SCALE * (low_pair[:, :128] + low_pair[:, 128:])
    state_ref[0:512] = query
    state_ref[512:1024] = context_rows
    state_ref[1024:1536] = probs
    state_ref[1536:2048] = capped
    state_ref[2048:2176] = keys
    state_ref[2176:2304] = values
    state_ref[2304:2352] = low_turned[:48]
    state_ref[2352:2368] = context_low
    halved = context.astype(jnp.bfloat16)
    turned = tall([context_low, jnp.zeros((112, 128), jnp.float32)]).T[:, :16]
    halved_low = flat(rounded_parts(turned, 2))
    leaving += launch([(state_ref, state_hbm)], semaphores, 11 + 6 * count)

    def write(step, _):
        finish(late(step))
        span = span_of(step)
        up = up_output_ref[:, span]
        terms = dot_halved(halved, output_weight_ref[:, span], 1, 0) + dot_halved(
            halved_low, tall([up, up]), 1, 0
        )
        out_ref[:, :, span] = terms.astype(jnp.bfloat16).reshape(8, 16, CHUNK)
        begin(departing(step))
        return 0

    lax.fori_loop(0, count, write, 0)
    for step in range(count):
        finish(departing(step))
    finish(leaving)


def forward(
    shards, query_weight, key_value_weight, down_rows, output_weight, up_output, *adapters
):
    width = shards[0].shape[1]
    query_cols = query_weight.shape[1]
    weights = (query_weight, key_value_weight, down_rows, output_weight, up_output)
    arrays = (*weights, *adapters)
    small = jax.ShapeDtypeStruct((16, 1280), jnp.bfloat16)
    results = [
        jax.ShapeDtypeStruct((128, width), jnp.bfloat16),
        jax.ShapeDtypeStruct((8, 16, width), jnp.bfloat16),
        jax.ShapeDtypeStruct((STATE_ROWS, 128), jnp.float32),
    ]
    scratch = [results[0], *weights, small, results[1], results[2]]
    return pl.pallas_call(
        forward_body,
        in_specs=[ANYWHERE] * (len(shards) + len(arrays)),
        out_specs=[ANYWHERE] * 3,
        out_shape=results,
        scratch_shapes=[pltpu.VMEM(array.shape, array.dtype) for array in scratch]
        + [
            pltpu.VMEM((128, query_cols), jnp.float32),
            pltpu.VMEM((128, 256), jnp.float32),
            pltpu.VMEM((128, 128), jnp.float32),
            pltpu.SemaphoreType.DMA((16 + 6 * (width // CHUNK),)),
        ],
        compiler_params=pltpu.CompilerParams(vmem_limit_bytes=LARGE),
        name="forward",
    )(*shards, *arrays)


def cotangents_body(
    lens_ref,
    shard_0,
    shard_1,
    shard_2,
    shard_3,
    shard_4,
    shard_5,
    shard_6,
    shard_7,
    shard_8,
    shard_9,
    weight_hbm,
    side_hbm,
    state_hbm,
    small_down_hbm,
    small_query_hbm,
    small_kv_hbm,
    resid_hbm,
    factors_ref,
    narrow_ref,
    scalars_ref,
    resid_ref,
    weight_ref,
    side_ref,
    state_ref,
    small_ref,
    through_ref,
    slow_ref,
    square_ref,
    semaphores,
):
    shards = [
        shard_0,
        shard_1,
        shard_2,
        shard_3,
        shard_4,
        shard_5,
        shard_6,
        shard_7,
        shard_8,
        shard_9,
    ]
    placed = place_shards(resid_ref, shards, semaphores)
    count = resid_ref.shape[1] // CHUNK

    def early(step):
        span = span_of(step)
        pairs = [
            (weight_hbm.at[:, span], weight_ref.at[:, span]),
            (side_hbm.at[:, span], side_ref.at[:, span]),
        ]
        return prepared(pairs, semaphores, 10 + 2 * step)

    for step in range(count):
        begin(early(step))
    first = 10 + 2 * count
    pairs = small_pairs(small_down_hbm, small_query_hbm, small_kv_hbm, small_ref)
    others = launch([(state_hbm, state_ref)] + pairs, semaphores, first)
    slow_ref[...] = jnp.zeros(slow_ref.shape, jnp.float32)
    through_ref[...] = jnp.zeros(through_ref.shape, jnp.float32)
    square_ref[...] = jnp.zeros(square_ref.shape, jnp.float32)
    narrow_ref[...] = jnp.zeros(narrow_ref.shape, jnp.float32)
    width = resid_ref.shape[1]
    finish(placed)
    leaving = launch([(resid_ref, resid_hbm)], semaphores, first + 5)

    def project(step, _):
        finish(early(step))
        span = span_of(step)
        chunk = resid_ref[:, span]
        side = side_ref[:, span]
        left = tall([chunk, side[16:]])
        through_ref[...] += dot_halved(left, weight_ref[:, span], 1, 1)
        slow_ref[:144, :32] += dot_halved(left, side, 1, 1)
        wide = chunk.astype(jnp.float32)
        square = jnp.zeros((128, 128), jnp.float32)
        for lanes in range(0, CHUNK, 128):
            square = square + wide[:, lanes : lanes + 128] * wide[:, lanes : lanes + 128]
        square_ref[...] += square
        return 0

    lax.fori_loop(0, count, project, 0)
    finish(others)
    finish_cotangents(
        lens_ref,
        width,
        state_ref,
        small_ref,
        factors_ref,
        narrow_ref,
        scalars_ref,
        through_ref,
        slow_ref,
        square_ref,
    )
    finish(leaving)


def finish_cotangents(
    lens_ref,
    width,
    state_ref,
    small_ref,
    factors_ref,
    narrow_ref,
    scalars_ref,
    through_ref,
    slow_ref,
    square_ref,
):
    if True:
        length_own = lens_ref[0]
        root = 1.0 / math.sqrt(HEAD_SIZE)
        slow = slow_ref[...]
        slow_turned = slow.T
        square = square_ref[...]
        inverse = lax.rsqrt(lane_sum(square) / width + NORM_EPS)
        inverse_turned = lax.rsqrt(row_sum(square.T) / width + NORM_EPS)
        each = 1.0 / jnp.broadcast_to(length_own, (1, 1)).astype(jnp.float32)
        share = jnp.where(
            lax.broadcasted_iota(jnp.int32, (128, 1), 0) < length_own, each, 0.0
        )
        share_turned = jnp.where(
            lax.broadcasted_iota(jnp.int32, (1, 128), 1) < length_own, each, 0.0
        )
        logits = inverse * slow[:128, 16:32]
        lead = share * inverse
        pulled = lead * inverse * logits / width
        lead_turned = share_turned * inverse_turned
        pulled_turned = (
            lead_turned * inverse_turned * inverse_turned * slow_turned[16:32, :128] / width
        )
        low_turned = slow_turned[:16, :128]
        scalars_ref[:8] = jnp.zeros((8, 128), jnp.float32)
        scalars_ref[:1, :16] = row_sum(share * logits)
        down = small_ref[:, :512]
        through = through_ref[...] + ADAPTER_SCALE * dot_halved(
            flat(rounded_parts(slow[:144, :16], 2)), tall([down, down]), 1, 0
        )
        query = state_ref[0:512]
        context_rows = state_ref[512:1024]
        probs = state_ref[1024:1536]
        capped = state_ref[1536:2048]
        keys = state_ref[2048:2176]
        values = state_ref[2176:2304]
        low_q = state_ref[2304:2320]
        low_k = state_ref[2320:2336]
        low_v = state_ref[2336:2352]
        context_low = state_ref[2352:2368]
        small = small_ref[:, 512:].astype(jnp.float32)
        up_query, up_keys, up_values = small[:, :512], small[:, 512:640], small[:, 640:]
        objectives = range(OBJ)
        head_spots = range(4)
        across = stack(through[:128])
        heads = stack(through[128:136])
        on_values = product(tall([across, heads]), values, 1)
        heads_on_values = on_values[512:]
        slope = probs * (1.0 - capped * capped) * root
        shared = slope * (on_values[:512] - lane_sum(across * context_rows))
        leading = slope * tall([lead] * 4)
        heads_on_context = product(heads, context_rows, 1)
        query_on_keys = product(stack(up_query), keys, 1)
        keys_on_query = product(up_keys, query, 1)
        padded = tall([across, heads, jnp.zeros((96, 128), jnp.float32)])
        values_on_cot = product(up_values, padded, 1)
        low_on_probs = product(low_v, probs, 1)

        def block(array, head):
            return array[:, 128 * head : 128 * head + 128]

        def row_of(array, row):
            return array[row : row + 1]

        left_values = []
        right_values = []
        for obj in objectives:
            pull = row_of(pulled_turned, obj)
            parts = []
            for head in head_spots:
                spot = 512 + 8 * head + obj
                parts.append(
                    values_on_cot[:, spot : spot + 1] * lead_turned
                    - pull * block(values_on_cot, head)
                )
            left_values.append(flat(parts))
            right_values.append(low_on_probs * flat([pull] * 4))
        factor_values = product(tall(left_values), probs, 0)
        jac_values = -product(tall(right_values), across, 0)
        low_lead = [lane_sum(block(low_on_probs, head) * lead_turned) for head in head_spots]
        factor_query = [0.0] * OBJ
        factor_keys = [0.0] * OBJ
        query_rows = [[] for _ in objectives]
        keys_rows = [[] for _ in objectives]
        for head in head_spots:
            rows = slice(128 * head, 128 * head + 128)
            score_lead, score_shared = leading[rows], shared[rows]
            on_context = block(heads_on_context, head)[8 * head : 8 * head + 8]
            on_value = heads_on_values[8 * head : 8 * head + 8]
            base = tall([low_q, block(keys_on_query, head)])
            first = product(
                tall([base] + [base * row_of(on_context, obj) for obj in objectives]),
                score_lead,
                0,
            )
            second = product(
                tall([base * row_of(pulled_turned, obj) for obj in objectives]), score_shared, 0
            )
            base = tall([query_on_keys[16 * head : 16 * head + 16], low_k])
            third = product(
                tall([base] + [base * row_of(on_value, obj) for obj in objectives]),
                score_lead,
                1,
            )
            fourth = product(base, score_shared, 1)
            for obj in objectives:
                spot = slice(32 + 32 * obj, 64 + 32 * obj)
                by_rows = (
                    first[:32] * row_of(on_value, obj)
                    - first[spot]
                    - second[32 * obj : 32 * obj + 32]
                )
                by_lanes = (
                    third[spot]
                    - row_of(on_context, obj) * third[:32]
                    - row_of(pulled_turned, obj) * fourth
                )
                query_rows[obj].append(by_rows[:16])
                factor_keys[obj] += by_rows[16:]
                factor_query[obj] += by_lanes[:16]
                keys_rows[obj].append(by_lanes[16:])
        jac_query = product(tall([tall(rows) for rows in query_rows]), keys, 0)
        jac_keys = product(tall([flat(rows) for rows in keys_rows]), query, 0)
        cot_low = [
            slow_turned[:16, 128 + obj : 129 + obj] * lead_turned
            - row_of(pulled_turned, obj) * low_turned
            for obj in objectives
        ]
        jac_down = product(tall(cot_low), unstack(context_rows), 0)
        for obj in objectives:
            own = slice(16 * obj, 16 * obj + 16)
            rows = [
                ADAPTER_SCALE * factor_query[obj],
                ADAPTER_SCALE * factor_keys[obj],
                ADAPTER_SCALE * factor_values[own],
                context_low,
            ]
            for piece in range(4):
                for half in range(2):
                    factors_ref[pl.ds(20 * half + 5 * piece + obj, 8, stride=40), :] = rows[
                        piece
                    ][8 * half : 8 * half + 8]
            own_values = jac_values[own]
            for head in head_spots:
                own_values += low_lead[head] * row_of(heads, 8 * head + obj)
            blocks = [
                jac_query[64 * obj + 16 * head : 64 * obj + 16 * head + 16]
                for head in head_spots
            ]
            blocks += [block(jac_down, head)[own] for head in head_spots]
            blocks += [jac_keys[own], own_values]
            spots = [(0, 0), (0, 1), (0, 2), (0, 3), (5, 0), (5, 1), (5, 2), (5, 3)]
            spots += [(10, 0), (10, 1)]
            for (row, tile), part in zip(spots, blocks):
                for half in range(2):
                    narrow_ref[tile, pl.ds(128 * half + row + obj, 8, stride=16), :] = (
                        ADAPTER_SCALE * part[8 * half : 8 * half + 8]
                    )
        blank = jnp.zeros((15, 128), jnp.float32)
        scalars_ref[8:48] = jnp.concatenate([blank, pulled_turned[:5]] * 2, 0)
        scalars_ref[48:] = jnp.broadcast_to(lead_turned, (40, 128))


def cotangents(lens, shards, output_weight, side, state, *adapters):
    width = shards[0].shape[1]
    query_cols = output_weight.shape[0]
    arrays = (output_weight, side, state, *adapters)
    small = jax.ShapeDtypeStruct((16, 1280), jnp.bfloat16)
    scratch = [output_weight, side, state, small]
    results = [
        jax.ShapeDtypeStruct((128, width), jnp.bfloat16),
        jax.ShapeDtypeStruct((320, 128), jnp.float32),
        jax.ShapeDtypeStruct((4, 256, 128), jnp.float32),
        jax.ShapeDtypeStruct((88, 128), jnp.float32),
    ]
    return pl.pallas_call(
        cotangents_body,
        in_specs=[pl.BlockSpec(memory_space=pltpu.SMEM)]
        + [ANYWHERE] * (len(shards) + len(arrays)),
        out_specs=[ANYWHERE] + whole(3),
        out_shape=results,
        scratch_shapes=[pltpu.VMEM(array.shape, array.dtype) for array in (results[0], *scratch)]
        + [
            pltpu.VMEM((144, query_cols), jnp.float32),
            pltpu.VMEM((256, 128), jnp.float32),
            pltpu.VMEM((128, 128), jnp.float32),
            pltpu.SemaphoreType.DMA((16 + 2 * (width // CHUNK),)),
        ],
        compiler_params=pltpu.CompilerParams(vmem_limit_bytes=LARGE),
        name="cotangents",
    )(lens, *shards, *arrays)


def jacobian_body(
    factors_hbm,
    tokens_hbm,
    resid_hbm,
    heads_hbm,
    scalars_hbm,
    narrow_hbm,
    payload_hbm,
    factors_ref,
    tokens_ref,
    resid_ref,
    heads_ref,
    scalars_ref,
    narrow_ref,
    payload_ref,
    semaphores,
):
    early = launch([(factors_hbm, factors_ref), (scalars_hbm, scalars_ref)], semaphores, 0)
    count = tokens_ref.shape[1] // CHUNK
    per_step = CHUNK // LANES

    def arriving(step):
        span = span_of(step)
        pairs = [
            (tokens_hbm.at[:, span], tokens_ref.at[:, span]),
            (resid_hbm.at[:, span], resid_ref.at[:, span]),
            (heads_hbm.at[:, span], heads_ref.at[:, span]),
        ]
        return prepared(pairs, semaphores, 3 + 3 * step)

    def departing(step):
        groups = pl.ds(step * per_step, per_step)
        pairs = [(payload_ref.at[groups], payload_hbm.at[groups])]
        return prepared(pairs, semaphores, 3 + 3 * count + step)

    begin(arriving(0))
    early += launch([(narrow_hbm, narrow_ref)], semaphores, 2)
    for step in range(1, count):
        begin(arriving(step))
    finish(early)
    factors = jnp.sum(factors_ref[...], axis=0)
    row = lax.broadcasted_iota(jnp.int32, (40, 1), 0) % 20
    last = row >= 15
    left = flat(
        [jnp.where(last, 0.0, factors), jnp.where(last, -factors * scalars_ref[8:48], 0.0)]
    )
    lead = lane_sum(factors * scalars_ref[48:])

    def both(rows):
        upper = rows.astype(jnp.bfloat16).astype(jnp.float32)
        return tall([upper, rows - upper]).astype(jnp.bfloat16)

    left = both(left)

    def place(step, _):
        finish(arriving(step))
        span = span_of(step)
        right = tall([tokens_ref[:, span], resid_ref[:, span]])
        pair = dot_halved(left, right, 1, 0)
        rows = pair[:40] + pair[40:] + lead * heads_ref[:40, span].astype(jnp.float32)
        for inner in range(per_step):
            group = step * per_step + inner
            below = flat(
                [
                    narrow_ref[tile, pl.ds(pl.multiple_of(group * 16, 16), 16), :]
                    for tile in range(4)
                ]
            )
            block = tall([rows[:, inner * LANES : (inner + 1) * LANES], below])
            payload_ref[group] = block.astype(jnp.bfloat16)
        begin(departing(step))
        return 0

    lax.fori_loop(0, count, place, 0)
    for step in range(count):
        finish(departing(step))


def jacobian(*arrays):
    result = jax.ShapeDtypeStruct((16, PIECE_ROWS, LANES), jnp.bfloat16)
    steps = arrays[1].shape[1] // CHUNK
    return pl.pallas_call(
        jacobian_body,
        in_specs=[ANYWHERE] * len(arrays),
        out_specs=ANYWHERE,
        out_shape=result,
        scratch_shapes=[pltpu.VMEM(array.shape, array.dtype) for array in (*arrays, result)]
        + [pltpu.SemaphoreType.DMA((3 + 4 * steps,))],
        compiler_params=pltpu.CompilerParams(vmem_limit_bytes=LARGE),
        name="jacobian",
    )(*arrays)


def assemble(part, own, other, *shapes):
    steps = 4
    blocks = [
        pl.BlockSpec((3, 16, 4 * LANES), lambda step: (0, 0, step)),
        pl.BlockSpec((16, 2 * LANES), lambda step: (0, step)),
        pl.BlockSpec((2, 16, 2 * HEAD_SIZE), lambda step: (0, 0, step)),
        pl.BlockSpec((16, 2 * LANES), lambda step: (0, step)),
        pl.BlockSpec((16, 4 * LANES), lambda step: (0, step)),
    ]
    return pl.pallas_call(
        assemble_body,
        grid=(steps,),
        in_specs=[
            pl.BlockSpec(memory_space=pltpu.SMEM),
            pl.BlockSpec(own.shape, lambda step: (0, 0, 0)),
            pl.BlockSpec(other.shape, lambda step: (0, 0, 0)),
        ]
        + blocks,
        out_specs=blocks,
        out_shape=[jax.ShapeDtypeStruct(shape.shape, jnp.float32) for shape in shapes],
        compiler_params=pltpu.CompilerParams(vmem_limit_bytes=14 * 2**20),
        name="assemble",
    )(part, own, other, *shapes)


def local(
    hidden,
    query_weight,
    key_value_weight,
    output_weight,
    head,
    lens,
    partner,
    adapter_down_qkv,
    adapter_up_query,
    adapter_up_key_value,
    adapter_down_output,
    adapter_up_output,
    initial_down_qkv,
    initial_up_query,
    initial_up_key_value,
    initial_down_output,
    initial_up_output,
):
    _, part_length, width = hidden.shape
    shards = lax.axis_size("tensor")
    groups = lax.axis_size("dp")
    tensor_rank = lax.axis_index("tensor")
    group_rank = lax.axis_index("dp")
    query_cols = query_weight.shape[1]
    length = part_length * shards

    down_rows = jnp.transpose(adapter_down_qkv, (0, 2, 1)).reshape(48, width)
    down_output = adapter_down_output.T
    head_rows = head.T
    side = jnp.concatenate([adapter_up_output, head_rows, jnp.zeros((11, width), head.dtype)], 0)
    heads = jnp.pad(head_rows, ((15, 0), (0, 0)))
    heads = jnp.pad(jnp.concatenate([heads, heads], 0), ((0, 8), (0, 0)))
    adapters = (down_output, adapter_up_query, adapter_up_key_value)
    tokens, out_terms, state = forward(
        gather_by_relays(hidden[0]),
        query_weight,
        key_value_weight,
        down_rows,
        output_weight,
        adapter_up_output,
        *adapters,
    )
    out_pieces = lax.all_to_all(out_terms, "tensor", 0, 0)
    resid_own = hidden[0].astype(jnp.float32) + jnp.sum(out_pieces.astype(jnp.float32), 0)
    resid, factors, narrow, scalars = cotangents(
        lens,
        gather_by_relays(resid_own.astype(jnp.bfloat16)),
        output_weight,
        side,
        state,
        *adapters,
    )
    factors = lax.all_to_all(factors.reshape(shards, 8 * OBJ, length), "tensor", 0, 0)
    payload = jacobian(factors, tokens, resid, heads, scalars, narrow)
    spread = lax.all_to_all(payload, "dp", 0, 0)
    jac = (
        spread[:, : PIECES * OBJ]
        .reshape(groups, PIECES, OBJ, LANES)
        .transpose(0, 2, 1, 3)
        .reshape(groups * OBJ, PIECES * LANES)
    )

    starts = (
        jnp.transpose(initial_down_qkv, (0, 2, 1)),
        initial_up_query,
        initial_up_key_value,
        initial_down_output.T,
        initial_up_output,
    )
    starts = [pltpu.with_memory_space_constraint(start, pltpu.HBM) for start in starts]
    sequences = jnp.arange(groups)
    leads = sequences < partner
    order = jnp.sum((sequences[None, :] < sequences[:, None]) & leads[None, :], 1)
    chosen = (
        leads[None, :] & (order[None, :] == jnp.arange(groups // 2)[:, None])
    ).astype(jnp.float32)
    differences = chosen - jnp.take(chosen, partner, axis=1)
    pairs = (
        differences[:, None, :, None] * jnp.eye(OBJ, dtype=jnp.float32)[None, :, None, :]
    ).reshape(PAIR_ROWS, groups * OBJ)
    pairs = jnp.pad(pairs, ((0, PACK_ROWS - PAIR_ROWS), (0, 128 - groups * OBJ)))
    packed = pl.pallas_call(
        gram_body,
        in_specs=whole(3) + [ANYWHERE] * 5,
        out_specs=pl.BlockSpec(memory_space=pltpu.VMEM),
        out_shape=jax.ShapeDtypeStruct((16, 128), jnp.float32),
        scratch_shapes=[
            pltpu.VMEM((3, 16, LANES), jnp.float32),
            pltpu.VMEM((16, LANES), jnp.float32),
            pltpu.VMEM((2, 16, HEAD_SIZE), jnp.float32),
            pltpu.VMEM((16, LANES), jnp.float32),
            pltpu.VMEM((16, LANES), jnp.float32),
            pltpu.SemaphoreType.DMA((5,)),
        ],
        compiler_params=pltpu.CompilerParams(vmem_limit_bytes=6 * 2**20),
        name="gram",
    )(jac, pairs, scalars[:8], *starts)
    packed = jnp.sum(gather_by_exchange(packed, "dp"), 0)
    packed = gather_by_exchange(packed, "tensor")
    own_result, part = pl.pallas_call(
        lanczos_body,
        in_specs=whole(3),
        out_specs=whole(2),
        out_shape=[
            jax.ShapeDtypeStruct((8, RESULT_LANES), jnp.bfloat16),
            jax.ShapeDtypeStruct((1, 128), jnp.float32),
        ],
        compiler_params=pltpu.CompilerParams(vmem_limit_bytes=6 * 2**20),
        name="lanczos",
    )(packed, pairs, jac)
    half = groups * shards // 2
    same_core = [
        [at for at in range(2 * half) if (at // shards) % 2 == core] for core in range(2)
    ]
    own_half = lax.all_to_all(
        jnp.broadcast_to(own_result[None], (half,) + own_result.shape),
        ("dp", "tensor"),
        0,
        0,
        axis_index_groups=same_core,
    )
    other_half = lax.ppermute(own_half, "dp", [(at, at ^ 1) for at in range(groups)])
    next_a, next_bq, next_bkv, next_ao, next_bo = assemble(part, own_half, other_half, *starts)
    return jnp.transpose(next_a, (0, 2, 1)), next_bq, next_bkv, next_ao.T, next_bo


def solution(mesh):
    in_specs = (
        P("dp", "tensor", None),
        P(None, "tensor"),
        P(None, None, "tensor"),
        P("tensor", None),
        P(),
        P("dp"),
        P(),
        P(),
        P(None, "tensor"),
        P(None, None, "tensor"),
        P("tensor", None),
        P(),
        P(),
        P(),
        P(),
        P(),
        P(),
    )
    out_specs = (P(), P(), P(), P(), P())
    return jax.shard_map(local, mesh=mesh, in_specs=in_specs, out_specs=out_specs, check_vma=False)
```

```python
import math

import jax
import jax.numpy as jnp
from jax import lax
from jax.experimental import pallas as pl
from jax.experimental.pallas import tpu as pltpu
from jax.sharding import PartitionSpec as P

HEAD_SIZE = 128
NPARAM = 688128
ADAPTER_SCALE = 2.0
NORM_EPS = 1e-05
LANCZOS_EPS = 1e-06
SCORE_CAP = 30.0
PRECISE = lax.Precision.HIGHEST
OBJ = 5
PIECES = 11
PIECE_ROWS = 56
LANES = 512


def dot_halved(left_side, right_side, left_dim, right_dim):
    return lax.dot_general(
        left_side,
        right_side,
        (((left_dim,), (right_dim,)), ((), ())),
        preferred_element_type=jnp.float32,
    )


def dot_entire(left_side, right_side, left_dim, right_dim):
    return lax.dot_general(
        left_side,
        right_side,
        (((left_dim,), (right_dim,)), ((), ())),
        precision=PRECISE,
        preferred_element_type=jnp.float32,
    )


def gather_by_exchange(block, axis):
    count = lax.axis_size(axis)
    copies = jnp.broadcast_to(block[None], (count,) + block.shape)
    return lax.all_to_all(copies, axis, 0, 0)


PAIR_ROWS = 40
PACK_ROWS = 48
PACK_LANES = 42
RESULT_LANES = 768


def rounded_parts(entire, count):
    parts = []
    for _ in range(count):
        part = entire.astype(jnp.bfloat16)
        parts.append(part)
        entire = entire - part.astype(jnp.float32)
    return parts


def lane_sum(values):
    return jnp.sum(values, axis=1, keepdims=True)


def row_sum(values):
    return jnp.sum(values, axis=0, keepdims=True)


def gram_body(
    jac_ref,
    pairs_ref,
    rewards_ref,
    a_hbm,
    bq_hbm,
    bkv_hbm,
    ao_hbm,
    bo_hbm,
    packed_ref,
    a_ref,
    bq_ref,
    bkv_ref,
    ao_ref,
    bo_ref,
    semaphores,
):
    group = lax.axis_index("dp").astype(jnp.int32)
    rank = lax.axis_index("tensor").astype(jnp.int32)
    by_group = pl.ds(pl.multiple_of(group * LANES, LANES), LANES)
    by_rank = pl.ds(pl.multiple_of(rank * LANES, LANES), LANES)
    narrow = pl.ds(pl.multiple_of(rank * HEAD_SIZE, HEAD_SIZE), HEAD_SIZE)
    pairs = [
        (a_hbm.at[:, :, by_group], a_ref),
        (bq_hbm.at[:, by_rank], bq_ref),
        (bkv_hbm.at[:, :, narrow], bkv_ref),
        (ao_hbm.at[:, by_rank], ao_ref),
        (bo_hbm.at[:, by_group], bo_ref),
    ]
    copies = launch(pairs, semaphores, 0)
    jac = jac_ref[...]
    pairs = pairs_ref[...]
    rows = jac.shape[0]
    gram = dot_halved(jac, jac, 1, 1)
    finish(copies)
    blocks = []
    for row in (rank, rank + 8):
        blocks += [a_ref[piece, pl.ds(row, 1), :] for piece in range(3)]
        blocks.append(bo_ref[pl.ds(row, 1), :])
    blocks += [bq_ref[pl.ds(group, 1), :], ao_ref[pl.ds(group, 1), :]]
    blocks += [bkv_ref[piece, pl.ds(group, 1), :] for piece in range(2)]
    start = flat(blocks + [jnp.zeros((1, LANES - 2 * HEAD_SIZE), jnp.float32)])
    starts = jnp.concatenate(rounded_parts(start, 3), 0)
    along = lane_sum(dot_halved(jac, starts, 1, 1))
    own_pairs = pairs[:, :rows]
    gram = dot_entire(dot_entire(own_pairs, gram, 1, 0), own_pairs, 1, 1)
    along = dot_entire(own_pairs, jnp.broadcast_to(along, (rows, 128)), 1, 0)
    rewards = pltpu.roll(rewards_ref[...], OBJ * group, axis=1)[:1]
    rewards = jnp.where(rank == 0, rewards, 0.0)
    apart = lane_sum(pairs * rewards)
    square = jnp.sum(start * start)
    lane = lax.broadcasted_iota(jnp.int32, (PACK_ROWS, 128), 1)
    row = lax.broadcasted_iota(jnp.int32, (PACK_ROWS, 128), 0)
    wide = jnp.concatenate([gram, jnp.zeros((PACK_ROWS, 128 - PACK_ROWS), jnp.float32)], 1)
    wide = jnp.where(lane < PAIR_ROWS, wide, 0.0)
    wide = jnp.where(lane == PAIR_ROWS, along, wide)
    wide = jnp.where(lane == PAIR_ROWS + 1, apart, wide)
    wide = jnp.where((row == PAIR_ROWS) & (lane == 0), square, wide)
    packed_ref[...] = (
        wide[:16]
        + pltpu.roll(wide[16:32], PACK_LANES, axis=1)
        + pltpu.roll(wide[32:], 2 * PACK_LANES, axis=1)
    )


def lanczos_body(packed_ref, pairs_ref, jac_ref, result_ref, part_ref):
    packed = jnp.sum(packed_ref[...], axis=0)
    wide = jnp.concatenate(
        [
            packed,
            pltpu.roll(packed, 128 - PACK_LANES, axis=1),
            pltpu.roll(packed, 128 - 2 * PACK_LANES, axis=1),
        ],
        0,
    )
    lane = lax.broadcasted_iota(jnp.int32, (PACK_ROWS, 128), 1)
    row = lax.broadcasted_iota(jnp.int32, (PACK_ROWS, 128), 0)
    inside = row < PAIR_ROWS
    gram = jnp.where(inside & (lane < PAIR_ROWS), wide, 0.0)
    along = lane_sum(jnp.where(inside & (lane == PAIR_ROWS), wide, 0.0))
    apart = lane_sum(jnp.where(inside & (lane == PAIR_ROWS + 1), wide, 0.0))
    picked = jnp.where((row == PAIR_ROWS) & (lane == 0), wide, 0.0)
    start_square = lane_sum(row_sum(picked)) / NPARAM
    diagonal = row == lane

    def gram_times(column):
        across = row_sum(jnp.where(diagonal, column, 0.0))
        return lane_sum(gram * across)

    def inner(left_side, right_side):
        return row_sum(left_side * right_side) / NPARAM

    decayed = jnp.exp(-jnp.abs(apart))
    curvature = decayed / ((1.0 + decayed) * (1.0 + decayed)) / (16 // 2)
    start_scale = lax.rsqrt(start_square + LANCZOS_EPS)
    first_square = start_square * start_scale * start_scale
    along_one = along * start_scale
    pull_one = curvature * along_one
    alpha_one = inner(pull_one, along_one)
    gram_pull = gram_times(pull_one)
    beta_one = jnp.sqrt(
        inner(pull_one, gram_pull) - alpha_one * alpha_one * (2.0 - first_square) + LANCZOS_EPS
    )
    along_two = (gram_pull - alpha_one * along_one) / beta_one
    pull_two = curvature * along_two
    first_second = alpha_one * (1.0 - first_square) / beta_one
    alpha_two = inner(pull_two, along_two) - beta_one * first_second
    mixed = pull_two - (alpha_two / beta_one) * pull_one
    first_part = alpha_two * alpha_one / beta_one - beta_one
    beta_two = jnp.sqrt(
        inner(mixed, gram_times(mixed))
        + 2.0 * first_part * inner(mixed, along_one)
        + first_part * first_part * first_square
        + LANCZOS_EPS
    )
    part_ref[...] = jnp.broadcast_to(first_part * start_scale / beta_two, part_ref.shape)
    across = row_sum(pairs_ref[...] * (mixed / beta_two))
    jac = jac_ref[...]
    rows = jac.shape[0]
    parts = rounded_parts(jnp.broadcast_to(across[:, :rows], (8, rows)), 3)
    result = sum(dot_halved(part, jac, 1, 0) for part in parts)[:1]
    spare = jnp.zeros((6, 128), jnp.float32)

    def chunks(start, count, size):
        return [result[:, start + size * step : start + size * (step + 1)] for step in range(count)]

    main = jnp.concatenate(chunks(0, 8, LANES), 0)
    middle = jnp.concatenate(chunks(8 * LANES, 8, 128), 0)
    last = jnp.concatenate(chunks(10 * LANES, 2, 128) + [spare], 0)
    result_ref[...] = jnp.concatenate([main, middle, last], 1).astype(jnp.bfloat16)


def assemble_body(
    part_ref,
    own_ref,
    other_ref,
    a_ref,
    bq_ref,
    bkv_ref,
    ao_ref,
    bo_ref,
    out_a_ref,
    out_bq_ref,
    out_bkv_ref,
    out_ao_ref,
    out_bo_ref,
):
    step = pl.program_id(0)
    part = part_ref[0, 0]

    def one_hot(size, first, second):
        row = lax.broadcasted_iota(jnp.int32, (size, size), 0)
        lane = lax.broadcasted_iota(jnp.int32, (size, size), 1)
        wanted = (row % second) * first + row // second
        return jnp.where(lane == wanted, 1.0, 0.0).astype(jnp.bfloat16)

    row = lax.broadcasted_iota(jnp.int32, (64, 64), 0)
    lane = lax.broadcasted_iota(jnp.int32, (64, 64), 1)
    wanted = (row % 8) * 8 + ((row % 16) // 8) * 4 + row // 16
    moved = jnp.where(lane == wanted, 1.0, 0.0).astype(jnp.bfloat16)

    mine = lax.axis_index("dp").astype(jnp.int32) % 2

    def pick(core, spot, lanes):
        return jnp.where(
            mine == core, own_ref[spot, :, lanes], other_ref[spot, :, lanes]
        )

    for half in range(4):
        spot = pl.ds(pl.multiple_of(16 * step + 8 * (half // 2), 8), 8)
        block = pick(half % 2, spot, slice(0, LANES)).reshape(64, LANES)
        placed = dot_halved(moved, block, 1, 0).reshape(4, 16, LANES)
        lanes = slice(half * LANES, (half + 1) * LANES)
        out_a_ref[:, :, lanes] = placed[:3] + part * a_ref[:, :, lanes]
        out_bo_ref[:, lanes] = placed[3] + part * bo_ref[:, lanes]
    turned = one_hot(128, 8, 16)
    for sub in range(2):
        block = jnp.concatenate(
            [
                pick(at % 2, 8 * (at // 2) + 2 * step + sub, slice(LANES, None))
                for at in range(16)
            ],
            0,
        )
        placed = dot_halved(turned, block, 1, 0)
        for chunk in range(4):
            lanes = slice(sub * LANES + chunk * 128, sub * LANES + (chunk + 1) * 128)
            rows = slice(16 * chunk, 16 * chunk + 16)
            out_bq_ref[:, lanes] = placed[rows, :128] + part * bq_ref[:, lanes]
            rows = slice(64 + 16 * chunk, 80 + 16 * chunk)
            out_ao_ref[:, lanes] = placed[rows, :128] + part * ao_ref[:, lanes]
        lanes = slice(sub * HEAD_SIZE, (sub + 1) * HEAD_SIZE)
        out_bkv_ref[0, :, lanes] = placed[:16, 128:] + part * bkv_ref[0, :, lanes]
        out_bkv_ref[1, :, lanes] = placed[16:32, 128:] + part * bkv_ref[1, :, lanes]


def whole(count):
    return [pl.BlockSpec(memory_space=pltpu.VMEM)] * count


def product(left, right, right_dim):
    left_both = jnp.concatenate(rounded_parts(left, 2), 1)
    upper, lower = rounded_parts(right, 2)
    if right_dim == 0:
        rows = jnp.concatenate([upper, lower], 1)
        both = dot_halved(left_both, jnp.concatenate([rows, rows], 0), 1, 0)
    else:
        rows = jnp.concatenate([upper, lower], 0)
        both = dot_halved(left_both, jnp.concatenate([rows, rows], 1), 1, 1)
    size = right.shape[1 - right_dim]
    return both[:, :size] + both[:, size:]


def tall(parts):
    return jnp.concatenate(parts, 0)


def flat(parts):
    return jnp.concatenate(parts, 1)


def stack(rows):
    return tall([rows[:, at : at + 128] for at in range(0, rows.shape[1], 128)])


def unstack(rows):
    return flat([rows[at : at + 128] for at in range(0, rows.shape[0], 128)])


def place_shards(whole_ref, shards, semaphores):
    spots = shard_spots()
    half = whole_ref.shape[1] // 2
    copies = []
    for at, shard in enumerate(shards):
        spot = at if at < 6 else 6 + (at - 6) // 2
        rows = pl.ds(pl.multiple_of(spots[spot] * 16, 16), 16)
        if at < 6:
            target = whole_ref.at[rows, :]
        else:
            target = whole_ref.at[rows, pl.ds((at % 2) * half, half)]
        copies.append(pltpu.make_async_copy(shard, target, semaphores.at[at]))
    for copy in copies:
        copy.start()
    return copies


def launch(pairs, semaphores, first):
    copies = prepared(pairs, semaphores, first)
    begin(copies)
    return copies


def finish(copies):
    for copy in copies:
        copy.wait()


def prepared(pairs, semaphores, first):
    return [
        pltpu.make_async_copy(source, target, semaphores.at[first + at])
        for at, (source, target) in enumerate(pairs)
    ]


def begin(copies):
    for copy in copies:
        copy.start()


def span_of(step):
    if isinstance(step, int):
        return pl.ds(step * CHUNK, CHUNK)
    return pl.ds(pl.multiple_of(step * CHUNK, CHUNK), CHUNK)


ANYWHERE = pl.BlockSpec(memory_space=pl.ANY)


def in_hbm(arrays):
    return [pltpu.with_memory_space_constraint(array, pltpu.HBM) for array in arrays]


def hbm_like(results):
    return [pltpu.HBM(result.shape, result.dtype) for result in results]


def gather_by_relays(block):
    half = block.shape[1] // 2

    def permute(array, y_step, z_step):
        pairs = [
            (at, ((at // 4 + y_step) % 2) * 4 + (at % 4 + z_step) % 4) for at in range(8)
        ]
        return lax.ppermute(array, "tensor", pairs)

    across = permute(block, 1, 0)
    below = permute(block, 0, 1)
    above = permute(block, 0, 3)
    across_below = permute(across, 0, 1)
    across_above = permute(across, 0, 3)
    far = [permute(below[:, :half], 0, 1), permute(above[:, half:], 0, 3)]
    across_far = [
        permute(across_below[:, :half], 0, 1),
        permute(across_above[:, half:], 0, 3),
    ]
    return [block, across, below, above, across_below, across_above] + far + across_far


def shard_spots():
    rank = lax.axis_index("tensor").astype(jnp.int32)
    y, z = rank // 4 * 4, rank % 4
    other = 4 - y
    return [
        y + z,
        other + z,
        y + (z + 3) % 4,
        y + (z + 1) % 4,
        other + (z + 3) % 4,
        other + (z + 1) % 4,
        y + (z + 2) % 4,
        other + (z + 2) % 4,
    ]


def small_pairs(down_hbm, up_query_hbm, up_kv_hbm, small_ref):
    return [
        (down_hbm, small_ref.at[:, 0:512]),
        (up_query_hbm, small_ref.at[:, 512:1024]),
        (up_kv_hbm.at[0], small_ref.at[:, 1024:1152]),
        (up_kv_hbm.at[1], small_ref.at[:, 1152:1280]),
    ]


CHUNK = 2048
STATE_ROWS = 2368


def forward_body(
    shard_0,
    shard_1,
    shard_2,
    shard_3,
    shard_4,
    shard_5,
    shard_6,
    shard_7,
    shard_8,
    shard_9,
    query_weight_hbm,
    kv_weight_hbm,
    down_hbm,
    output_weight_hbm,
    up_output_hbm,
    small_down_hbm,
    small_query_hbm,
    small_kv_hbm,
    tokens_hbm,
    out_hbm,
    state_hbm,
    tokens_ref,
    query_weight_ref,
    kv_weight_ref,
    down_ref,
    output_weight_ref,
    up_output_ref,
    small_ref,
    out_ref,
    state_ref,
    query_sum,
    kv_sum,
    low_sum,
    semaphores,
):
    shards = [
        shard_0,
        shard_1,
        shard_2,
        shard_3,
        shard_4,
        shard_5,
        shard_6,
        shard_7,
        shard_8,
        shard_9,
    ]
    placed = place_shards(tokens_ref, shards, semaphores)
    count = tokens_ref.shape[1] // CHUNK

    def early(step):
        span = span_of(step)
        pairs = [
            (query_weight_hbm.at[span, :], query_weight_ref.at[span, :]),
            (kv_weight_hbm.at[:, span, :], kv_weight_ref.at[:, span, :]),
            (down_hbm.at[:, span], down_ref.at[:, span]),
        ]
        return prepared(pairs, semaphores, 10 + 3 * step)

    def late(step):
        span = span_of(step)
        pairs = [
            (output_weight_hbm.at[:, span], output_weight_ref.at[:, span]),
            (up_output_hbm.at[:, span], up_output_ref.at[:, span]),
        ]
        return prepared(pairs, semaphores, 10 + 3 * count + 2 * step)

    def departing(step):
        span = span_of(step)
        pairs = [(out_ref.at[:, :, span], out_hbm.at[:, :, span])]
        return prepared(pairs, semaphores, 10 + 5 * count + step)

    for step in range(count):
        begin(early(step))
    pairs = small_pairs(small_down_hbm, small_query_hbm, small_kv_hbm, small_ref)
    small_copy = launch(pairs, semaphores, 12 + 6 * count)
    finish(placed)
    leaving = launch([(tokens_ref, tokens_hbm)], semaphores, 10 + 6 * count)
    query_sum[...] = jnp.zeros(query_sum.shape, jnp.float32)
    kv_sum[...] = jnp.zeros(kv_sum.shape, jnp.float32)
    low_sum[...] = jnp.zeros(low_sum.shape, jnp.float32)

    def project(step, _):
        finish(early(step))
        begin(late(step))
        span = span_of(step)
        tokens = tokens_ref[:, span]
        query_sum[...] += dot_halved(tokens, query_weight_ref[span, :], 1, 0)
        kv_sum[...] += dot_halved(
            tokens, flat([kv_weight_ref[0, span, :], kv_weight_ref[1, span, :]]), 1, 0
        )
        low_sum[:48] += dot_halved(down_ref[:, span], tokens, 1, 1)
        return 0

    lax.fori_loop(0, count, project, 0)
    finish(small_copy)
    low_turned = low_sum[...]
    low = low_turned.T
    root = 1.0 / math.sqrt(HEAD_SIZE)

    def adapted(total, piece, up):
        parts = rounded_parts(low[:, 16 * piece : 16 * piece + 16], 2)
        return total + ADAPTER_SCALE * dot_halved(flat(parts), tall([up, up]), 1, 0)

    query = stack(adapted(query_sum[...], 0, small_ref[:, 512:1024]))
    keys = adapted(kv_sum[:, :128], 1, small_ref[:, 1024:1152])
    values = adapted(kv_sum[:, 128:], 2, small_ref[:, 1152:])
    capped = jnp.tanh(product(query, keys, 1) * (root / SCORE_CAP))
    row = lax.broadcasted_iota(jnp.int32, (512, 128), 0) % 128
    lane = lax.broadcasted_iota(jnp.int32, (512, 128), 1)
    weights = jnp.where(row >= lane, jnp.exp(SCORE_CAP * capped), 0.0)
    probs = weights / lane_sum(weights)
    context_rows = product(probs, values, 0)
    context = unstack(context_rows)
    low_pair = dot_halved(small_ref[:, :512], tall(rounded_parts(context, 2)), 1, 1)
    context_low = ADAPTER_SCALE * (low_pair[:, :128] + low_pair[:, 128:])
    state_ref[0:512] = query
    state_ref[512:1024] = context_rows
    state_ref[1024:1536] = probs
    state_ref[1536:2048] = capped
    state_ref[2048:2176] = keys
    state_ref[2176:2304] = values
    state_ref[2304:2352] = low_turned[:48]
    state_ref[2352:2368] = context_low
    halved = context.astype(jnp.bfloat16)
    turned = tall([context_low, jnp.zeros((112, 128), jnp.float32)]).T[:, :16]
    halved_low = flat(rounded_parts(turned, 2))
    leaving += launch([(state_ref, state_hbm)], semaphores, 11 + 6 * count)

    def write(step, _):
        finish(late(step))
        span = span_of(step)
        up = up_output_ref[:, span]
        terms = dot_halved(halved, output_weight_ref[:, span], 1, 0) + dot_halved(
            halved_low, tall([up, up]), 1, 0
        )
        out_ref[:, :, span] = terms.astype(jnp.bfloat16).reshape(8, 16, CHUNK)
        begin(departing(step))
        return 0

    lax.fori_loop(0, count, write, 0)
    for step in range(count):
        finish(departing(step))
    finish(leaving)


def forward(
    shards, query_weight, key_value_weight, down_rows, output_weight, up_output, *adapters
):
    width = shards[0].shape[1]
    query_cols = query_weight.shape[1]
    weights = (query_weight, key_value_weight, down_rows, output_weight, up_output)
    arrays = (*weights, *adapters)
    small = jax.ShapeDtypeStruct((16, 1280), jnp.bfloat16)
    results = [
        jax.ShapeDtypeStruct((128, width), jnp.bfloat16),
        jax.ShapeDtypeStruct((8, 16, width), jnp.bfloat16),
        jax.ShapeDtypeStruct((STATE_ROWS, 128), jnp.float32),
    ]
    scratch = [results[0], *weights, small, results[1], results[2]]
    return pl.pallas_call(
        forward_body,
        in_specs=[ANYWHERE] * (len(shards) + len(arrays)),
        out_specs=[ANYWHERE] * 3,
        out_shape=hbm_like(results),
        scratch_shapes=[pltpu.VMEM(array.shape, array.dtype) for array in scratch]
        + [
            pltpu.VMEM((128, query_cols), jnp.float32),
            pltpu.VMEM((128, 256), jnp.float32),
            pltpu.VMEM((128, 128), jnp.float32),
            pltpu.SemaphoreType.DMA((16 + 6 * (width // CHUNK),)),
        ],
        compiler_params=pltpu.CompilerParams(vmem_limit_bytes=40 * 2**20),
        name="forward",
    )(*in_hbm(shards[:1]), *shards[1:], *in_hbm(arrays))


def cotangents_body(
    lens_ref,
    shard_0,
    shard_1,
    shard_2,
    shard_3,
    shard_4,
    shard_5,
    shard_6,
    shard_7,
    shard_8,
    shard_9,
    weight_hbm,
    side_hbm,
    state_hbm,
    small_down_hbm,
    small_query_hbm,
    small_kv_hbm,
    resid_hbm,
    factors_ref,
    narrow_ref,
    scalars_ref,
    resid_ref,
    weight_ref,
    side_ref,
    state_ref,
    small_ref,
    through_ref,
    slow_ref,
    square_ref,
    semaphores,
):
    shards = [
        shard_0,
        shard_1,
        shard_2,
        shard_3,
        shard_4,
        shard_5,
        shard_6,
        shard_7,
        shard_8,
        shard_9,
    ]
    placed = place_shards(resid_ref, shards, semaphores)
    count = resid_ref.shape[1] // CHUNK

    def early(step):
        span = span_of(step)
        pairs = [
            (weight_hbm.at[:, span], weight_ref.at[:, span]),
            (side_hbm.at[:, span], side_ref.at[:, span]),
        ]
        return prepared(pairs, semaphores, 10 + 2 * step)

    for step in range(count):
        begin(early(step))
    first = 10 + 2 * count
    pairs = small_pairs(small_down_hbm, small_query_hbm, small_kv_hbm, small_ref)
    others = launch([(state_hbm, state_ref)] + pairs, semaphores, first)
    slow_ref[...] = jnp.zeros(slow_ref.shape, jnp.float32)
    through_ref[...] = jnp.zeros(through_ref.shape, jnp.float32)
    square_ref[...] = jnp.zeros(square_ref.shape, jnp.float32)
    narrow_ref[...] = jnp.zeros(narrow_ref.shape, jnp.float32)
    width = resid_ref.shape[1]
    finish(placed)
    leaving = launch([(resid_ref, resid_hbm)], semaphores, first + 5)

    def project(step, _):
        finish(early(step))
        span = span_of(step)
        chunk = resid_ref[:, span]
        side = side_ref[:, span]
        left = tall([chunk, side[16:]])
        through_ref[...] += dot_halved(left, weight_ref[:, span], 1, 1)
        slow_ref[:144, :32] += dot_halved(left, side, 1, 1)
        wide = chunk.astype(jnp.float32)
        square = jnp.zeros((128, 128), jnp.float32)
        for lanes in range(0, CHUNK, 128):
            square = square + wide[:, lanes : lanes + 128] * wide[:, lanes : lanes + 128]
        square_ref[...] += square
        return 0

    lax.fori_loop(0, count, project, 0)
    finish(others)
    finish_cotangents(
        lens_ref,
        width,
        state_ref,
        small_ref,
        factors_ref,
        narrow_ref,
        scalars_ref,
        through_ref,
        slow_ref,
        square_ref,
    )
    finish(leaving)


def finish_cotangents(
    lens_ref,
    width,
    state_ref,
    small_ref,
    factors_ref,
    narrow_ref,
    scalars_ref,
    through_ref,
    slow_ref,
    square_ref,
):
    if True:
        length_own = lens_ref[0]
        root = 1.0 / math.sqrt(HEAD_SIZE)
        slow = slow_ref[...]
        slow_turned = slow.T
        square = square_ref[...]
        inverse = lax.rsqrt(lane_sum(square) / width + NORM_EPS)
        inverse_turned = lax.rsqrt(row_sum(square.T) / width + NORM_EPS)
        each = 1.0 / jnp.broadcast_to(length_own, (1, 1)).astype(jnp.float32)
        share = jnp.where(
            lax.broadcasted_iota(jnp.int32, (128, 1), 0) < length_own, each, 0.0
        )
        share_turned = jnp.where(
            lax.broadcasted_iota(jnp.int32, (1, 128), 1) < length_own, each, 0.0
        )
        logits = inverse * slow[:128, 16:32]
        lead = share * inverse
        pulled = lead * inverse * logits / width
        lead_turned = share_turned * inverse_turned
        pulled_turned = (
            lead_turned * inverse_turned * inverse_turned * slow_turned[16:32, :128] / width
        )
        low_turned = slow_turned[:16, :128]
        scalars_ref[:8] = jnp.zeros((8, 128), jnp.float32)
        scalars_ref[:1, :16] = row_sum(share * logits)
        down = small_ref[:, :512]
        through = through_ref[...] + ADAPTER_SCALE * dot_halved(
            flat(rounded_parts(slow[:144, :16], 2)), tall([down, down]), 1, 0
        )
        query = state_ref[0:512]
        context_rows = state_ref[512:1024]
        probs = state_ref[1024:1536]
        capped = state_ref[1536:2048]
        keys = state_ref[2048:2176]
        values = state_ref[2176:2304]
        low_q = state_ref[2304:2320]
        low_k = state_ref[2320:2336]
        low_v = state_ref[2336:2352]
        context_low = state_ref[2352:2368]
        small = small_ref[:, 512:].astype(jnp.float32)
        up_query, up_keys, up_values = small[:, :512], small[:, 512:640], small[:, 640:]
        objectives = range(OBJ)
        head_spots = range(4)
        across = stack(through[:128])
        heads = stack(through[128:136])
        on_values = product(tall([across, heads]), values, 1)
        heads_on_values = on_values[512:]
        slope = probs * (1.0 - capped * capped) * root
        shared = slope * (on_values[:512] - lane_sum(across * context_rows))
        leading = slope * tall([lead] * 4)
        heads_on_context = product(heads, context_rows, 1)
        query_on_keys = product(stack(up_query), keys, 1)
        keys_on_query = product(up_keys, query, 1)
        padded = tall([across, heads, jnp.zeros((96, 128), jnp.float32)])
        values_on_cot = product(up_values, padded, 1)
        low_on_probs = product(low_v, probs, 1)

        def block(array, head):
            return array[:, 128 * head : 128 * head + 128]

        def row_of(array, row):
            return array[row : row + 1]

        left_values = []
        right_values = []
        for obj in objectives:
            pull = row_of(pulled_turned, obj)
            parts = []
            for head in head_spots:
                spot = 512 + 8 * head + obj
                parts.append(
                    values_on_cot[:, spot : spot + 1] * lead_turned
                    - pull * block(values_on_cot, head)
                )
            left_values.append(flat(parts))
            right_values.append(low_on_probs * flat([pull] * 4))
        factor_values = product(tall(left_values), probs, 0)
        jac_values = -product(tall(right_values), across, 0)
        low_lead = [lane_sum(block(low_on_probs, head) * lead_turned) for head in head_spots]
        factor_query = [0.0] * OBJ
        factor_keys = [0.0] * OBJ
        query_rows = [[] for _ in objectives]
        keys_rows = [[] for _ in objectives]
        for head in head_spots:
            rows = slice(128 * head, 128 * head + 128)
            score_lead, score_shared = leading[rows], shared[rows]
            on_context = block(heads_on_context, head)[8 * head : 8 * head + 8]
            on_value = heads_on_values[8 * head : 8 * head + 8]
            base = tall([low_q, block(keys_on_query, head)])
            first = product(
                tall([base] + [base * row_of(on_context, obj) for obj in objectives]),
                score_lead,
                0,
            )
            second = product(
                tall([base * row_of(pulled_turned, obj) for obj in objectives]), score_shared, 0
            )
            base = tall([query_on_keys[16 * head : 16 * head + 16], low_k])
            third = product(
                tall([base] + [base * row_of(on_value, obj) for obj in objectives]),
                score_lead,
                1,
            )
            fourth = product(base, score_shared, 1)
            for obj in objectives:
                spot = slice(32 + 32 * obj, 64 + 32 * obj)
                by_rows = (
                    first[:32] * row_of(on_value, obj)
                    - first[spot]
                    - second[32 * obj : 32 * obj + 32]
                )
                by_lanes = (
                    third[spot]
                    - row_of(on_context, obj) * third[:32]
                    - row_of(pulled_turned, obj) * fourth
                )
                query_rows[obj].append(by_rows[:16])
                factor_keys[obj] += by_rows[16:]
                factor_query[obj] += by_lanes[:16]
                keys_rows[obj].append(by_lanes[16:])
        jac_query = product(tall([tall(rows) for rows in query_rows]), keys, 0)
        jac_keys = product(tall([flat(rows) for rows in keys_rows]), query, 0)
        cot_low = [
            slow_turned[:16, 128 + obj : 129 + obj] * lead_turned
            - row_of(pulled_turned, obj) * low_turned
            for obj in objectives
        ]
        jac_down = product(tall(cot_low), unstack(context_rows), 0)
        for obj in objectives:
            own = slice(16 * obj, 16 * obj + 16)
            rows = [
                ADAPTER_SCALE * factor_query[obj],
                ADAPTER_SCALE * factor_keys[obj],
                ADAPTER_SCALE * factor_values[own],
                context_low,
            ]
            for piece in range(4):
                for half in range(2):
                    factors_ref[pl.ds(20 * half + 5 * piece + obj, 8, stride=40), :] = rows[
                        piece
                    ][8 * half : 8 * half + 8]
            own_values = jac_values[own]
            for head in head_spots:
                own_values += low_lead[head] * row_of(heads, 8 * head + obj)
            blocks = [
                jac_query[64 * obj + 16 * head : 64 * obj + 16 * head + 16]
                for head in head_spots
            ]
            blocks += [block(jac_down, head)[own] for head in head_spots]
            blocks += [jac_keys[own], own_values]
            spots = [(0, 0), (0, 1), (0, 2), (0, 3), (5, 0), (5, 1), (5, 2), (5, 3)]
            spots += [(10, 0), (10, 1)]
            for (row, tile), part in zip(spots, blocks):
                for half in range(2):
                    narrow_ref[tile, pl.ds(128 * half + row + obj, 8, stride=16), :] = (
                        ADAPTER_SCALE * part[8 * half : 8 * half + 8]
                    )
        blank = jnp.zeros((15, 128), jnp.float32)
        scalars_ref[8:48] = jnp.concatenate([blank, pulled_turned[:5]] * 2, 0)
        scalars_ref[48:] = jnp.broadcast_to(lead_turned, (40, 128))


def cotangents(lens, shards, output_weight, side, state, *adapters):
    width = shards[0].shape[1]
    query_cols = output_weight.shape[0]
    arrays = (output_weight, side, state, *adapters)
    small = jax.ShapeDtypeStruct((16, 1280), jnp.bfloat16)
    scratch = [output_weight, side, state, small]
    results = [
        jax.ShapeDtypeStruct((128, width), jnp.bfloat16),
        jax.ShapeDtypeStruct((320, 128), jnp.float32),
        jax.ShapeDtypeStruct((4, 256, 128), jnp.float32),
        jax.ShapeDtypeStruct((88, 128), jnp.float32),
    ]
    return pl.pallas_call(
        cotangents_body,
        in_specs=[pl.BlockSpec(memory_space=pltpu.SMEM)]
        + [ANYWHERE] * (len(shards) + len(arrays)),
        out_specs=[ANYWHERE] + whole(3),
        out_shape=hbm_like(results),
        scratch_shapes=[pltpu.VMEM(array.shape, array.dtype) for array in (results[0], *scratch)]
        + [
            pltpu.VMEM((144, query_cols), jnp.float32),
            pltpu.VMEM((256, 128), jnp.float32),
            pltpu.VMEM((128, 128), jnp.float32),
            pltpu.SemaphoreType.DMA((16 + 2 * (width // CHUNK),)),
        ],
        compiler_params=pltpu.CompilerParams(vmem_limit_bytes=32 * 2**20),
        name="cotangents",
    )(lens, *shards, *in_hbm(arrays))


def jacobian_body(
    factors_hbm,
    tokens_hbm,
    resid_hbm,
    heads_hbm,
    scalars_hbm,
    narrow_hbm,
    payload_hbm,
    factors_ref,
    tokens_ref,
    resid_ref,
    heads_ref,
    scalars_ref,
    narrow_ref,
    payload_ref,
    semaphores,
):
    early = launch([(factors_hbm, factors_ref), (scalars_hbm, scalars_ref)], semaphores, 0)
    count = tokens_ref.shape[1] // CHUNK
    per_step = CHUNK // LANES

    def arriving(step):
        span = span_of(step)
        pairs = [
            (tokens_hbm.at[:, span], tokens_ref.at[:, span]),
            (resid_hbm.at[:, span], resid_ref.at[:, span]),
            (heads_hbm.at[:, span], heads_ref.at[:, span]),
        ]
        return prepared(pairs, semaphores, 3 + 3 * step)

    def departing(step):
        groups = pl.ds(step * per_step, per_step)
        pairs = [(payload_ref.at[groups], payload_hbm.at[groups])]
        return prepared(pairs, semaphores, 3 + 3 * count + step)

    begin(arriving(0))
    early += launch([(narrow_hbm, narrow_ref)], semaphores, 2)
    for step in range(1, count):
        begin(arriving(step))
    finish(early)
    factors = jnp.sum(factors_ref[...], axis=0)
    row = lax.broadcasted_iota(jnp.int32, (40, 1), 0) % 20
    last = row >= 15
    left = flat(
        [jnp.where(last, 0.0, factors), jnp.where(last, -factors * scalars_ref[8:48], 0.0)]
    )
    lead = lane_sum(factors * scalars_ref[48:])

    def both(rows):
        upper = rows.astype(jnp.bfloat16).astype(jnp.float32)
        return tall([upper, rows - upper]).astype(jnp.bfloat16)

    left = both(left)

    def place(step, _):
        finish(arriving(step))
        span = span_of(step)
        right = tall([tokens_ref[:, span], resid_ref[:, span]])
        pair = dot_halved(left, right, 1, 0)
        rows = pair[:40] + pair[40:] + lead * heads_ref[:40, span].astype(jnp.float32)
        for inner in range(per_step):
            group = step * per_step + inner
            below = flat(
                [
                    narrow_ref[tile, pl.ds(pl.multiple_of(group * 16, 16), 16), :]
                    for tile in range(4)
                ]
            )
            block = tall([rows[:, inner * LANES : (inner + 1) * LANES], below])
            payload_ref[group] = block.astype(jnp.bfloat16)
        begin(departing(step))
        return 0

    lax.fori_loop(0, count, place, 0)
    for step in range(count):
        finish(departing(step))


def jacobian(*arrays):
    result = jax.ShapeDtypeStruct((16, PIECE_ROWS, LANES), jnp.bfloat16)
    steps = arrays[1].shape[1] // CHUNK
    return pl.pallas_call(
        jacobian_body,
        in_specs=[ANYWHERE] * len(arrays),
        out_specs=ANYWHERE,
        out_shape=hbm_like([result])[0],
        scratch_shapes=[pltpu.VMEM(array.shape, array.dtype) for array in (*arrays, result)]
        + [pltpu.SemaphoreType.DMA((3 + 4 * steps,))],
        compiler_params=pltpu.CompilerParams(vmem_limit_bytes=24 * 2**20),
        name="jacobian",
    )(arrays[0], *in_hbm(arrays[1:]))


def assemble(part, own, other, *shapes):
    steps = 4
    blocks = [
        pl.BlockSpec((3, 16, 4 * LANES), lambda step: (0, 0, step)),
        pl.BlockSpec((16, 2 * LANES), lambda step: (0, step)),
        pl.BlockSpec((2, 16, 2 * HEAD_SIZE), lambda step: (0, 0, step)),
        pl.BlockSpec((16, 2 * LANES), lambda step: (0, step)),
        pl.BlockSpec((16, 4 * LANES), lambda step: (0, step)),
    ]
    return pl.pallas_call(
        assemble_body,
        grid=(steps,),
        in_specs=[
            pl.BlockSpec(memory_space=pltpu.SMEM),
            pl.BlockSpec(own.shape, lambda step: (0, 0, 0)),
            pl.BlockSpec(other.shape, lambda step: (0, 0, 0)),
        ]
        + blocks,
        out_specs=blocks,
        out_shape=[jax.ShapeDtypeStruct(shape.shape, jnp.float32) for shape in shapes],
        compiler_params=pltpu.CompilerParams(vmem_limit_bytes=14 * 2**20),
        name="assemble",
    )(part, own, other, *shapes)


def local(
    hidden,
    query_weight,
    key_value_weight,
    output_weight,
    head,
    lens,
    partner,
    adapter_down_qkv,
    adapter_up_query,
    adapter_up_key_value,
    adapter_down_output,
    adapter_up_output,
    initial_down_qkv,
    initial_up_query,
    initial_up_key_value,
    initial_down_output,
    initial_up_output,
):
    _, part_length, width = hidden.shape
    shards = lax.axis_size("tensor")
    groups = lax.axis_size("dp")
    tensor_rank = lax.axis_index("tensor")
    group_rank = lax.axis_index("dp")
    query_cols = query_weight.shape[1]
    length = part_length * shards

    down_rows = jnp.transpose(adapter_down_qkv, (0, 2, 1)).reshape(48, width)
    down_output = adapter_down_output.T
    head_rows = head.T
    side = jnp.concatenate([adapter_up_output, head_rows, jnp.zeros((11, width), head.dtype)], 0)
    heads = jnp.pad(head_rows, ((15, 0), (0, 0)))
    heads = jnp.pad(jnp.concatenate([heads, heads], 0), ((0, 8), (0, 0)))
    adapters = (down_output, adapter_up_query, adapter_up_key_value)
    tokens, out_terms, state = forward(
        gather_by_relays(hidden[0]),
        query_weight,
        key_value_weight,
        down_rows,
        output_weight,
        adapter_up_output,
        *adapters,
    )
    out_pieces = lax.all_to_all(out_terms, "tensor", 0, 0)
    resid_own = hidden[0].astype(jnp.float32) + jnp.sum(out_pieces.astype(jnp.float32), 0)
    resid, factors, narrow, scalars = cotangents(
        lens,
        gather_by_relays(resid_own.astype(jnp.bfloat16)),
        output_weight,
        side,
        state,
        *adapters,
    )
    factors = lax.all_to_all(factors.reshape(shards, 8 * OBJ, length), "tensor", 0, 0)
    payload = jacobian(factors, tokens, resid, heads, scalars, narrow)
    spread = lax.all_to_all(payload, "dp", 0, 0)
    jac = (
        spread[:, : PIECES * OBJ]
        .reshape(groups, PIECES, OBJ, LANES)
        .transpose(0, 2, 1, 3)
        .reshape(groups * OBJ, PIECES * LANES)
    )

    starts = (
        jnp.transpose(initial_down_qkv, (0, 2, 1)),
        initial_up_query,
        initial_up_key_value,
        initial_down_output.T,
        initial_up_output,
    )
    starts = [pltpu.with_memory_space_constraint(start, pltpu.HBM) for start in starts]
    sequences = jnp.arange(groups)
    leads = sequences < partner
    order = jnp.sum((sequences[None, :] < sequences[:, None]) & leads[None, :], 1)
    chosen = (
        leads[None, :] & (order[None, :] == jnp.arange(groups // 2)[:, None])
    ).astype(jnp.float32)
    differences = chosen - jnp.take(chosen, partner, axis=1)
    pairs = (
        differences[:, None, :, None] * jnp.eye(OBJ, dtype=jnp.float32)[None, :, None, :]
    ).reshape(PAIR_ROWS, groups * OBJ)
    pairs = jnp.pad(pairs, ((0, PACK_ROWS - PAIR_ROWS), (0, 128 - groups * OBJ)))
    packed = pl.pallas_call(
        gram_body,
        in_specs=whole(3) + [ANYWHERE] * 5,
        out_specs=pl.BlockSpec(memory_space=pltpu.VMEM),
        out_shape=jax.ShapeDtypeStruct((16, 128), jnp.float32),
        scratch_shapes=[
            pltpu.VMEM((3, 16, LANES), jnp.float32),
            pltpu.VMEM((16, LANES), jnp.float32),
            pltpu.VMEM((2, 16, HEAD_SIZE), jnp.float32),
            pltpu.VMEM((16, LANES), jnp.float32),
            pltpu.VMEM((16, LANES), jnp.float32),
            pltpu.SemaphoreType.DMA((5,)),
        ],
        compiler_params=pltpu.CompilerParams(vmem_limit_bytes=6 * 2**20),
        name="gram",
    )(jac, pairs, scalars[:8], *starts)
    packed = jnp.sum(gather_by_exchange(packed, "dp"), 0)
    packed = gather_by_exchange(packed, "tensor")
    own_result, part = pl.pallas_call(
        lanczos_body,
        in_specs=whole(3),
        out_specs=whole(2),
        out_shape=[
            jax.ShapeDtypeStruct((8, RESULT_LANES), jnp.bfloat16),
            jax.ShapeDtypeStruct((1, 128), jnp.float32),
        ],
        compiler_params=pltpu.CompilerParams(vmem_limit_bytes=6 * 2**20),
        name="lanczos",
    )(packed, pairs, jac)
    half = groups * shards // 2
    same_core = [
        [at for at in range(2 * half) if (at // shards) % 2 == core] for core in range(2)
    ]
    own_half = lax.all_to_all(
        jnp.broadcast_to(own_result[None], (half,) + own_result.shape),
        ("dp", "tensor"),
        0,
        0,
        axis_index_groups=same_core,
    )
    other_half = lax.ppermute(own_half, "dp", [(at, at ^ 1) for at in range(groups)])
    next_a, next_bq, next_bkv, next_ao, next_bo = assemble(part, own_half, other_half, *starts)
    return jnp.transpose(next_a, (0, 2, 1)), next_bq, next_bkv, next_ao.T, next_bo


def solution(mesh):
    in_specs = (
        P("dp", "tensor", None),
        P(None, "tensor"),
        P(None, None, "tensor"),
        P("tensor", None),
        P(),
        P("dp"),
        P(),
        P(),
        P(None, "tensor"),
        P(None, None, "tensor"),
        P("tensor", None),
        P(),
        P(),
        P(),
        P(),
        P(),
        P(),
    )
    out_specs = (P(), P(), P(), P(), P())
    return jax.shard_map(local, mesh=mesh, in_specs=in_specs, out_specs=out_specs, check_vma=False)
```

```python
import math

import jax
import jax.numpy as jnp
from jax import lax
from jax.experimental import pallas as pl
from jax.experimental.pallas import tpu as pltpu
from jax.sharding import PartitionSpec as P

HEAD_SIZE = 128
NPARAM = 688128
ADAPTER_SCALE = 2.0
NORM_EPS = 1e-05
LANCZOS_EPS = 1e-06
SCORE_CAP = 30.0
PRECISE = lax.Precision.HIGHEST
OBJ = 5
PIECES = 11
PIECE_ROWS = 56
LANES = 512


def dot_halved(left_side, right_side, left_dim, right_dim):
    return lax.dot_general(
        left_side,
        right_side,
        (((left_dim,), (right_dim,)), ((), ())),
        preferred_element_type=jnp.float32,
    )


def dot_entire(left_side, right_side, left_dim, right_dim):
    return lax.dot_general(
        left_side,
        right_side,
        (((left_dim,), (right_dim,)), ((), ())),
        precision=PRECISE,
        preferred_element_type=jnp.float32,
    )


def gather_by_exchange(block, axis):
    count = lax.axis_size(axis)
    copies = jnp.broadcast_to(block[None], (count,) + block.shape)
    return lax.all_to_all(copies, axis, 0, 0)


PAIR_ROWS = 40
PACK_ROWS = 48
PACK_LANES = 42
RESULT_LANES = 768


def rounded_parts(entire, count):
    parts = []
    for _ in range(count):
        part = entire.astype(jnp.bfloat16)
        parts.append(part)
        entire = entire - part.astype(jnp.float32)
    return parts


def lane_sum(values):
    return jnp.sum(values, axis=1, keepdims=True)


def row_sum(values):
    return jnp.sum(values, axis=0, keepdims=True)


def gram_body(
    jac_ref,
    pairs_ref,
    rewards_ref,
    a_hbm,
    bq_hbm,
    bkv_hbm,
    ao_hbm,
    bo_hbm,
    packed_ref,
    a_ref,
    bq_ref,
    bkv_ref,
    ao_ref,
    bo_ref,
    semaphores,
):
    group = lax.axis_index("dp").astype(jnp.int32)
    rank = lax.axis_index("tensor").astype(jnp.int32)
    by_group = pl.ds(pl.multiple_of(group * LANES, LANES), LANES)
    by_rank = pl.ds(pl.multiple_of(rank * LANES, LANES), LANES)
    narrow = pl.ds(pl.multiple_of(rank * HEAD_SIZE, HEAD_SIZE), HEAD_SIZE)
    pairs = [
        (a_hbm.at[:, :, by_group], a_ref),
        (bq_hbm.at[:, by_rank], bq_ref),
        (bkv_hbm.at[:, :, narrow], bkv_ref),
        (ao_hbm.at[:, by_rank], ao_ref),
        (bo_hbm.at[:, by_group], bo_ref),
    ]
    copies = launch(pairs, semaphores, 0)
    jac = jac_ref[...]
    pairs = pairs_ref[...]
    rows = jac.shape[0]
    gram = dot_halved(jac, jac, 1, 1)
    finish(copies)
    blocks = []
    for row in (rank, rank + 8):
        blocks += [a_ref[piece, pl.ds(row, 1), :] for piece in range(3)]
        blocks.append(bo_ref[pl.ds(row, 1), :])
    blocks += [bq_ref[pl.ds(group, 1), :], ao_ref[pl.ds(group, 1), :]]
    blocks += [bkv_ref[piece, pl.ds(group, 1), :] for piece in range(2)]
    start = flat(blocks + [jnp.zeros((1, LANES - 2 * HEAD_SIZE), jnp.float32)])
    starts = jnp.concatenate(rounded_parts(start, 3), 0)
    along = lane_sum(dot_halved(jac, starts, 1, 1))
    own_pairs = pairs[:, :rows]
    gram = dot_entire(dot_entire(own_pairs, gram, 1, 0), own_pairs, 1, 1)
    along = dot_entire(own_pairs, jnp.broadcast_to(along, (rows, 128)), 1, 0)
    rewards = pltpu.roll(rewards_ref[...], OBJ * group, axis=1)[:1]
    rewards = jnp.where(rank == 0, rewards, 0.0)
    apart = lane_sum(pairs * rewards)
    square = jnp.sum(start * start)
    lane = lax.broadcasted_iota(jnp.int32, (PACK_ROWS, 128), 1)
    row = lax.broadcasted_iota(jnp.int32, (PACK_ROWS, 128), 0)
    wide = jnp.concatenate([gram, jnp.zeros((PACK_ROWS, 128 - PACK_ROWS), jnp.float32)], 1)
    wide = jnp.where(lane < PAIR_ROWS, wide, 0.0)
    wide = jnp.where(lane == PAIR_ROWS, along, wide)
    wide = jnp.where(lane == PAIR_ROWS + 1, apart, wide)
    wide = jnp.where((row == PAIR_ROWS) & (lane == 0), square, wide)
    packed_ref[...] = (
        wide[:16]
        + pltpu.roll(wide[16:32], PACK_LANES, axis=1)
        + pltpu.roll(wide[32:], 2 * PACK_LANES, axis=1)
    )


def lanczos_body(packed_ref, pairs_ref, jac_ref, result_ref, part_ref):
    packed = jnp.sum(packed_ref[...], axis=0)
    wide = jnp.concatenate(
        [
            packed,
            pltpu.roll(packed, 128 - PACK_LANES, axis=1),
            pltpu.roll(packed, 128 - 2 * PACK_LANES, axis=1),
        ],
        0,
    )
    lane = lax.broadcasted_iota(jnp.int32, (PACK_ROWS, 128), 1)
    row = lax.broadcasted_iota(jnp.int32, (PACK_ROWS, 128), 0)
    inside = row < PAIR_ROWS
    gram = jnp.where(inside & (lane < PAIR_ROWS), wide, 0.0)
    along = lane_sum(jnp.where(inside & (lane == PAIR_ROWS), wide, 0.0))
    apart = lane_sum(jnp.where(inside & (lane == PAIR_ROWS + 1), wide, 0.0))
    picked = jnp.where((row == PAIR_ROWS) & (lane == 0), wide, 0.0)
    start_square = lane_sum(row_sum(picked)) / NPARAM
    diagonal = row == lane

    def gram_times(column):
        across = row_sum(jnp.where(diagonal, column, 0.0))
        return lane_sum(gram * across)

    def inner(left_side, right_side):
        return row_sum(left_side * right_side) / NPARAM

    decayed = jnp.exp(-jnp.abs(apart))
    curvature = decayed / ((1.0 + decayed) * (1.0 + decayed)) / (16 // 2)
    start_scale = lax.rsqrt(start_square + LANCZOS_EPS)
    first_square = start_square * start_scale * start_scale
    along_one = along * start_scale
    pull_one = curvature * along_one
    alpha_one = inner(pull_one, along_one)
    gram_pull = gram_times(pull_one)
    beta_one = jnp.sqrt(
        inner(pull_one, gram_pull) - alpha_one * alpha_one * (2.0 - first_square) + LANCZOS_EPS
    )
    along_two = (gram_pull - alpha_one * along_one) / beta_one
    pull_two = curvature * along_two
    first_second = alpha_one * (1.0 - first_square) / beta_one
    alpha_two = inner(pull_two, along_two) - beta_one * first_second
    mixed = pull_two - (alpha_two / beta_one) * pull_one
    first_part = alpha_two * alpha_one / beta_one - beta_one
    beta_two = jnp.sqrt(
        inner(mixed, gram_times(mixed))
        + 2.0 * first_part * inner(mixed, along_one)
        + first_part * first_part * first_square
        + LANCZOS_EPS
    )
    part_ref[...] = jnp.broadcast_to(first_part * start_scale / beta_two, part_ref.shape)
    across = row_sum(pairs_ref[...] * (mixed / beta_two))
    jac = jac_ref[...]
    rows = jac.shape[0]
    parts = rounded_parts(jnp.broadcast_to(across[:, :rows], (8, rows)), 3)
    result = sum(dot_halved(part, jac, 1, 0) for part in parts)[:1]
    spare = jnp.zeros((6, 128), jnp.float32)

    def chunks(start, count, size):
        return [result[:, start + size * step : start + size * (step + 1)] for step in range(count)]

    main = jnp.concatenate(chunks(0, 8, LANES), 0)
    middle = jnp.concatenate(chunks(8 * LANES, 8, 128), 0)
    last = jnp.concatenate(chunks(10 * LANES, 2, 128) + [spare], 0)
    result_ref[...] = jnp.concatenate([main, middle, last], 1).astype(jnp.bfloat16)


def assemble_body(
    part_ref,
    own_ref,
    other_ref,
    a_ref,
    bq_ref,
    bkv_ref,
    ao_ref,
    bo_ref,
    out_a_ref,
    out_bq_ref,
    out_bkv_ref,
    out_ao_ref,
    out_bo_ref,
):
    step = pl.program_id(0)
    part = part_ref[0, 0]

    def one_hot(size, first, second):
        row = lax.broadcasted_iota(jnp.int32, (size, size), 0)
        lane = lax.broadcasted_iota(jnp.int32, (size, size), 1)
        wanted = (row % second) * first + row // second
        return jnp.where(lane == wanted, 1.0, 0.0).astype(jnp.bfloat16)

    row = lax.broadcasted_iota(jnp.int32, (64, 64), 0)
    lane = lax.broadcasted_iota(jnp.int32, (64, 64), 1)
    wanted = (row % 8) * 8 + ((row % 16) // 8) * 4 + row // 16
    moved = jnp.where(lane == wanted, 1.0, 0.0).astype(jnp.bfloat16)

    mine = lax.axis_index("dp").astype(jnp.int32) % 2

    def pick(core, spot, lanes):
        return jnp.where(
            mine == core, own_ref[spot, :, lanes], other_ref[spot, :, lanes]
        )

    for half in range(4):
        spot = pl.ds(pl.multiple_of(16 * step + 8 * (half // 2), 8), 8)
        block = pick(half % 2, spot, slice(0, LANES)).reshape(64, LANES)
        placed = dot_halved(moved, block, 1, 0).reshape(4, 16, LANES)
        lanes = slice(half * LANES, (half + 1) * LANES)
        out_a_ref[:, :, lanes] = placed[:3] + part * a_ref[:, :, lanes]
        out_bo_ref[:, lanes] = placed[3] + part * bo_ref[:, lanes]
    turned = one_hot(128, 8, 16)
    for sub in range(2):
        block = jnp.concatenate(
            [
                pick(at % 2, 8 * (at // 2) + 2 * step + sub, slice(LANES, None))
                for at in range(16)
            ],
            0,
        )
        placed = dot_halved(turned, block, 1, 0)
        for chunk in range(4):
            lanes = slice(sub * LANES + chunk * 128, sub * LANES + (chunk + 1) * 128)
            rows = slice(16 * chunk, 16 * chunk + 16)
            out_bq_ref[:, lanes] = placed[rows, :128] + part * bq_ref[:, lanes]
            rows = slice(64 + 16 * chunk, 80 + 16 * chunk)
            out_ao_ref[:, lanes] = placed[rows, :128] + part * ao_ref[:, lanes]
        lanes = slice(sub * HEAD_SIZE, (sub + 1) * HEAD_SIZE)
        out_bkv_ref[0, :, lanes] = placed[:16, 128:] + part * bkv_ref[0, :, lanes]
        out_bkv_ref[1, :, lanes] = placed[16:32, 128:] + part * bkv_ref[1, :, lanes]


def whole(count):
    return [pl.BlockSpec(memory_space=pltpu.VMEM)] * count


def product(left, right, right_dim):
    left_both = jnp.concatenate(rounded_parts(left, 2), 1)
    upper, lower = rounded_parts(right, 2)
    if right_dim == 0:
        rows = jnp.concatenate([upper, lower], 1)
        both = dot_halved(left_both, jnp.concatenate([rows, rows], 0), 1, 0)
    else:
        rows = jnp.concatenate([upper, lower], 0)
        both = dot_halved(left_both, jnp.concatenate([rows, rows], 1), 1, 1)
    size = right.shape[1 - right_dim]
    return both[:, :size] + both[:, size:]


def tall(parts):
    return jnp.concatenate(parts, 0)


def flat(parts):
    return jnp.concatenate(parts, 1)


def stack(rows):
    return tall([rows[:, at : at + 128] for at in range(0, rows.shape[1], 128)])


def unstack(rows):
    return flat([rows[at : at + 128] for at in range(0, rows.shape[0], 128)])


def place_shards(whole_ref, shards, semaphores):
    spots = shard_spots()
    half = whole_ref.shape[1] // 2
    copies = []
    for at, shard in enumerate(shards):
        spot = at if at < 6 else 6 + (at - 6) // 2
        rows = pl.ds(pl.multiple_of(spots[spot] * 16, 16), 16)
        if at < 6:
            target = whole_ref.at[rows, :]
        else:
            target = whole_ref.at[rows, pl.ds((at % 2) * half, half)]
        copies.append(pltpu.make_async_copy(shard, target, semaphores.at[at]))
    for copy in copies:
        copy.start()
    return copies


def launch(pairs, semaphores, first):
    copies = prepared(pairs, semaphores, first)
    begin(copies)
    return copies


def finish(copies):
    for copy in copies:
        copy.wait()


def prepared(pairs, semaphores, first):
    return [
        pltpu.make_async_copy(source, target, semaphores.at[first + at])
        for at, (source, target) in enumerate(pairs)
    ]


def begin(copies):
    for copy in copies:
        copy.start()


def span_of(step):
    if isinstance(step, int):
        return pl.ds(step * CHUNK, CHUNK)
    return pl.ds(pl.multiple_of(step * CHUNK, CHUNK), CHUNK)


ANYWHERE = pl.BlockSpec(memory_space=pl.ANY)


def in_hbm(arrays):
    return [pltpu.with_memory_space_constraint(array, pltpu.HBM) for array in arrays]


def hbm_like(results):
    return [pltpu.HBM(result.shape, result.dtype) for result in results]


def gather_by_relays(block):
    half = block.shape[1] // 2

    def permute(array, y_step, z_step):
        pairs = [
            (at, ((at // 4 + y_step) % 2) * 4 + (at % 4 + z_step) % 4) for at in range(8)
        ]
        return lax.ppermute(array, "tensor", pairs)

    across = permute(block, 1, 0)
    below = permute(block, 0, 1)
    above = permute(block, 0, 3)
    across_below = permute(across, 0, 1)
    across_above = permute(across, 0, 3)
    far = [permute(below[:, :half], 0, 1), permute(above[:, half:], 0, 3)]
    across_far = [
        permute(across_below[:, :half], 0, 1),
        permute(across_above[:, half:], 0, 3),
    ]
    return [block, across, below, above, across_below, across_above] + far + across_far


def shard_spots():
    rank = lax.axis_index("tensor").astype(jnp.int32)
    y, z = rank // 4 * 4, rank % 4
    other = 4 - y
    return [
        y + z,
        other + z,
        y + (z + 3) % 4,
        y + (z + 1) % 4,
        other + (z + 3) % 4,
        other + (z + 1) % 4,
        y + (z + 2) % 4,
        other + (z + 2) % 4,
    ]


def small_pairs(down_hbm, up_query_hbm, up_kv_hbm, small_ref):
    return [
        (down_hbm, small_ref.at[:, 0:512]),
        (up_query_hbm, small_ref.at[:, 512:1024]),
        (up_kv_hbm.at[0], small_ref.at[:, 1024:1152]),
        (up_kv_hbm.at[1], small_ref.at[:, 1152:1280]),
    ]


CHUNK = 2048
STATE_ROWS = 2368


def forward_body(
    shard_0,
    shard_1,
    shard_2,
    shard_3,
    shard_4,
    shard_5,
    shard_6,
    shard_7,
    shard_8,
    shard_9,
    query_weight_hbm,
    kv_weight_hbm,
    down_hbm,
    output_weight_hbm,
    up_output_hbm,
    small_down_hbm,
    small_query_hbm,
    small_kv_hbm,
    tokens_hbm,
    out_hbm,
    state_hbm,
    tokens_ref,
    query_weight_ref,
    kv_weight_ref,
    down_ref,
    output_weight_ref,
    up_output_ref,
    small_ref,
    out_ref,
    state_ref,
    query_sum,
    kv_sum,
    low_sum,
    semaphores,
):
    shards = [
        shard_0,
        shard_1,
        shard_2,
        shard_3,
        shard_4,
        shard_5,
        shard_6,
        shard_7,
        shard_8,
        shard_9,
    ]
    placed = place_shards(tokens_ref, shards, semaphores)
    count = tokens_ref.shape[1] // CHUNK

    def early(step):
        span = span_of(step)
        pairs = [
            (query_weight_hbm.at[span, :], query_weight_ref.at[span, :]),
            (kv_weight_hbm.at[:, span, :], kv_weight_ref.at[:, span, :]),
            (down_hbm.at[:, span], down_ref.at[:, span]),
        ]
        return prepared(pairs, semaphores, 10 + 3 * step)

    def late(step):
        span = span_of(step)
        pairs = [
            (output_weight_hbm.at[:, span], output_weight_ref.at[:, span]),
            (up_output_hbm.at[:, span], up_output_ref.at[:, span]),
        ]
        return prepared(pairs, semaphores, 10 + 3 * count + 2 * step)

    def departing(step):
        span = span_of(step)
        pairs = [(out_ref.at[:, :, span], out_hbm.at[:, :, span])]
        return prepared(pairs, semaphores, 10 + 5 * count + step)

    for step in range(count):
        begin(early(step))
    pairs = small_pairs(small_down_hbm, small_query_hbm, small_kv_hbm, small_ref)
    small_copy = launch(pairs, semaphores, 12 + 6 * count)
    finish(placed)
    leaving = launch([(tokens_ref, tokens_hbm)], semaphores, 10 + 6 * count)
    query_sum[...] = jnp.zeros(query_sum.shape, jnp.float32)
    kv_sum[...] = jnp.zeros(kv_sum.shape, jnp.float32)
    low_sum[...] = jnp.zeros(low_sum.shape, jnp.float32)

    def project(step, _):
        finish(early(step))
        begin(late(step))
        span = span_of(step)
        tokens = tokens_ref[:, span]
        query_sum[...] += dot_halved(tokens, query_weight_ref[span, :], 1, 0)
        kv_sum[...] += dot_halved(
            tokens, flat([kv_weight_ref[0, span, :], kv_weight_ref[1, span, :]]), 1, 0
        )
        low_sum[:48] += dot_halved(down_ref[:, span], tokens, 1, 1)
        return 0

    lax.fori_loop(0, count, project, 0)
    finish(small_copy)
    low_turned = low_sum[...]
    low = low_turned.T
    root = 1.0 / math.sqrt(HEAD_SIZE)

    def adapted(total, piece, up):
        parts = rounded_parts(low[:, 16 * piece : 16 * piece + 16], 2)
        return total + ADAPTER_SCALE * dot_halved(flat(parts), tall([up, up]), 1, 0)

    query = stack(adapted(query_sum[...], 0, small_ref[:, 512:1024]))
    keys = adapted(kv_sum[:, :128], 1, small_ref[:, 1024:1152])
    values = adapted(kv_sum[:, 128:], 2, small_ref[:, 1152:])
    capped = jnp.tanh(product(query, keys, 1) * (root / SCORE_CAP))
    row = lax.broadcasted_iota(jnp.int32, (512, 128), 0) % 128
    lane = lax.broadcasted_iota(jnp.int32, (512, 128), 1)
    weights = jnp.where(row >= lane, jnp.exp(SCORE_CAP * capped), 0.0)
    probs = weights / lane_sum(weights)
    context_rows = product(probs, values, 0)
    context = unstack(context_rows)
    low_pair = dot_halved(small_ref[:, :512], tall(rounded_parts(context, 2)), 1, 1)
    context_low = ADAPTER_SCALE * (low_pair[:, :128] + low_pair[:, 128:])
    state_ref[0:512] = query
    state_ref[512:1024] = context_rows
    state_ref[1024:1536] = probs
    state_ref[1536:2048] = capped
    state_ref[2048:2176] = keys
    state_ref[2176:2304] = values
    state_ref[2304:2352] = low_turned[:48]
    state_ref[2352:2368] = context_low
    halved = context.astype(jnp.bfloat16)
    turned = tall([context_low, jnp.zeros((112, 128), jnp.float32)]).T[:, :16]
    halved_low = flat(rounded_parts(turned, 2))
    leaving += launch([(state_ref, state_hbm)], semaphores, 11 + 6 * count)

    def write(step, _):
        finish(late(step))
        span = span_of(step)
        up = up_output_ref[:, span]
        terms = dot_halved(halved, output_weight_ref[:, span], 1, 0) + dot_halved(
            halved_low, tall([up, up]), 1, 0
        )
        out_ref[:, :, span] = terms.astype(jnp.bfloat16).reshape(8, 16, CHUNK)
        begin(departing(step))
        return 0

    lax.fori_loop(0, count, write, 0)
    for step in range(count):
        finish(departing(step))
    finish(leaving)


def forward(
    shards, query_weight, key_value_weight, down_rows, output_weight, up_output, *adapters
):
    width = shards[0].shape[1]
    query_cols = query_weight.shape[1]
    weights = (query_weight, key_value_weight, down_rows, output_weight, up_output)
    arrays = (*weights, *adapters)
    small = jax.ShapeDtypeStruct((16, 1280), jnp.bfloat16)
    results = [
        jax.ShapeDtypeStruct((128, width), jnp.bfloat16),
        jax.ShapeDtypeStruct((8, 16, width), jnp.bfloat16),
        jax.ShapeDtypeStruct((STATE_ROWS, 128), jnp.float32),
    ]
    scratch = [results[0], *weights, small, results[1], results[2]]
    return pl.pallas_call(
        forward_body,
        in_specs=[ANYWHERE] * (len(shards) + len(arrays)),
        out_specs=[ANYWHERE] * 3,
        out_shape=hbm_like(results),
        scratch_shapes=[pltpu.VMEM(array.shape, array.dtype) for array in scratch]
        + [
            pltpu.VMEM((128, query_cols), jnp.float32),
            pltpu.VMEM((128, 256), jnp.float32),
            pltpu.VMEM((128, 128), jnp.float32),
            pltpu.SemaphoreType.DMA((16 + 6 * (width // CHUNK),)),
        ],
        compiler_params=pltpu.CompilerParams(vmem_limit_bytes=40 * 2**20),
        name="forward",
    )(*in_hbm(shards[:1]), *shards[1:], *in_hbm(arrays))


def cotangents_body(
    lens_ref,
    shard_0,
    shard_1,
    shard_2,
    shard_3,
    shard_4,
    shard_5,
    shard_6,
    shard_7,
    shard_8,
    shard_9,
    weight_hbm,
    side_hbm,
    state_hbm,
    small_down_hbm,
    small_query_hbm,
    small_kv_hbm,
    resid_hbm,
    factors_ref,
    later_ref,
    scalars_ref,
    resid_ref,
    weight_ref,
    side_ref,
    state_ref,
    small_ref,
    through_ref,
    slow_ref,
    square_ref,
    semaphores,
):
    shards = [
        shard_0,
        shard_1,
        shard_2,
        shard_3,
        shard_4,
        shard_5,
        shard_6,
        shard_7,
        shard_8,
        shard_9,
    ]
    placed = place_shards(resid_ref, shards, semaphores)
    count = resid_ref.shape[1] // CHUNK

    def early(step):
        span = span_of(step)
        pairs = [
            (weight_hbm.at[:, span], weight_ref.at[:, span]),
            (side_hbm.at[:, span], side_ref.at[:, span]),
        ]
        return prepared(pairs, semaphores, 10 + 2 * step)

    for step in range(count):
        begin(early(step))
    first = 10 + 2 * count
    pairs = small_pairs(small_down_hbm, small_query_hbm, small_kv_hbm, small_ref)
    others = launch([(state_hbm, state_ref)] + pairs, semaphores, first)
    slow_ref[...] = jnp.zeros(slow_ref.shape, jnp.float32)
    through_ref[...] = jnp.zeros(through_ref.shape, jnp.float32)
    square_ref[...] = jnp.zeros(square_ref.shape, jnp.float32)
    width = resid_ref.shape[1]
    finish(placed)
    leaving = launch([(resid_ref, resid_hbm)], semaphores, first + 5)

    def project(step, _):
        finish(early(step))
        span = span_of(step)
        chunk = resid_ref[:, span]
        side = side_ref[:, span]
        left = tall([chunk, side[16:]])
        through_ref[...] += dot_halved(left, weight_ref[:, span], 1, 1)
        slow_ref[:144, :32] += dot_halved(left, side, 1, 1)
        wide = chunk.astype(jnp.float32)
        square = jnp.zeros((128, 128), jnp.float32)
        for lanes in range(0, CHUNK, 128):
            square = square + wide[:, lanes : lanes + 128] * wide[:, lanes : lanes + 128]
        square_ref[...] += square
        return 0

    lax.fori_loop(0, count, project, 0)
    finish(others)
    finish_cotangents(
        lens_ref,
        width,
        state_ref,
        small_ref,
        factors_ref,
        later_ref,
        scalars_ref,
        through_ref,
        slow_ref,
        square_ref,
    )
    finish(leaving)


def finish_cotangents(
    lens_ref,
    width,
    state_ref,
    small_ref,
    factors_ref,
    later_ref,
    scalars_ref,
    through_ref,
    slow_ref,
    square_ref,
):
    if True:
        length_own = lens_ref[0]
        root = 1.0 / math.sqrt(HEAD_SIZE)
        slow = slow_ref[...]
        slow_turned = slow.T
        square = square_ref[...]
        inverse = lax.rsqrt(lane_sum(square) / width + NORM_EPS)
        inverse_turned = lax.rsqrt(row_sum(square.T) / width + NORM_EPS)
        each = 1.0 / jnp.broadcast_to(length_own, (1, 1)).astype(jnp.float32)
        share = jnp.where(
            lax.broadcasted_iota(jnp.int32, (128, 1), 0) < length_own, each, 0.0
        )
        share_turned = jnp.where(
            lax.broadcasted_iota(jnp.int32, (1, 128), 1) < length_own, each, 0.0
        )
        logits = inverse * slow[:128, 16:32]
        lead = share * inverse
        pulled = lead * inverse * logits / width
        lead_turned = share_turned * inverse_turned
        pulled_turned = (
            lead_turned * inverse_turned * inverse_turned * slow_turned[16:32, :128] / width
        )
        low_turned = slow_turned[:16, :128]
        scalars_ref[:8] = jnp.zeros((8, 128), jnp.float32)
        scalars_ref[:1, :16] = row_sum(share * logits)
        down = small_ref[:, :512]
        through = through_ref[...] + ADAPTER_SCALE * dot_halved(
            flat(rounded_parts(slow[:144, :16], 2)), tall([down, down]), 1, 0
        )
        query = state_ref[0:512]
        context_rows = state_ref[512:1024]
        probs = state_ref[1024:1536]
        capped = state_ref[1536:2048]
        keys = state_ref[2048:2176]
        values = state_ref[2176:2304]
        low_q = state_ref[2304:2320]
        low_k = state_ref[2320:2336]
        low_v = state_ref[2336:2352]
        context_low = state_ref[2352:2368]
        small = small_ref[:, 512:].astype(jnp.float32)
        up_query, up_keys, up_values = small[:, :512], small[:, 512:640], small[:, 640:]
        objectives = range(OBJ)
        head_spots = range(4)
        across = stack(through[:128])
        heads = stack(through[128:136])
        on_values = product(tall([across, heads]), values, 1)
        heads_on_values = on_values[512:]
        slope = probs * (1.0 - capped * capped) * root
        shared = slope * (on_values[:512] - lane_sum(across * context_rows))
        leading = slope * tall([lead] * 4)
        heads_on_context = product(heads, context_rows, 1)
        query_on_keys = product(stack(up_query), keys, 1)
        keys_on_query = product(up_keys, query, 1)
        padded = tall([across, heads, jnp.zeros((96, 128), jnp.float32)])
        values_on_cot = product(up_values, padded, 1)
        low_on_probs = product(low_v, probs, 1)

        def block(array, head):
            return array[:, 128 * head : 128 * head + 128]

        def row_of(array, row):
            return array[row : row + 1]

        left_values = []
        for obj in objectives:
            pull = row_of(pulled_turned, obj)
            parts = []
            for head in head_spots:
                spot = 512 + 8 * head + obj
                parts.append(
                    values_on_cot[:, spot : spot + 1] * lead_turned
                    - pull * block(values_on_cot, head)
                )
            left_values.append(flat(parts))
        factor_values = product(tall(left_values), probs, 0)
        factor_query = [0.0] * OBJ
        factor_keys = [0.0] * OBJ
        query_rows = [[] for _ in objectives]
        keys_rows = [[] for _ in objectives]
        for head in head_spots:
            rows = slice(128 * head, 128 * head + 128)
            score_lead, score_shared = leading[rows], shared[rows]
            on_context = block(heads_on_context, head)[8 * head : 8 * head + 8]
            on_value = heads_on_values[8 * head : 8 * head + 8]
            base = tall([low_q, block(keys_on_query, head)])
            first = product(
                tall([base] + [base * row_of(on_context, obj) for obj in objectives]),
                score_lead,
                0,
            )
            second = product(
                tall([base * row_of(pulled_turned, obj) for obj in objectives]), score_shared, 0
            )
            base = tall([query_on_keys[16 * head : 16 * head + 16], low_k])
            third = product(
                tall([base] + [base * row_of(on_value, obj) for obj in objectives]),
                score_lead,
                1,
            )
            fourth = product(base, score_shared, 1)
            for obj in objectives:
                spot = slice(32 + 32 * obj, 64 + 32 * obj)
                by_rows = (
                    first[:32] * row_of(on_value, obj)
                    - first[spot]
                    - second[32 * obj : 32 * obj + 32]
                )
                by_lanes = (
                    third[spot]
                    - row_of(on_context, obj) * third[:32]
                    - row_of(pulled_turned, obj) * fourth
                )
                query_rows[obj].append(by_rows[:16])
                factor_keys[obj] += by_rows[16:]
                factor_query[obj] += by_lanes[:16]
                keys_rows[obj].append(by_lanes[16:])
        later_ref[0:320] = tall([tall(rows) for rows in query_rows])
        for head in head_spots:
            spot = 320 + 80 * head
            later_ref[spot : spot + 80] = tall([rows[head] for rows in keys_rows])
            spot = 1264 + 16 * head
            later_ref[spot : spot + 16] = block(low_on_probs, head)
        later_ref[720:1232] = across
        later_ref[1232:1264] = heads
        cot_low = [
            slow_turned[:16, 128 + obj : 129 + obj] * lead_turned
            - row_of(pulled_turned, obj) * low_turned
            for obj in objectives
        ]
        later_ref[640:720] = tall(cot_low)
        for obj in objectives:
            own = slice(16 * obj, 16 * obj + 16)
            rows = [
                ADAPTER_SCALE * factor_query[obj],
                ADAPTER_SCALE * factor_keys[obj],
                ADAPTER_SCALE * factor_values[own],
                context_low,
            ]
            for piece in range(4):
                for half in range(2):
                    factors_ref[pl.ds(20 * half + 5 * piece + obj, 8, stride=40), :] = rows[
                        piece
                    ][8 * half : 8 * half + 8]
        blank = jnp.zeros((15, 128), jnp.float32)
        scalars_ref[8:48] = jnp.concatenate([blank, pulled_turned[:5]] * 2, 0)
        scalars_ref[48:] = jnp.broadcast_to(lead_turned, (40, 128))


def cotangents(lens, shards, output_weight, side, state, *adapters):
    width = shards[0].shape[1]
    query_cols = output_weight.shape[0]
    arrays = (output_weight, side, state, *adapters)
    small = jax.ShapeDtypeStruct((16, 1280), jnp.bfloat16)
    scratch = [output_weight, side, state, small]
    results = [
        jax.ShapeDtypeStruct((128, width), jnp.bfloat16),
        jax.ShapeDtypeStruct((320, 128), jnp.float32),
        jax.ShapeDtypeStruct((1328, 128), jnp.float32),
        jax.ShapeDtypeStruct((88, 128), jnp.float32),
    ]
    return pl.pallas_call(
        cotangents_body,
        in_specs=[pl.BlockSpec(memory_space=pltpu.SMEM)]
        + [ANYWHERE] * (len(shards) + len(arrays)),
        out_specs=[ANYWHERE] + whole(3),
        out_shape=hbm_like(results),
        scratch_shapes=[pltpu.VMEM(array.shape, array.dtype) for array in (results[0], *scratch)]
        + [
            pltpu.VMEM((144, query_cols), jnp.float32),
            pltpu.VMEM((256, 128), jnp.float32),
            pltpu.VMEM((128, 128), jnp.float32),
            pltpu.SemaphoreType.DMA((16 + 2 * (width // CHUNK),)),
        ],
        compiler_params=pltpu.CompilerParams(vmem_limit_bytes=32 * 2**20),
        name="cotangents",
    )(lens, *shards, *in_hbm(arrays))


def narrow_body(
    later_hbm, state_hbm, scalars_hbm, narrow_ref, later_ref, state_ref, scalars_ref, semaphores
):
    pairs = [(later_hbm, later_ref), (state_hbm, state_ref), (scalars_hbm, scalars_ref)]
    copies = launch(pairs, semaphores, 0)
    narrow_ref[...] = jnp.zeros(narrow_ref.shape, jnp.float32)
    finish(copies)
    objectives = range(OBJ)
    head_spots = range(4)
    across = later_ref[720:1232]
    heads = later_ref[1232:1264]
    low_on_probs = flat([later_ref[1264 + 16 * at : 1280 + 16 * at] for at in head_spots])
    pulls = [scalars_ref[23 + obj : 24 + obj] for obj in objectives]
    lead_turned = scalars_ref[48:49]

    def block(array, head):
        return array[:, 128 * head : 128 * head + 128]

    def row_of(array, row):
        return array[row : row + 1]

    right_values = [low_on_probs * flat([pull] * 4) for pull in pulls]
    jac_values = -product(tall(right_values), across, 0)
    low_lead = [lane_sum(block(low_on_probs, head) * lead_turned) for head in head_spots]
    jac_query = product(later_ref[0:320], state_ref[2048:2176], 0)
    keys_rows = flat([later_ref[320 + 80 * at : 400 + 80 * at] for at in head_spots])
    jac_keys = product(keys_rows, state_ref[0:512], 0)
    jac_down = product(later_ref[640:720], unstack(state_ref[512:1024]), 0)
    for obj in objectives:
        own = slice(16 * obj, 16 * obj + 16)
        own_values = jac_values[own]
        for head in head_spots:
            own_values += low_lead[head] * row_of(heads, 8 * head + obj)
        blocks = [
            jac_query[64 * obj + 16 * head : 64 * obj + 16 * head + 16]
            for head in head_spots
        ]
        blocks += [block(jac_down, head)[own] for head in head_spots]
        blocks += [jac_keys[own], own_values]
        spots = [(0, 0), (0, 1), (0, 2), (0, 3), (5, 0), (5, 1), (5, 2), (5, 3)]
        spots += [(10, 0), (10, 1)]
        for (row, tile), part in zip(spots, blocks):
            for half in range(2):
                narrow_ref[tile, pl.ds(128 * half + row + obj, 8, stride=16), :] = (
                    ADAPTER_SCALE * part[8 * half : 8 * half + 8]
                )


def narrow_rows(*arrays):
    return pl.pallas_call(
        narrow_body,
        in_specs=[ANYWHERE] * 3,
        out_specs=pl.BlockSpec(memory_space=pltpu.VMEM),
        out_shape=pltpu.HBM((4, 256, 128), jnp.float32),
        scratch_shapes=[pltpu.VMEM(array.shape, array.dtype) for array in arrays]
        + [pltpu.SemaphoreType.DMA((3,))],
        compiler_params=pltpu.CompilerParams(vmem_limit_bytes=16 * 2**20),
        cost_estimate=pl.CostEstimate(flops=0, bytes_accessed=8_000_000, transcendentals=0),
        name="narrow_rows",
    )(*in_hbm(arrays))


def jacobian_body(
    factors_hbm,
    tokens_hbm,
    resid_hbm,
    heads_hbm,
    scalars_hbm,
    narrow_hbm,
    payload_hbm,
    factors_ref,
    tokens_ref,
    resid_ref,
    heads_ref,
    scalars_ref,
    narrow_ref,
    payload_ref,
    semaphores,
):
    early = launch([(factors_hbm, factors_ref), (scalars_hbm, scalars_ref)], semaphores, 0)
    count = tokens_ref.shape[1] // CHUNK
    per_step = CHUNK // LANES

    def arriving(step):
        span = span_of(step)
        pairs = [
            (tokens_hbm.at[:, span], tokens_ref.at[:, span]),
            (resid_hbm.at[:, span], resid_ref.at[:, span]),
            (heads_hbm.at[:, span], heads_ref.at[:, span]),
        ]
        return prepared(pairs, semaphores, 3 + 3 * step)

    def departing(step):
        groups = pl.ds(step * per_step, per_step)
        pairs = [(payload_ref.at[groups], payload_hbm.at[groups])]
        return prepared(pairs, semaphores, 3 + 3 * count + step)

    begin(arriving(0))
    early += launch([(narrow_hbm, narrow_ref)], semaphores, 2)
    for step in range(1, count):
        begin(arriving(step))
    finish(early)
    factors = jnp.sum(factors_ref[...], axis=0)
    row = lax.broadcasted_iota(jnp.int32, (40, 1), 0) % 20
    last = row >= 15
    left = flat(
        [jnp.where(last, 0.0, factors), jnp.where(last, -factors * scalars_ref[8:48], 0.0)]
    )
    lead = lane_sum(factors * scalars_ref[48:])

    def both(rows):
        upper = rows.astype(jnp.bfloat16).astype(jnp.float32)
        return tall([upper, rows - upper]).astype(jnp.bfloat16)

    left = both(left)

    def place(step, _):
        finish(arriving(step))
        span = span_of(step)
        right = tall([tokens_ref[:, span], resid_ref[:, span]])
        pair = dot_halved(left, right, 1, 0)
        rows = pair[:40] + pair[40:] + lead * heads_ref[:40, span].astype(jnp.float32)
        for inner in range(per_step):
            group = step * per_step + inner
            below = flat(
                [
                    narrow_ref[tile, pl.ds(pl.multiple_of(group * 16, 16), 16), :]
                    for tile in range(4)
                ]
            )
            block = tall([rows[:, inner * LANES : (inner + 1) * LANES], below])
            payload_ref[group] = block.astype(jnp.bfloat16)
        begin(departing(step))
        return 0

    lax.fori_loop(0, count, place, 0)
    for step in range(count):
        finish(departing(step))


def jacobian(*arrays):
    result = jax.ShapeDtypeStruct((16, PIECE_ROWS, LANES), jnp.bfloat16)
    steps = arrays[1].shape[1] // CHUNK
    return pl.pallas_call(
        jacobian_body,
        in_specs=[ANYWHERE] * len(arrays),
        out_specs=ANYWHERE,
        out_shape=hbm_like([result])[0],
        scratch_shapes=[pltpu.VMEM(array.shape, array.dtype) for array in (*arrays, result)]
        + [pltpu.SemaphoreType.DMA((3 + 4 * steps,))],
        compiler_params=pltpu.CompilerParams(vmem_limit_bytes=24 * 2**20),
        name="jacobian",
    )(arrays[0], *in_hbm(arrays[1:]))


def assemble(part, own, other, *shapes):
    steps = 4
    blocks = [
        pl.BlockSpec((3, 16, 4 * LANES), lambda step: (0, 0, step)),
        pl.BlockSpec((16, 2 * LANES), lambda step: (0, step)),
        pl.BlockSpec((2, 16, 2 * HEAD_SIZE), lambda step: (0, 0, step)),
        pl.BlockSpec((16, 2 * LANES), lambda step: (0, step)),
        pl.BlockSpec((16, 4 * LANES), lambda step: (0, step)),
    ]
    return pl.pallas_call(
        assemble_body,
        grid=(steps,),
        in_specs=[
            pl.BlockSpec(memory_space=pltpu.SMEM),
            pl.BlockSpec(own.shape, lambda step: (0, 0, 0)),
            pl.BlockSpec(other.shape, lambda step: (0, 0, 0)),
        ]
        + blocks,
        out_specs=blocks,
        out_shape=[jax.ShapeDtypeStruct(shape.shape, jnp.float32) for shape in shapes],
        compiler_params=pltpu.CompilerParams(vmem_limit_bytes=14 * 2**20),
        name="assemble",
    )(part, own, other, *shapes)


def local(
    hidden,
    query_weight,
    key_value_weight,
    output_weight,
    head,
    lens,
    partner,
    adapter_down_qkv,
    adapter_up_query,
    adapter_up_key_value,
    adapter_down_output,
    adapter_up_output,
    initial_down_qkv,
    initial_up_query,
    initial_up_key_value,
    initial_down_output,
    initial_up_output,
):
    _, part_length, width = hidden.shape
    shards = lax.axis_size("tensor")
    groups = lax.axis_size("dp")
    tensor_rank = lax.axis_index("tensor")
    group_rank = lax.axis_index("dp")
    query_cols = query_weight.shape[1]
    length = part_length * shards

    down_rows = jnp.transpose(adapter_down_qkv, (0, 2, 1)).reshape(48, width)
    down_output = adapter_down_output.T
    head_rows = head.T
    side = jnp.concatenate([adapter_up_output, head_rows, jnp.zeros((11, width), head.dtype)], 0)
    heads = jnp.pad(head_rows, ((15, 0), (0, 0)))
    heads = jnp.pad(jnp.concatenate([heads, heads], 0), ((0, 8), (0, 0)))
    adapters = (down_output, adapter_up_query, adapter_up_key_value)
    tokens, out_terms, state = forward(
        gather_by_relays(hidden[0]),
        query_weight,
        key_value_weight,
        down_rows,
        output_weight,
        adapter_up_output,
        *adapters,
    )
    out_pieces = lax.all_to_all(out_terms, "tensor", 0, 0)
    resid_own = hidden[0].astype(jnp.float32) + jnp.sum(out_pieces.astype(jnp.float32), 0)
    resid, factors, later, scalars = cotangents(
        lens,
        gather_by_relays(resid_own.astype(jnp.bfloat16)),
        output_weight,
        side,
        state,
        *adapters,
    )
    factors = lax.all_to_all(factors.reshape(shards, 8 * OBJ, length), "tensor", 0, 0)
    narrow = narrow_rows(later, state, scalars)
    payload = jacobian(factors, tokens, resid, heads, scalars, narrow)
    spread = lax.all_to_all(payload, "dp", 0, 0)
    jac = (
        spread[:, : PIECES * OBJ]
        .reshape(groups, PIECES, OBJ, LANES)
        .transpose(0, 2, 1, 3)
        .reshape(groups * OBJ, PIECES * LANES)
    )

    starts = (
        jnp.transpose(initial_down_qkv, (0, 2, 1)),
        initial_up_query,
        initial_up_key_value,
        initial_down_output.T,
        initial_up_output,
    )
    starts = [pltpu.with_memory_space_constraint(start, pltpu.HBM) for start in starts]
    sequences = jnp.arange(groups)
    leads = sequences < partner
    order = jnp.sum((sequences[None, :] < sequences[:, None]) & leads[None, :], 1)
    chosen = (
        leads[None, :] & (order[None, :] == jnp.arange(groups // 2)[:, None])
    ).astype(jnp.float32)
    differences = chosen - jnp.take(chosen, partner, axis=1)
    pairs = (
        differences[:, None, :, None] * jnp.eye(OBJ, dtype=jnp.float32)[None, :, None, :]
    ).reshape(PAIR_ROWS, groups * OBJ)
    pairs = jnp.pad(pairs, ((0, PACK_ROWS - PAIR_ROWS), (0, 128 - groups * OBJ)))
    packed = pl.pallas_call(
        gram_body,
        in_specs=whole(3) + [ANYWHERE] * 5,
        out_specs=pl.BlockSpec(memory_space=pltpu.VMEM),
        out_shape=jax.ShapeDtypeStruct((16, 128), jnp.float32),
        scratch_shapes=[
            pltpu.VMEM((3, 16, LANES), jnp.float32),
            pltpu.VMEM((16, LANES), jnp.float32),
            pltpu.VMEM((2, 16, HEAD_SIZE), jnp.float32),
            pltpu.VMEM((16, LANES), jnp.float32),
            pltpu.VMEM((16, LANES), jnp.float32),
            pltpu.SemaphoreType.DMA((5,)),
        ],
        compiler_params=pltpu.CompilerParams(vmem_limit_bytes=6 * 2**20),
        name="gram",
    )(jac, pairs, scalars[:8], *starts)
    packed = jnp.sum(gather_by_exchange(packed, "dp"), 0)
    packed = gather_by_exchange(packed, "tensor")
    own_result, part = pl.pallas_call(
        lanczos_body,
        in_specs=whole(3),
        out_specs=whole(2),
        out_shape=[
            jax.ShapeDtypeStruct((8, RESULT_LANES), jnp.bfloat16),
            jax.ShapeDtypeStruct((1, 128), jnp.float32),
        ],
        compiler_params=pltpu.CompilerParams(vmem_limit_bytes=6 * 2**20),
        name="lanczos",
    )(packed, pairs, jac)
    half = groups * shards // 2
    same_core = [
        [at for at in range(2 * half) if (at // shards) % 2 == core] for core in range(2)
    ]
    own_half = lax.all_to_all(
        jnp.broadcast_to(own_result[None], (half,) + own_result.shape),
        ("dp", "tensor"),
        0,
        0,
        axis_index_groups=same_core,
    )
    other_half = lax.ppermute(own_half, "dp", [(at, at ^ 1) for at in range(groups)])
    next_a, next_bq, next_bkv, next_ao, next_bo = assemble(part, own_half, other_half, *starts)
    return jnp.transpose(next_a, (0, 2, 1)), next_bq, next_bkv, next_ao.T, next_bo


def solution(mesh):
    in_specs = (
        P("dp", "tensor", None),
        P(None, "tensor"),
        P(None, None, "tensor"),
        P("tensor", None),
        P(),
        P("dp"),
        P(),
        P(),
        P(None, "tensor"),
        P(None, None, "tensor"),
        P("tensor", None),
        P(),
        P(),
        P(),
        P(),
        P(),
        P(),
    )
    out_specs = (P(), P(), P(), P(), P())
    return jax.shard_map(local, mesh=mesh, in_specs=in_specs, out_specs=out_specs, check_vma=False)
```

```python
import math

import jax
import jax.numpy as jnp
from jax import lax
from jax.experimental import pallas as pl
from jax.experimental.pallas import tpu as pltpu
from jax.sharding import PartitionSpec as P

HEAD_SIZE = 128
NPARAM = 688128
ADAPTER_SCALE = 2.0
NORM_EPS = 1e-05
LANCZOS_EPS = 1e-06
SCORE_CAP = 30.0
PRECISE = lax.Precision.HIGHEST
OBJ = 5
PIECES = 11
PIECE_ROWS = 56
LANES = 512


def dot_halved(left_side, right_side, left_dim, right_dim):
    return lax.dot_general(
        left_side,
        right_side,
        (((left_dim,), (right_dim,)), ((), ())),
        preferred_element_type=jnp.float32,
    )


def dot_entire(left_side, right_side, left_dim, right_dim):
    return lax.dot_general(
        left_side,
        right_side,
        (((left_dim,), (right_dim,)), ((), ())),
        precision=PRECISE,
        preferred_element_type=jnp.float32,
    )


def gather_by_exchange(block, axis):
    count = lax.axis_size(axis)
    copies = jnp.broadcast_to(block[None], (count,) + block.shape)
    return lax.all_to_all(copies, axis, 0, 0)


PAIR_ROWS = 40
PACK_ROWS = 48
PACK_LANES = 42
RESULT_LANES = 768


def rounded_parts(entire, count):
    parts = []
    for _ in range(count):
        part = entire.astype(jnp.bfloat16)
        parts.append(part)
        entire = entire - part.astype(jnp.float32)
    return parts


def lane_sum(values):
    return jnp.sum(values, axis=1, keepdims=True)


def row_sum(values):
    return jnp.sum(values, axis=0, keepdims=True)


def gram_body(
    jac_ref,
    pairs_ref,
    rewards_ref,
    a_hbm,
    bq_hbm,
    bkv_hbm,
    ao_hbm,
    bo_hbm,
    packed_ref,
    a_ref,
    bq_ref,
    bkv_ref,
    ao_ref,
    bo_ref,
    semaphores,
):
    group = lax.axis_index("dp").astype(jnp.int32)
    rank = lax.axis_index("tensor").astype(jnp.int32)
    by_group = pl.ds(pl.multiple_of(group * LANES, LANES), LANES)
    by_rank = pl.ds(pl.multiple_of(rank * LANES, LANES), LANES)
    narrow = pl.ds(pl.multiple_of(rank * HEAD_SIZE, HEAD_SIZE), HEAD_SIZE)
    pairs = [
        (a_hbm.at[:, :, by_group], a_ref),
        (bq_hbm.at[:, by_rank], bq_ref),
        (bkv_hbm.at[:, :, narrow], bkv_ref),
        (ao_hbm.at[:, by_rank], ao_ref),
        (bo_hbm.at[:, by_group], bo_ref),
    ]
    copies = launch(pairs, semaphores, 0)
    jac = jac_ref[...]
    pairs = pairs_ref[...]
    rows = jac.shape[0]
    gram = dot_halved(jac, jac, 1, 1)
    finish(copies)
    blocks = []
    for row in (rank, rank + 8):
        blocks += [a_ref[piece, pl.ds(row, 1), :] for piece in range(3)]
        blocks.append(bo_ref[pl.ds(row, 1), :])
    blocks += [bq_ref[pl.ds(group, 1), :], ao_ref[pl.ds(group, 1), :]]
    blocks += [bkv_ref[piece, pl.ds(group, 1), :] for piece in range(2)]
    start = flat(blocks + [jnp.zeros((1, LANES - 2 * HEAD_SIZE), jnp.float32)])
    starts = jnp.concatenate(rounded_parts(start, 3), 0)
    along = lane_sum(dot_halved(jac, starts, 1, 1))
    own_pairs = pairs[:, :rows]
    gram = dot_entire(dot_entire(own_pairs, gram, 1, 0), own_pairs, 1, 1)
    along = dot_entire(own_pairs, jnp.broadcast_to(along, (rows, 128)), 1, 0)
    rewards = pltpu.roll(rewards_ref[...], OBJ * group, axis=1)[:1]
    rewards = jnp.where(rank == 0, rewards, 0.0)
    apart = lane_sum(pairs * rewards)
    square = jnp.sum(start * start)
    lane = lax.broadcasted_iota(jnp.int32, (PACK_ROWS, 128), 1)
    row = lax.broadcasted_iota(jnp.int32, (PACK_ROWS, 128), 0)
    wide = jnp.concatenate([gram, jnp.zeros((PACK_ROWS, 128 - PACK_ROWS), jnp.float32)], 1)
    wide = jnp.where(lane < PAIR_ROWS, wide, 0.0)
    wide = jnp.where(lane == PAIR_ROWS, along, wide)
    wide = jnp.where(lane == PAIR_ROWS + 1, apart, wide)
    wide = jnp.where((row == PAIR_ROWS) & (lane == 0), square, wide)
    packed_ref[...] = (
        wide[:16]
        + pltpu.roll(wide[16:32], PACK_LANES, axis=1)
        + pltpu.roll(wide[32:], 2 * PACK_LANES, axis=1)
    )


def lanczos_body(packed_ref, pairs_ref, jac_ref, result_ref, part_ref):
    packed = jnp.sum(packed_ref[...], axis=0)
    wide = jnp.concatenate(
        [
            packed,
            pltpu.roll(packed, 128 - PACK_LANES, axis=1),
            pltpu.roll(packed, 128 - 2 * PACK_LANES, axis=1),
        ],
        0,
    )
    lane = lax.broadcasted_iota(jnp.int32, (PACK_ROWS, 128), 1)
    row = lax.broadcasted_iota(jnp.int32, (PACK_ROWS, 128), 0)
    inside = row < PAIR_ROWS
    gram = jnp.where(inside & (lane < PAIR_ROWS), wide, 0.0)
    along = lane_sum(jnp.where(inside & (lane == PAIR_ROWS), wide, 0.0))
    apart = lane_sum(jnp.where(inside & (lane == PAIR_ROWS + 1), wide, 0.0))
    picked = jnp.where((row == PAIR_ROWS) & (lane == 0), wide, 0.0)
    start_square = lane_sum(row_sum(picked)) / NPARAM
    diagonal = row == lane

    def gram_times(column):
        across = row_sum(jnp.where(diagonal, column, 0.0))
        return lane_sum(gram * across)

    def inner(left_side, right_side):
        return row_sum(left_side * right_side) / NPARAM

    decayed = jnp.exp(-jnp.abs(apart))
    curvature = decayed / ((1.0 + decayed) * (1.0 + decayed)) / (16 // 2)
    start_scale = lax.rsqrt(start_square + LANCZOS_EPS)
    first_square = start_square * start_scale * start_scale
    along_one = along * start_scale
    pull_one = curvature * along_one
    alpha_one = inner(pull_one, along_one)
    gram_pull = gram_times(pull_one)
    beta_one = jnp.sqrt(
        inner(pull_one, gram_pull) - alpha_one * alpha_one * (2.0 - first_square) + LANCZOS_EPS
    )
    along_two = (gram_pull - alpha_one * along_one) / beta_one
    pull_two = curvature * along_two
    first_second = alpha_one * (1.0 - first_square) / beta_one
    alpha_two = inner(pull_two, along_two) - beta_one * first_second
    mixed = pull_two - (alpha_two / beta_one) * pull_one
    first_part = alpha_two * alpha_one / beta_one - beta_one
    beta_two = jnp.sqrt(
        inner(mixed, gram_times(mixed))
        + 2.0 * first_part * inner(mixed, along_one)
        + first_part * first_part * first_square
        + LANCZOS_EPS
    )
    part_ref[...] = jnp.broadcast_to(first_part * start_scale / beta_two, part_ref.shape)
    across = row_sum(pairs_ref[...] * (mixed / beta_two))
    jac = jac_ref[...]
    rows = jac.shape[0]
    parts = rounded_parts(jnp.broadcast_to(across[:, :rows], (8, rows)), 3)
    result = sum(dot_halved(part, jac, 1, 0) for part in parts)[:1]
    spare = jnp.zeros((6, 128), jnp.float32)

    def chunks(start, count, size):
        return [result[:, start + size * step : start + size * (step + 1)] for step in range(count)]

    main = jnp.concatenate(chunks(0, 8, LANES), 0)
    middle = jnp.concatenate(chunks(8 * LANES, 8, 128), 0)
    last = jnp.concatenate(chunks(10 * LANES, 2, 128) + [spare], 0)
    result_ref[...] = jnp.concatenate([main, middle, last], 1).astype(jnp.bfloat16)


def assemble_body(
    part_ref,
    own_ref,
    other_ref,
    a_ref,
    bq_ref,
    bkv_ref,
    ao_ref,
    bo_ref,
    out_a_ref,
    out_bq_ref,
    out_bkv_ref,
    out_ao_ref,
    out_bo_ref,
):
    step = pl.program_id(0)
    part = part_ref[0, 0]

    def one_hot(size, first, second):
        row = lax.broadcasted_iota(jnp.int32, (size, size), 0)
        lane = lax.broadcasted_iota(jnp.int32, (size, size), 1)
        wanted = (row % second) * first + row // second
        return jnp.where(lane == wanted, 1.0, 0.0).astype(jnp.bfloat16)

    row = lax.broadcasted_iota(jnp.int32, (64, 64), 0)
    lane = lax.broadcasted_iota(jnp.int32, (64, 64), 1)
    wanted = (row % 8) * 8 + ((row % 16) // 8) * 4 + row // 16
    moved = jnp.where(lane == wanted, 1.0, 0.0).astype(jnp.bfloat16)

    mine = lax.axis_index("dp").astype(jnp.int32) % 2

    def pick(core, spot, lanes):
        return jnp.where(
            mine == core, own_ref[spot, :, lanes], other_ref[spot, :, lanes]
        )

    for half in range(4):
        spot = pl.ds(pl.multiple_of(16 * step + 8 * (half // 2), 8), 8)
        block = pick(half % 2, spot, slice(0, LANES)).reshape(64, LANES)
        placed = dot_halved(moved, block, 1, 0).reshape(4, 16, LANES)
        lanes = slice(half * LANES, (half + 1) * LANES)
        out_a_ref[:, :, lanes] = placed[:3] + part * a_ref[:, :, lanes]
        out_bo_ref[:, lanes] = placed[3] + part * bo_ref[:, lanes]
    turned = one_hot(128, 8, 16)
    for sub in range(2):
        block = jnp.concatenate(
            [
                pick(at % 2, 8 * (at // 2) + 2 * step + sub, slice(LANES, None))
                for at in range(16)
            ],
            0,
        )
        placed = dot_halved(turned, block, 1, 0)
        for chunk in range(4):
            lanes = slice(sub * LANES + chunk * 128, sub * LANES + (chunk + 1) * 128)
            rows = slice(16 * chunk, 16 * chunk + 16)
            out_bq_ref[:, lanes] = placed[rows, :128] + part * bq_ref[:, lanes]
            rows = slice(64 + 16 * chunk, 80 + 16 * chunk)
            out_ao_ref[:, lanes] = placed[rows, :128] + part * ao_ref[:, lanes]
        lanes = slice(sub * HEAD_SIZE, (sub + 1) * HEAD_SIZE)
        out_bkv_ref[0, :, lanes] = placed[:16, 128:] + part * bkv_ref[0, :, lanes]
        out_bkv_ref[1, :, lanes] = placed[16:32, 128:] + part * bkv_ref[1, :, lanes]


def whole(count):
    return [pl.BlockSpec(memory_space=pltpu.VMEM)] * count


def product(left, right, right_dim):
    left_both = jnp.concatenate(rounded_parts(left, 2), 1)
    upper, lower = rounded_parts(right, 2)
    if right_dim == 0:
        rows = jnp.concatenate([upper, lower], 1)
        both = dot_halved(left_both, jnp.concatenate([rows, rows], 0), 1, 0)
    else:
        rows = jnp.concatenate([upper, lower], 0)
        both = dot_halved(left_both, jnp.concatenate([rows, rows], 1), 1, 1)
    size = right.shape[1 - right_dim]
    return both[:, :size] + both[:, size:]


def tall(parts):
    return jnp.concatenate(parts, 0)


def flat(parts):
    return jnp.concatenate(parts, 1)


def stack(rows):
    return tall([rows[:, at : at + 128] for at in range(0, rows.shape[1], 128)])


def unstack(rows):
    return flat([rows[at : at + 128] for at in range(0, rows.shape[0], 128)])


def place_shards(whole_ref, shards, semaphores):
    spots = shard_spots()
    half = whole_ref.shape[1] // 2
    copies = []
    for at, shard in enumerate(shards):
        spot = at if at < 6 else 6 + (at - 6) // 2
        rows = pl.ds(pl.multiple_of(spots[spot] * 16, 16), 16)
        if at < 6:
            target = whole_ref.at[rows, :]
        else:
            target = whole_ref.at[rows, pl.ds((at % 2) * half, half)]
        copies.append(pltpu.make_async_copy(shard, target, semaphores.at[at]))
    for copy in copies:
        copy.start()
    return copies


def launch(pairs, semaphores, first):
    copies = prepared(pairs, semaphores, first)
    begin(copies)
    return copies


def finish(copies):
    for copy in copies:
        copy.wait()


def prepared(pairs, semaphores, first):
    return [
        pltpu.make_async_copy(source, target, semaphores.at[first + at])
        for at, (source, target) in enumerate(pairs)
    ]


def begin(copies):
    for copy in copies:
        copy.start()


def span_of(step):
    if isinstance(step, int):
        return pl.ds(step * CHUNK, CHUNK)
    return pl.ds(pl.multiple_of(step * CHUNK, CHUNK), CHUNK)


ANYWHERE = pl.BlockSpec(memory_space=pl.ANY)


def in_hbm(arrays):
    return [pltpu.with_memory_space_constraint(array, pltpu.HBM) for array in arrays]


def hbm_like(results):
    return [pltpu.HBM(result.shape, result.dtype) for result in results]


def gather_by_relays(block):
    half = block.shape[1] // 2

    def permute(array, y_step, z_step):
        pairs = [
            (at, ((at // 4 + y_step) % 2) * 4 + (at % 4 + z_step) % 4) for at in range(8)
        ]
        return lax.ppermute(array, "tensor", pairs)

    across = permute(block, 1, 0)
    below = permute(block, 0, 1)
    above = permute(block, 0, 3)
    across_below = permute(across, 0, 1)
    across_above = permute(across, 0, 3)
    far = [permute(below[:, :half], 0, 1), permute(above[:, half:], 0, 3)]
    across_far = [
        permute(across_below[:, :half], 0, 1),
        permute(across_above[:, half:], 0, 3),
    ]
    return [block, across, below, above, across_below, across_above] + far + across_far


def shard_spots():
    rank = lax.axis_index("tensor").astype(jnp.int32)
    y, z = rank // 4 * 4, rank % 4
    other = 4 - y
    return [
        y + z,
        other + z,
        y + (z + 3) % 4,
        y + (z + 1) % 4,
        other + (z + 3) % 4,
        other + (z + 1) % 4,
        y + (z + 2) % 4,
        other + (z + 2) % 4,
    ]


def small_pairs(down_hbm, up_query_hbm, up_kv_hbm, small_ref):
    return [
        (down_hbm, small_ref.at[:, 0:512]),
        (up_query_hbm, small_ref.at[:, 512:1024]),
        (up_kv_hbm.at[0], small_ref.at[:, 1024:1152]),
        (up_kv_hbm.at[1], small_ref.at[:, 1152:1280]),
    ]


CHUNK = 2048
STATE_ROWS = 2368


def forward_body(
    shard_0,
    shard_1,
    shard_2,
    shard_3,
    shard_4,
    shard_5,
    shard_6,
    shard_7,
    shard_8,
    shard_9,
    query_weight_hbm,
    kv_weight_hbm,
    down_hbm,
    output_weight_hbm,
    up_output_hbm,
    small_down_hbm,
    small_query_hbm,
    small_kv_hbm,
    tokens_hbm,
    out_hbm,
    state_hbm,
    tokens_ref,
    query_weight_ref,
    kv_weight_ref,
    down_ref,
    output_weight_ref,
    up_output_ref,
    small_ref,
    out_ref,
    state_ref,
    query_sum,
    kv_sum,
    low_sum,
    semaphores,
):
    shards = [
        shard_0,
        shard_1,
        shard_2,
        shard_3,
        shard_4,
        shard_5,
        shard_6,
        shard_7,
        shard_8,
        shard_9,
    ]
    placed = place_shards(tokens_ref, shards, semaphores)
    count = tokens_ref.shape[1] // CHUNK

    def early(step):
        span = span_of(step)
        pairs = [
            (query_weight_hbm.at[span, :], query_weight_ref.at[span, :]),
            (kv_weight_hbm.at[:, span, :], kv_weight_ref.at[:, span, :]),
            (down_hbm.at[:, span], down_ref.at[:, span]),
        ]
        return prepared(pairs, semaphores, 10 + 3 * step)

    def late(step):
        span = span_of(step)
        pairs = [
            (output_weight_hbm.at[:, span], output_weight_ref.at[:, span]),
            (up_output_hbm.at[:, span], up_output_ref.at[:, span]),
        ]
        return prepared(pairs, semaphores, 10 + 3 * count + 2 * step)

    def departing(step):
        span = span_of(step)
        pairs = [(out_ref.at[:, :, span], out_hbm.at[:, :, span])]
        return prepared(pairs, semaphores, 10 + 5 * count + step)

    for step in range(count):
        begin(early(step))
    pairs = small_pairs(small_down_hbm, small_query_hbm, small_kv_hbm, small_ref)
    small_copy = launch(pairs, semaphores, 12 + 6 * count)
    finish(placed)
    leaving = launch([(tokens_ref, tokens_hbm)], semaphores, 10 + 6 * count)
    query_sum[...] = jnp.zeros(query_sum.shape, jnp.float32)
    kv_sum[...] = jnp.zeros(kv_sum.shape, jnp.float32)
    low_sum[...] = jnp.zeros(low_sum.shape, jnp.float32)

    def project(step, _):
        finish(early(step))
        begin(late(step))
        span = span_of(step)
        tokens = tokens_ref[:, span]
        query_sum[...] += dot_halved(tokens, query_weight_ref[span, :], 1, 0)
        kv_sum[...] += dot_halved(
            tokens, flat([kv_weight_ref[0, span, :], kv_weight_ref[1, span, :]]), 1, 0
        )
        low_sum[:48] += dot_halved(down_ref[:, span], tokens, 1, 1)
        return 0

    lax.fori_loop(0, count, project, 0)
    finish(small_copy)
    low_turned = low_sum[...]
    low = low_turned.T
    root = 1.0 / math.sqrt(HEAD_SIZE)

    def adapted(total, piece, up):
        parts = rounded_parts(low[:, 16 * piece : 16 * piece + 16], 2)
        return total + ADAPTER_SCALE * dot_halved(flat(parts), tall([up, up]), 1, 0)

    query = stack(adapted(query_sum[...], 0, small_ref[:, 512:1024]))
    keys = adapted(kv_sum[:, :128], 1, small_ref[:, 1024:1152])
    values = adapted(kv_sum[:, 128:], 2, small_ref[:, 1152:])
    capped = jnp.tanh(product(query, keys, 1) * (root / SCORE_CAP))
    row = lax.broadcasted_iota(jnp.int32, (512, 128), 0) % 128
    lane = lax.broadcasted_iota(jnp.int32, (512, 128), 1)
    weights = jnp.where(row >= lane, jnp.exp(SCORE_CAP * capped), 0.0)
    probs = weights / lane_sum(weights)
    context_rows = product(probs, values, 0)
    context = unstack(context_rows)
    low_pair = dot_halved(small_ref[:, :512], tall(rounded_parts(context, 2)), 1, 1)
    context_low = ADAPTER_SCALE * (low_pair[:, :128] + low_pair[:, 128:])
    state_ref[0:512] = query
    state_ref[512:1024] = context_rows
    state_ref[1024:1536] = probs
    state_ref[1536:2048] = capped
    state_ref[2048:2176] = keys
    state_ref[2176:2304] = values
    state_ref[2304:2352] = low_turned[:48]
    state_ref[2352:2368] = context_low
    halved = context.astype(jnp.bfloat16)
    turned = tall([context_low, jnp.zeros((112, 128), jnp.float32)]).T[:, :16]
    halved_low = flat(rounded_parts(turned, 2))
    leaving += launch([(state_ref, state_hbm)], semaphores, 11 + 6 * count)

    def write(step, _):
        finish(late(step))
        span = span_of(step)
        up = up_output_ref[:, span]
        terms = dot_halved(halved, output_weight_ref[:, span], 1, 0) + dot_halved(
            halved_low, tall([up, up]), 1, 0
        )
        out_ref[:, :, span] = terms.astype(jnp.bfloat16).reshape(8, 16, CHUNK)
        begin(departing(step))
        return 0

    lax.fori_loop(0, count, write, 0)
    for step in range(count):
        finish(departing(step))
    finish(leaving)


def forward(
    shards, query_weight, key_value_weight, down_rows, output_weight, up_output, *adapters
):
    width = shards[0].shape[1]
    query_cols = query_weight.shape[1]
    weights = (query_weight, key_value_weight, down_rows, output_weight, up_output)
    arrays = (*weights, *adapters)
    small = jax.ShapeDtypeStruct((16, 1280), jnp.bfloat16)
    results = [
        jax.ShapeDtypeStruct((128, width), jnp.bfloat16),
        jax.ShapeDtypeStruct((8, 16, width), jnp.bfloat16),
        jax.ShapeDtypeStruct((STATE_ROWS, 128), jnp.float32),
    ]
    scratch = [results[0], *weights, small, results[1], results[2]]
    return pl.pallas_call(
        forward_body,
        in_specs=[ANYWHERE] * (len(shards) + len(arrays)),
        out_specs=[ANYWHERE] * 3,
        out_shape=hbm_like(results),
        scratch_shapes=[pltpu.VMEM(array.shape, array.dtype) for array in scratch]
        + [
            pltpu.VMEM((128, query_cols), jnp.float32),
            pltpu.VMEM((128, 256), jnp.float32),
            pltpu.VMEM((128, 128), jnp.float32),
            pltpu.SemaphoreType.DMA((16 + 6 * (width // CHUNK),)),
        ],
        compiler_params=pltpu.CompilerParams(vmem_limit_bytes=40 * 2**20),
        name="forward",
    )(*in_hbm(shards[:1]), *shards[1:], *in_hbm(arrays))


def cotangents_body(
    lens_ref,
    shard_0,
    shard_1,
    shard_2,
    shard_3,
    shard_4,
    shard_5,
    shard_6,
    shard_7,
    shard_8,
    shard_9,
    weight_hbm,
    side_hbm,
    state_hbm,
    small_down_hbm,
    small_query_hbm,
    small_kv_hbm,
    resid_hbm,
    factors_ref,
    later_ref,
    scalars_ref,
    resid_ref,
    weight_ref,
    side_ref,
    state_ref,
    small_ref,
    through_ref,
    slow_ref,
    square_ref,
    semaphores,
):
    shards = [
        shard_0,
        shard_1,
        shard_2,
        shard_3,
        shard_4,
        shard_5,
        shard_6,
        shard_7,
        shard_8,
        shard_9,
    ]
    placed = place_shards(resid_ref, shards, semaphores)
    count = resid_ref.shape[1] // CHUNK

    def early(step):
        span = span_of(step)
        pairs = [
            (weight_hbm.at[:, span], weight_ref.at[:, span]),
            (side_hbm.at[:, span], side_ref.at[:, span]),
        ]
        return prepared(pairs, semaphores, 10 + 2 * step)

    for step in range(count):
        begin(early(step))
    first = 10 + 2 * count
    pairs = small_pairs(small_down_hbm, small_query_hbm, small_kv_hbm, small_ref)
    others = launch([(state_hbm, state_ref)] + pairs, semaphores, first)
    slow_ref[...] = jnp.zeros(slow_ref.shape, jnp.float32)
    through_ref[...] = jnp.zeros(through_ref.shape, jnp.float32)
    square_ref[...] = jnp.zeros(square_ref.shape, jnp.float32)
    width = resid_ref.shape[1]
    finish(placed)
    leaving = launch([(resid_ref, resid_hbm)], semaphores, first + 5)

    def project(step, _):
        finish(early(step))
        span = span_of(step)
        chunk = resid_ref[:, span]
        side = side_ref[:, span]
        left = tall([chunk, side[16:]])
        through_ref[...] += dot_halved(left, weight_ref[:, span], 1, 1)
        slow_ref[:144, :32] += dot_halved(left, side, 1, 1)
        wide = chunk.astype(jnp.float32)
        square = jnp.zeros((128, 128), jnp.float32)
        for lanes in range(0, CHUNK, 128):
            square = square + wide[:, lanes : lanes + 128] * wide[:, lanes : lanes + 128]
        square_ref[...] += square
        return 0

    lax.fori_loop(0, count, project, 0)
    finish(others)
    finish_cotangents(
        lens_ref,
        width,
        state_ref,
        small_ref,
        factors_ref,
        later_ref,
        scalars_ref,
        through_ref,
        slow_ref,
        square_ref,
    )
    finish(leaving)


def finish_cotangents(
    lens_ref,
    width,
    state_ref,
    small_ref,
    factors_ref,
    later_ref,
    scalars_ref,
    through_ref,
    slow_ref,
    square_ref,
):
    if True:
        length_own = lens_ref[0]
        root = 1.0 / math.sqrt(HEAD_SIZE)
        slow = slow_ref[...]
        slow_turned = slow.T
        square = square_ref[...]
        inverse = lax.rsqrt(lane_sum(square) / width + NORM_EPS)
        inverse_turned = lax.rsqrt(row_sum(square.T) / width + NORM_EPS)
        each = 1.0 / jnp.broadcast_to(length_own, (1, 1)).astype(jnp.float32)
        share = jnp.where(
            lax.broadcasted_iota(jnp.int32, (128, 1), 0) < length_own, each, 0.0
        )
        share_turned = jnp.where(
            lax.broadcasted_iota(jnp.int32, (1, 128), 1) < length_own, each, 0.0
        )
        logits = inverse * slow[:128, 16:32]
        lead = share * inverse
        pulled = lead * inverse * logits / width
        lead_turned = share_turned * inverse_turned
        pulled_turned = (
            lead_turned * inverse_turned * inverse_turned * slow_turned[16:32, :128] / width
        )
        low_turned = slow_turned[:16, :128]
        scalars_ref[:8] = jnp.zeros((8, 128), jnp.float32)
        scalars_ref[:1, :16] = row_sum(share * logits)
        down = small_ref[:, :512]
        through = through_ref[...] + ADAPTER_SCALE * dot_halved(
            flat(rounded_parts(slow[:144, :16], 2)), tall([down, down]), 1, 0
        )
        query = state_ref[0:512]
        context_rows = state_ref[512:1024]
        probs = state_ref[1024:1536]
        capped = state_ref[1536:2048]
        keys = state_ref[2048:2176]
        values = state_ref[2176:2304]
        low_q = state_ref[2304:2320]
        low_k = state_ref[2320:2336]
        low_v = state_ref[2336:2352]
        context_low = state_ref[2352:2368]
        small = small_ref[:, 512:].astype(jnp.float32)
        up_query, up_keys, up_values = small[:, :512], small[:, 512:640], small[:, 640:]
        objectives = range(OBJ)
        head_spots = range(4)
        across = stack(through[:128])
        heads = stack(through[128:136])
        on_values = product(tall([across, heads]), values, 1)
        heads_on_values = on_values[512:]
        slope = probs * (1.0 - capped * capped) * root
        shared = slope * (on_values[:512] - lane_sum(across * context_rows))
        leading = slope * tall([lead] * 4)
        heads_on_context = product(heads, context_rows, 1)
        query_on_keys = product(stack(up_query), keys, 1)
        keys_on_query = product(up_keys, query, 1)
        padded = tall([across, heads, jnp.zeros((96, 128), jnp.float32)])
        values_on_cot = product(up_values, padded, 1)
        low_on_probs = product(low_v, probs, 1)

        def block(array, head):
            return array[:, 128 * head : 128 * head + 128]

        def row_of(array, row):
            return array[row : row + 1]

        left_values = []
        for obj in objectives:
            pull = row_of(pulled_turned, obj)
            parts = []
            for head in head_spots:
                spot = 512 + 8 * head + obj
                parts.append(
                    values_on_cot[:, spot : spot + 1] * lead_turned
                    - pull * block(values_on_cot, head)
                )
            left_values.append(flat(parts))
        factor_values = product(tall(left_values), probs, 0)
        factor_query = [0.0] * OBJ
        factor_keys = [0.0] * OBJ
        query_rows = [[] for _ in objectives]
        keys_rows = [[] for _ in objectives]
        for head in head_spots:
            rows = slice(128 * head, 128 * head + 128)
            score_lead, score_shared = leading[rows], shared[rows]
            on_context = block(heads_on_context, head)[8 * head : 8 * head + 8]
            on_value = heads_on_values[8 * head : 8 * head + 8]
            base = tall([low_q, block(keys_on_query, head)])
            first = product(
                tall([base] + [base * row_of(on_context, obj) for obj in objectives]),
                score_lead,
                0,
            )
            second = product(
                tall([base * row_of(pulled_turned, obj) for obj in objectives]), score_shared, 0
            )
            base = tall([query_on_keys[16 * head : 16 * head + 16], low_k])
            third = product(
                tall([base] + [base * row_of(on_value, obj) for obj in objectives]),
                score_lead,
                1,
            )
            fourth = product(base, score_shared, 1)
            for obj in objectives:
                spot = slice(32 + 32 * obj, 64 + 32 * obj)
                by_rows = (
                    first[:32] * row_of(on_value, obj)
                    - first[spot]
                    - second[32 * obj : 32 * obj + 32]
                )
                by_lanes = (
                    third[spot]
                    - row_of(on_context, obj) * third[:32]
                    - row_of(pulled_turned, obj) * fourth
                )
                query_rows[obj].append(by_rows[:16])
                factor_keys[obj] += by_rows[16:]
                factor_query[obj] += by_lanes[:16]
                keys_rows[obj].append(by_lanes[16:])
        later_ref[0:320] = tall([tall(rows) for rows in query_rows])
        for head in head_spots:
            spot = 320 + 80 * head
            later_ref[spot : spot + 80] = tall([rows[head] for rows in keys_rows])
            spot = 1264 + 16 * head
            later_ref[spot : spot + 16] = block(low_on_probs, head)
        later_ref[720:1232] = across
        later_ref[1232:1264] = heads
        cot_low = [
            slow_turned[:16, 128 + obj : 129 + obj] * lead_turned
            - row_of(pulled_turned, obj) * low_turned
            for obj in objectives
        ]
        later_ref[640:720] = tall(cot_low)
        for obj in objectives:
            own = slice(16 * obj, 16 * obj + 16)
            rows = [
                ADAPTER_SCALE * factor_query[obj],
                ADAPTER_SCALE * factor_keys[obj],
                ADAPTER_SCALE * factor_values[own],
                context_low,
            ]
            for piece in range(4):
                for half in range(2):
                    factors_ref[pl.ds(20 * half + 5 * piece + obj, 8, stride=40), :] = rows[
                        piece
                    ][8 * half : 8 * half + 8]
        blank = jnp.zeros((15, 128), jnp.float32)
        scalars_ref[8:48] = jnp.concatenate([blank, pulled_turned[:5]] * 2, 0)
        scalars_ref[48:] = jnp.broadcast_to(lead_turned, (40, 128))


def cotangents(lens, shards, output_weight, side, state, *adapters):
    width = shards[0].shape[1]
    query_cols = output_weight.shape[0]
    arrays = (output_weight, side, state, *adapters)
    small = jax.ShapeDtypeStruct((16, 1280), jnp.bfloat16)
    scratch = [output_weight, side, state, small]
    results = [
        jax.ShapeDtypeStruct((128, width), jnp.bfloat16),
        jax.ShapeDtypeStruct((320, 128), jnp.float32),
        jax.ShapeDtypeStruct((1328, 128), jnp.float32),
        jax.ShapeDtypeStruct((88, 128), jnp.float32),
    ]
    return pl.pallas_call(
        cotangents_body,
        in_specs=[pl.BlockSpec(memory_space=pltpu.SMEM)]
        + [ANYWHERE] * (len(shards) + len(arrays)),
        out_specs=[ANYWHERE] + whole(3),
        out_shape=hbm_like(results),
        scratch_shapes=[pltpu.VMEM(array.shape, array.dtype) for array in (results[0], *scratch)]
        + [
            pltpu.VMEM((144, query_cols), jnp.float32),
            pltpu.VMEM((256, 128), jnp.float32),
            pltpu.VMEM((128, 128), jnp.float32),
            pltpu.SemaphoreType.DMA((16 + 2 * (width // CHUNK),)),
        ],
        compiler_params=pltpu.CompilerParams(vmem_limit_bytes=32 * 2**20),
        name="cotangents",
    )(lens, *shards, *in_hbm(arrays))


def narrow_body(
    later_hbm, state_hbm, scalars_hbm, narrow_ref, later_ref, state_ref, scalars_ref, semaphores
):
    pairs = [(later_hbm, later_ref), (state_hbm, state_ref), (scalars_hbm, scalars_ref)]
    copies = launch(pairs, semaphores, 0)
    narrow_ref[...] = jnp.zeros(narrow_ref.shape, jnp.float32)
    finish(copies)
    objectives = range(OBJ)
    head_spots = range(4)
    across = later_ref[720:1232]
    heads = later_ref[1232:1264]
    low_on_probs = flat([later_ref[1264 + 16 * at : 1280 + 16 * at] for at in head_spots])
    pulls = [scalars_ref[23 + obj : 24 + obj] for obj in objectives]
    lead_turned = scalars_ref[48:49]

    def block(array, head):
        return array[:, 128 * head : 128 * head + 128]

    def row_of(array, row):
        return array[row : row + 1]

    right_values = [low_on_probs * flat([pull] * 4) for pull in pulls]
    jac_values = -product(tall(right_values), across, 0)
    low_lead = [lane_sum(block(low_on_probs, head) * lead_turned) for head in head_spots]
    jac_query = product(later_ref[0:320], state_ref[2048:2176], 0)
    keys_rows = flat([later_ref[320 + 80 * at : 400 + 80 * at] for at in head_spots])
    jac_keys = product(keys_rows, state_ref[0:512], 0)
    jac_down = product(later_ref[640:720], unstack(state_ref[512:1024]), 0)
    for obj in objectives:
        own = slice(16 * obj, 16 * obj + 16)
        own_values = jac_values[own]
        for head in head_spots:
            own_values += low_lead[head] * row_of(heads, 8 * head + obj)
        blocks = [
            jac_query[64 * obj + 16 * head : 64 * obj + 16 * head + 16]
            for head in head_spots
        ]
        blocks += [block(jac_down, head)[own] for head in head_spots]
        blocks += [jac_keys[own], own_values]
        spots = [(0, 0), (0, 1), (0, 2), (0, 3), (5, 0), (5, 1), (5, 2), (5, 3)]
        spots += [(10, 0), (10, 1)]
        for (row, tile), part in zip(spots, blocks):
            for half in range(2):
                narrow_ref[tile, pl.ds(128 * half + row + obj, 8, stride=16), :] = (
                    ADAPTER_SCALE * part[8 * half : 8 * half + 8]
                )


def narrow_rows(*arrays):
    return pl.pallas_call(
        narrow_body,
        in_specs=[ANYWHERE] * 3,
        out_specs=pl.BlockSpec(memory_space=pltpu.VMEM),
        out_shape=pltpu.HBM((4, 256, 128), jnp.float32),
        scratch_shapes=[pltpu.VMEM(array.shape, array.dtype) for array in arrays]
        + [pltpu.SemaphoreType.DMA((3,))],
        compiler_params=pltpu.CompilerParams(vmem_limit_bytes=16 * 2**20),
        cost_estimate=pl.CostEstimate(flops=0, bytes_accessed=8_000_000, transcendentals=0),
        name="narrow_rows",
    )(*in_hbm(arrays))


def jacobian_body(
    factors_hbm,
    tokens_hbm,
    resid_hbm,
    heads_hbm,
    scalars_hbm,
    narrow_hbm,
    payload_hbm,
    factors_ref,
    tokens_ref,
    resid_ref,
    heads_ref,
    scalars_ref,
    narrow_ref,
    payload_ref,
    semaphores,
):
    early = launch([(factors_hbm, factors_ref), (scalars_hbm, scalars_ref)], semaphores, 0)
    count = tokens_ref.shape[1] // CHUNK
    per_step = CHUNK // LANES

    def arriving(step):
        span = span_of(step)
        pairs = [
            (tokens_hbm.at[:, span], tokens_ref.at[:, span]),
            (resid_hbm.at[:, span], resid_ref.at[:, span]),
            (heads_hbm.at[:, span], heads_ref.at[:, span]),
        ]
        return prepared(pairs, semaphores, 3 + 3 * step)

    def departing(step):
        groups = pl.ds(step * per_step, per_step)
        pairs = [(payload_ref.at[groups], payload_hbm.at[groups])]
        return prepared(pairs, semaphores, 3 + 3 * count + step)

    begin(arriving(0))
    early += launch([(narrow_hbm, narrow_ref)], semaphores, 2)
    for step in range(1, count):
        begin(arriving(step))
    finish(early)
    factors = jnp.sum(factors_ref[...], axis=0)
    row = lax.broadcasted_iota(jnp.int32, (40, 1), 0) % 20
    last = row >= 15
    left = flat(
        [jnp.where(last, 0.0, factors), jnp.where(last, -factors * scalars_ref[8:48], 0.0)]
    )
    lead = lane_sum(factors * scalars_ref[48:])

    def both(rows):
        upper = rows.astype(jnp.bfloat16).astype(jnp.float32)
        return tall([upper, rows - upper]).astype(jnp.bfloat16)

    left = both(left)

    def place(step, _):
        finish(arriving(step))
        span = span_of(step)
        right = tall([tokens_ref[:, span], resid_ref[:, span]])
        pair = dot_halved(left, right, 1, 0)
        rows = pair[:40] + pair[40:] + lead * heads_ref[:40, span].astype(jnp.float32)
        for inner in range(per_step):
            group = step * per_step + inner
            below = flat(
                [
                    narrow_ref[tile, pl.ds(pl.multiple_of(group * 16, 16), 16), :]
                    for tile in range(4)
                ]
            )
            block = tall([rows[:, inner * LANES : (inner + 1) * LANES], below])
            payload_ref[group] = block.astype(jnp.bfloat16)
        begin(departing(step))
        return 0

    lax.fori_loop(0, count, place, 0)
    for step in range(count):
        finish(departing(step))


def jacobian(*arrays):
    result = jax.ShapeDtypeStruct((16, PIECE_ROWS, LANES), jnp.bfloat16)
    steps = arrays[1].shape[1] // CHUNK
    return pl.pallas_call(
        jacobian_body,
        in_specs=[ANYWHERE] * len(arrays),
        out_specs=ANYWHERE,
        out_shape=hbm_like([result])[0],
        scratch_shapes=[pltpu.VMEM(array.shape, array.dtype) for array in (*arrays, result)]
        + [pltpu.SemaphoreType.DMA((3 + 4 * steps,))],
        compiler_params=pltpu.CompilerParams(vmem_limit_bytes=24 * 2**20),
        name="jacobian",
    )(arrays[0], *in_hbm(arrays[1:]))


def assemble(part, own, other, *shapes):
    steps = 4
    blocks = [
        pl.BlockSpec((3, 16, 4 * LANES), lambda step: (0, 0, step)),
        pl.BlockSpec((16, 2 * LANES), lambda step: (0, step)),
        pl.BlockSpec((2, 16, 2 * HEAD_SIZE), lambda step: (0, 0, step)),
        pl.BlockSpec((16, 2 * LANES), lambda step: (0, step)),
        pl.BlockSpec((16, 4 * LANES), lambda step: (0, step)),
    ]
    return pl.pallas_call(
        assemble_body,
        grid=(steps,),
        in_specs=[
            pl.BlockSpec(memory_space=pltpu.SMEM),
            pl.BlockSpec(own.shape, lambda step: (0, 0, 0)),
            pl.BlockSpec(other.shape, lambda step: (0, 0, 0)),
        ]
        + blocks,
        out_specs=blocks,
        out_shape=[jax.ShapeDtypeStruct(shape.shape, jnp.float32) for shape in shapes],
        compiler_params=pltpu.CompilerParams(vmem_limit_bytes=14 * 2**20),
        name="assemble",
    )(part, own, other, *shapes)


def local(
    hidden,
    query_weight,
    key_value_weight,
    output_weight,
    head,
    lens,
    partner,
    adapter_down_qkv,
    adapter_up_query,
    adapter_up_key_value,
    adapter_down_output,
    adapter_up_output,
    initial_down_qkv,
    initial_up_query,
    initial_up_key_value,
    initial_down_output,
    initial_up_output,
):
    _, part_length, width = hidden.shape
    shards = lax.axis_size("tensor")
    groups = lax.axis_size("dp")
    tensor_rank = lax.axis_index("tensor")
    group_rank = lax.axis_index("dp")
    query_cols = query_weight.shape[1]
    length = part_length * shards

    down_rows = jnp.transpose(adapter_down_qkv, (0, 2, 1)).reshape(48, width)
    down_output = adapter_down_output.T
    head_rows = head.T
    side = jnp.concatenate([adapter_up_output, head_rows, jnp.zeros((11, width), head.dtype)], 0)
    heads = jnp.pad(head_rows, ((15, 0), (0, 0)))
    heads = jnp.pad(jnp.concatenate([heads, heads], 0), ((0, 8), (0, 0)))
    adapters = (down_output, adapter_up_query, adapter_up_key_value)
    tokens, out_terms, state = forward(
        gather_by_relays(hidden[0]),
        query_weight,
        key_value_weight,
        down_rows,
        output_weight,
        adapter_up_output,
        *adapters,
    )
    out_pieces = lax.all_to_all(out_terms, "tensor", 0, 0)
    out_pieces, side, heads = lax.optimization_barrier((out_pieces, side, heads))
    resid_own = hidden[0].astype(jnp.float32) + jnp.sum(out_pieces.astype(jnp.float32), 0)
    resid, factors, later, scalars = cotangents(
        lens,
        gather_by_relays(resid_own.astype(jnp.bfloat16)),
        output_weight,
        side,
        state,
        *adapters,
    )
    factors = lax.all_to_all(factors.reshape(shards, 8 * OBJ, length), "tensor", 0, 0)
    narrow = narrow_rows(later, state, scalars)
    payload = jacobian(factors, tokens, resid, heads, scalars, narrow)
    spread = lax.all_to_all(payload, "dp", 0, 0)
    jac = (
        spread[:, : PIECES * OBJ]
        .reshape(groups, PIECES, OBJ, LANES)
        .transpose(0, 2, 1, 3)
        .reshape(groups * OBJ, PIECES * LANES)
    )

    starts = (
        jnp.transpose(initial_down_qkv, (0, 2, 1)),
        initial_up_query,
        initial_up_key_value,
        initial_down_output.T,
        initial_up_output,
    )
    starts = [pltpu.with_memory_space_constraint(start, pltpu.HBM) for start in starts]
    sequences = jnp.arange(groups)
    leads = sequences < partner
    order = jnp.sum((sequences[None, :] < sequences[:, None]) & leads[None, :], 1)
    chosen = (
        leads[None, :] & (order[None, :] == jnp.arange(groups // 2)[:, None])
    ).astype(jnp.float32)
    differences = chosen - jnp.take(chosen, partner, axis=1)
    pairs = (
        differences[:, None, :, None] * jnp.eye(OBJ, dtype=jnp.float32)[None, :, None, :]
    ).reshape(PAIR_ROWS, groups * OBJ)
    pairs = jnp.pad(pairs, ((0, PACK_ROWS - PAIR_ROWS), (0, 128 - groups * OBJ)))
    packed = pl.pallas_call(
        gram_body,
        in_specs=whole(3) + [ANYWHERE] * 5,
        out_specs=pl.BlockSpec(memory_space=pltpu.VMEM),
        out_shape=jax.ShapeDtypeStruct((16, 128), jnp.float32),
        scratch_shapes=[
            pltpu.VMEM((3, 16, LANES), jnp.float32),
            pltpu.VMEM((16, LANES), jnp.float32),
            pltpu.VMEM((2, 16, HEAD_SIZE), jnp.float32),
            pltpu.VMEM((16, LANES), jnp.float32),
            pltpu.VMEM((16, LANES), jnp.float32),
            pltpu.SemaphoreType.DMA((5,)),
        ],
        compiler_params=pltpu.CompilerParams(vmem_limit_bytes=6 * 2**20),
        name="gram",
    )(jac, pairs, scalars[:8], *starts)
    packed = jnp.sum(gather_by_exchange(packed, "dp"), 0)
    packed = gather_by_exchange(packed, "tensor")
    own_result, part = pl.pallas_call(
        lanczos_body,
        in_specs=whole(3),
        out_specs=whole(2),
        out_shape=[
            jax.ShapeDtypeStruct((8, RESULT_LANES), jnp.bfloat16),
            jax.ShapeDtypeStruct((1, 128), jnp.float32),
        ],
        compiler_params=pltpu.CompilerParams(vmem_limit_bytes=6 * 2**20),
        name="lanczos",
    )(packed, pairs, jac)
    half = groups * shards // 2
    same_core = [
        [at for at in range(2 * half) if (at // shards) % 2 == core] for core in range(2)
    ]
    own_half = lax.all_to_all(
        jnp.broadcast_to(own_result[None], (half,) + own_result.shape),
        ("dp", "tensor"),
        0,
        0,
        axis_index_groups=same_core,
    )
    other_half = lax.ppermute(own_half, "dp", [(at, at ^ 1) for at in range(groups)])
    next_a, next_bq, next_bkv, next_ao, next_bo = assemble(part, own_half, other_half, *starts)
    return jnp.transpose(next_a, (0, 2, 1)), next_bq, next_bkv, next_ao.T, next_bo


def solution(mesh):
    in_specs = (
        P("dp", "tensor", None),
        P(None, "tensor"),
        P(None, None, "tensor"),
        P("tensor", None),
        P(),
        P("dp"),
        P(),
        P(),
        P(None, "tensor"),
        P(None, None, "tensor"),
        P("tensor", None),
        P(),
        P(),
        P(),
        P(),
        P(),
        P(),
    )
    out_specs = (P(), P(), P(), P(), P())
    return jax.shard_map(local, mesh=mesh, in_specs=in_specs, out_specs=out_specs, check_vma=False)
```
